32 devices in a mesh: rep: 4 (over z), shard: 8 (over y, x, core).
Axes of the slice: x: 2, y: 2, z: 4, core: 2. Of those that a mesh axis runs over, the one named last changes fastest.
Arguments:
- block_input: bfloat16 [32, 128, 2048], P(('rep', 'shard')), may hold values from -6 to 6
- lengths: int32 [32], P(('rep', 'shard')), may hold values from 32 to 128, as said below
- first_gain: bfloat16 [2048], P('shard'), may hold values from 0.5 to 1.5
- first_shift: bfloat16 [2048], P('shard'), may hold values from -1 to 1
- query_weight: bfloat16 [2048, 2048], P('shard'), may hold values from -0.25 to 0.25
- query_bias: bfloat16 [2048], P('shard'), may hold values from -1.5 to 1.5
- key_weight: bfloat16 [2048, 2048], P('shard'), may hold values from -0.125 to 0.125
- value_weight: bfloat16 [2048, 2048], P('shard'), may hold values from -0.125 to 0.125
- value_bias: bfloat16 [2048], P('shard'), may hold values from -1.5 to 1.5
- out_weight: bfloat16 [2048, 2048], P('shard'), may hold values from -0.75 to 0.75
- out_bias: bfloat16 [2048], P('shard'), may hold values from -1.5 to 1.5
- second_gain: bfloat16 [2048], P('shard'), may hold values from 0.5 to 1.5
- second_shift: bfloat16 [2048], P('shard'), may hold values from -1 to 1
- up_weight: bfloat16 [2048, 8192], P('shard'), may hold values from -0.125 to 0.125
- up_bias: bfloat16 [8192], P('shard'), may hold values from -1.5 to 1.5
- down_weight: bfloat16 [8192, 2048], P('shard'), may hold values from -0.125 to 0.125
- down_bias: bfloat16 [2048], P('shard'), may hold values from -1.5 to 1.5
- cotangent: bfloat16 [32, 128, 2048], P(('rep', 'shard')), may hold values from -6 to 6
Outputs:
- block_output: bfloat16 [32, 128, 2048], P(('rep', 'shard'))
- input_grad: bfloat16 [32, 128, 2048], P(('rep', 'shard'))
- first_gain_grad: float32 [2048], P('shard')
- first_shift_grad: float32 [2048], P('shard')
- query_weight_grad: float32 [2048, 2048], P('shard')
- query_bias_grad: float32 [2048], P('shard')
- key_weight_grad: float32 [2048, 2048], P('shard')
- value_weight_grad: float32 [2048, 2048], P('shard')
- value_bias_grad: float32 [2048], P('shard')
- out_weight_grad: float32 [2048, 2048], P('shard')
- out_bias_grad: float32 [2048], P('shard')
- second_gain_grad: float32 [2048], P('shard')
- second_shift_grad: float32 [2048], P('shard')
- up_weight_grad: float32 [2048, 8192], P('shard')
- up_bias_grad: float32 [8192], P('shard')
- down_weight_grad: float32 [8192, 2048], P('shard')
- down_bias_grad: float32 [2048], P('shard')
The draws below stay inside these ranges and needn't reach their ends.
Inputs may be any that keep to these rules, and one draw needn't show every extreme that they name: `lengths`: one sequence has exactly 128 live slots and one exactly 32.
All inputs are finite; a program needn't handle non-finite values.
Results may differ from the reference program's by a relative error of at most 0.019.
Values may be sent and summed in bfloat16 or wider, within the bound.
A program may use at most 768 MiB of HBM per device.

```python
import math
import jax
import jax.numpy as jnp
from jax import lax

D = 2048
FF = 8192
HEADS = 16
HEAD_DIM = 128
SEQ = 128
SEQS = 32


def draw_lengths(key, part):
    value_key, pick_key = jax.random.split(jax.random.fold_in(key, 17))
    drawn = jax.random.randint(value_key, (SEQS,), SEQ // 4, SEQ + 1)
    order = jax.random.permutation(pick_key, SEQS)
    drawn = drawn.at[order[0]].set(SEQ)
    drawn = drawn.at[order[1]].set(SEQ // 4)
    return drawn.astype(jnp.int32)


def block_levels(rng, extent, pieces, smallest, top_value):
    level, own = 1.0, jax.random.fold_in(rng, 6)
    for axis_at, blocks in pieces:
        heights = jnp.exp(jax.random.uniform(jax.random.fold_in(own, axis_at), (blocks,), jnp.float32, smallest / len(pieces), top_value / len(pieces)))
        level = level * jnp.repeat(heights, extent[axis_at] // blocks).reshape([-1 if axis == axis_at else 1 for axis in range(len(extent))])
    return level


def gaussian(rng, extent, scale, limit, shards=(), kind=jnp.bfloat16):
    level = block_levels(rng, extent, shards, -0.22, 0.18) if shards else 1.0
    array = jax.random.normal(rng, extent, jnp.float32) * scale * level
    return jnp.minimum(jnp.maximum(array, -limit), limit).astype(kind)


def setup_inputs(seed: int = 0) -> dict:
    arg_keys = jax.random.split(jax.random.key(seed), 19)
    return {
        "block_input": gaussian(arg_keys[0], (SEQS, SEQ, D), 1.0, 6.0, ((0, 32),)),
        "lengths": draw_lengths(jax.random.fold_in(arg_keys[18], 71), 0),
        "first_gain": jnp.clip(1.0 + 0.1 * jax.random.normal(arg_keys[2], (D,), jnp.float32), 0.5, 1.5).astype(jnp.bfloat16),
        "first_shift": gaussian(arg_keys[3], (D,), 0.2, 1.0, ((0, 8),)),
        "query_weight": gaussian(arg_keys[4], (D, D), (D // 4) ** -0.5, 0.25, ((0, 8),)),
        "query_bias": gaussian(arg_keys[5], (D,), 0.3, 1.5, ((0, 8),)),
        "key_weight": gaussian(arg_keys[6], (D, D), D ** -0.5, 0.125, ((0, 8),)),
        "value_weight": gaussian(arg_keys[7], (D, D), D ** -0.5, 0.125, ((0, 8),)),
        "value_bias": gaussian(arg_keys[8], (D,), 0.3, 1.5, ((0, 8),)),
        "out_weight": gaussian(arg_keys[9], (D, D), (D // 32) ** -0.5, 0.75, ((0, 8),)),
        "out_bias": gaussian(arg_keys[10], (D,), 0.3, 1.5, ((0, 8),)),
        "second_gain": jnp.clip(1.0 + 0.1 * jax.random.normal(arg_keys[11], (D,), jnp.float32), 0.5, 1.5).astype(jnp.bfloat16),
        "second_shift": gaussian(arg_keys[12], (D,), 0.2, 1.0, ((0, 8),)),
        "up_weight": gaussian(arg_keys[13], (D, FF), D ** -0.5, 0.125, ((0, 8),)),
        "up_bias": gaussian(arg_keys[14], (FF,), 0.3, 1.5, ((0, 8),)),
        "down_weight": gaussian(arg_keys[15], (FF, D), (FF // 4) ** -0.5, 0.125, ((0, 8),)),
        "down_bias": gaussian(arg_keys[16], (D,), 0.3, 1.5, ((0, 8),)),
        "cotangent": gaussian(arg_keys[17], (SEQS, SEQ, D), 1.0, 6.0, ((0, 32),)),
    }


@jax.custom_vjp
def low(v):
    return lax.optimization_barrier(v.astype(jnp.bfloat16)).astype(jnp.float32)

@jax.custom_vjp
def low_back(v):
    return v

def low_keep(v):
    return (low(v), None)

def low_pass(kept, grad):
    return (grad,)

def back_keep(v):
    return (v, None)

def back_low(kept, grad):
    return (low(grad),)
low.defvjp(low_keep, low_pass)
low_back.defvjp(back_keep, back_low)

def highest(left, right):
    return jnp.dot(left, right, precision=lax.Precision.HIGHEST)

def layer_norm(values, gain, shift):
    center = values - lax.optimization_barrier(jnp.mean(values, axis=-1, keepdims=True))
    spread = lax.optimization_barrier(jnp.mean(center * center, axis=-1, keepdims=True))
    return center * lax.rsqrt(spread + 1e-05) * gain + shift

def sequence_forward(block, length, params):
    first_gain, first_shift, query_weight, query_bias, key_weight, value_weight, value_bias, out_weight, out_bias, second_gain, second_shift, up_weight, up_bias, down_weight, down_bias = params
    positions = jnp.arange(SEQ, dtype=jnp.int32)
    live = (positions < length).astype(jnp.float32)[:, None]
    normed = low(layer_norm(block, first_gain, first_shift))
    queries = low(low_back(highest(normed, query_weight) + query_bias))
    keys = low(low_back(highest(normed, key_weight)))
    values = low(low_back(highest(normed, value_weight) + value_bias))
    key_heads = keys.reshape(SEQ, HEADS, HEAD_DIM)
    value_heads = values.reshape(SEQ, HEADS, HEAD_DIM)
    block_rows = min(SEQ, 512)
    count = SEQ // block_rows
    query_blocks = queries.reshape(count, block_rows, HEADS, HEAD_DIM)
    starts = jnp.arange(count, dtype=jnp.int32) * block_rows
    scale = 1.0 / math.sqrt(HEAD_DIM)

    def attend(item):
        query_block, start = item
        scores = jnp.einsum('qhd,khd->hqk', query_block, key_heads, precision=lax.Precision.HIGHEST) * scale
        scores = low_back(scores)
        rows = start + jnp.arange(block_rows, dtype=jnp.int32)
        valid = (positions[None, :] <= rows[:, None]) & (positions[None, :] < length)
        scores = jnp.where(valid[None], scores, -1e+30)
        weights = low(jax.nn.softmax(scores, axis=-1))
        return jnp.einsum('hqk,khd->qhd', weights, value_heads, precision=lax.Precision.HIGHEST)
    context = lax.map(jax.checkpoint(attend), (query_blocks, starts))
    context = low(low_back(context.reshape(SEQ, D)))
    branch = low_back(highest(context, out_weight) + out_bias)
    middle = block + branch
    second = low(layer_norm(middle, second_gain, second_shift))
    upper = low_back(highest(second, up_weight) + up_bias)
    active = low(jax.nn.gelu(upper, approximate=False))
    mixed = low_back(highest(active, down_weight) + down_bias)
    return (middle + mixed) * live

def reference(block_input, lengths, first_gain, first_shift, query_weight, query_bias, key_weight, value_weight, value_bias, out_weight, out_bias, second_gain, second_shift, up_weight, up_bias, down_weight, down_bias, cotangent):
    params = tuple((item.astype(jnp.float32) for item in (first_gain, first_shift, query_weight, query_bias, key_weight, value_weight, value_bias, out_weight, out_bias, second_gain, second_shift, up_weight, up_bias, down_weight, down_bias)))
    group = math.gcd(SEQS, 16)
    steps_count = SEQS // group
    inputs = block_input.astype(jnp.float32).reshape(steps_count, group, SEQ, D)
    grouped_lengths = lengths.astype(jnp.int32).reshape(steps_count, group)
    grouped_cots = cotangent.astype(jnp.float32).reshape(steps_count, group, SEQ, D)

    def step(totals, item):
        blocks, group_lengths, group_cots = item

        def batched(blocks_in, params_in):
            return jax.vmap(sequence_forward, in_axes=(0, 0, None))(blocks_in, group_lengths, params_in)
        outputs, pullback = jax.vjp(batched, blocks, params)
        grad_blocks, grad_params = pullback(group_cots)
        totals = jax.tree.map(jnp.add, totals, grad_params)
        return (totals, (outputs.astype(jnp.bfloat16), grad_blocks.astype(jnp.bfloat16)))
    zeros = tuple((jnp.zeros_like(item) for item in params))
    totals, (outputs, grads) = lax.scan(step, zeros, (inputs, grouped_lengths, grouped_cots))
    first_gain_grad, first_shift_grad, query_weight_grad, query_bias_grad, key_weight_grad, value_weight_grad, value_bias_grad, out_weight_grad, out_bias_grad, second_gain_grad, second_shift_grad, up_weight_grad, up_bias_grad, down_weight_grad, down_bias_grad = totals
    return (outputs.reshape(SEQS, SEQ, D), grads.reshape(SEQS, SEQ, D), first_gain_grad, first_shift_grad, query_weight_grad, query_bias_grad, key_weight_grad, value_weight_grad, value_bias_grad, out_weight_grad, out_bias_grad, second_gain_grad, second_shift_grad, up_weight_grad, up_bias_grad, down_weight_grad, down_bias_grad)
```

```python
import functools
import math

import jax
import jax.numpy as jnp
from jax import lax
from jax.experimental import pallas as pl
from jax.experimental.pallas import tpu as pltpu
from jax.sharding import PartitionSpec as P

HEADS = 16
MESH = pl.DeviceIdType.MESH
BF = jnp.bfloat16
F32 = jnp.float32
VM = pl.BlockSpec(memory_space=pltpu.VMEM)
LIMIT = 60 * 2**20
SIZE = None


def flip(index, mask):
    bit = 1
    while bit <= mask:
        if mask & bit:
            index = index + bit - 2 * bit * ((index // bit) % 2)
        bit *= 2
    return index


def span(masks):
    out = [0]
    for m in masks:
        out = out + [h ^ m for h in out]
    return out


def pair_masks(size):
    masks, bit = [], 1
    while bit < size:
        masks.append(bit + bit // 2 if len(masks) % 2 and size >= 2 * bit else bit)
        bit *= 2
    return masks


def shard_masks(size):
    masks, bit = [], 2
    while bit < size:
        masks.append(bit if len(masks) < 2 else bit + bit // 2)
        bit *= 2
    return masks


def orders(masks):
    return [list(masks), list(masks[1:]) + list(masks[:1])]


class Net:
    def __init__(self, send, recv):
        self.send, self.recv, self.used, self.open = send, recv, 0, []

    def to(self, axis, mask, src, dst):
        k = self.used
        self.used += 1
        copy = pltpu.make_async_remote_copy(
            src_ref=src,
            dst_ref=dst,
            send_sem=self.send.at[k],
            recv_sem=self.recv.at[k],
            device_id={axis: flip(lax.axis_index(axis), mask)},
            device_id_type=MESH,
        )
        copy.start()
        self.open.append(copy)
        return copy

    def own(self, src, dst):
        k = self.used
        self.used += 1
        copy = pltpu.make_async_copy(src, dst, self.send.at[k])
        copy.start()
        return copy

    def finish(self):
        for copy in self.open:
            copy.wait_send()


def meet(shard_set, rep_set):
    barrier = pltpu.get_barrier_semaphore()
    for axis, masks in (("shard", shard_set), ("rep", rep_set)):
        for m in masks:
            pl.semaphore_signal(
                barrier,
                inc=1,
                device_id={axis: flip(lax.axis_index(axis), m)},
                device_id_type=MESH,
            )
    pl.semaphore_wait(barrier, len(shard_set) + len(rep_set))


class Gather:
    def __init__(self, net, buf, masks):
        self.net, self.buf = net, buf
        rows = buf.shape[1] // 2
        self.parts = [
            dict(rows=pl.ds(i * rows, rows), order=o, held=[0], wait=[])
            for i, o in enumerate(orders(masks))
        ]
        self.cores = []
        self.step = 0
        self.steps = len(masks)

    def start(self):
        net, buf = self.net, self.buf
        for part in self.parts:
            fresh = part["held"] if self.step == 0 else part["new"]
            if self.step < self.steps:
                m = part["order"][self.step]
                part["new"] = [h ^ m for h in part["held"]]
                part["wait"] = [
                    net.to("shard", m, buf.at[h, part["rows"]], buf.at[h ^ m, part["rows"]])
                    for h in part["held"]
                ]
                part["held"] = part["held"] + part["new"]
            self.cores += [
                net.to("shard", 1, buf.at[h, part["rows"]], buf.at[h ^ 1, part["rows"]])
                for h in fresh
            ]
        self.step += 1

    def arrive(self):
        for part in self.parts:
            for copy in part["wait"]:
                copy.wait_recv()
            part["wait"] = []

    def run(self):
        for _ in range(self.steps):
            self.start()
            self.arrive()
        self.start()
        self.end()

    def end(self):
        for copy in self.cores:
            copy.wait_recv()


def reduce_shapes(group, rows, width, masks):
    half = [pltpu.VMEM((group // 2, rows, width), BF)] * 2
    count = 0
    for i in range(len(masks)):
        count += 2 ** (len(masks) - 1 - i)
    return half + [pltpu.VMEM((count, rows, width), BF)]


class Reduce:
    def __init__(self, net, part, work, masks):
        self.net, self.part, self.masks = net, part, masks
        self.core_land, self.sums, self.land = work
        self.group, self.rows = part.shape[0], part.shape[1]
        self.cores = {}

    def begin(self):
        for j in range(1, self.group, 2):
            self.cores[j ^ 1] = self.net.to(
                "shard", 1, self.part.at[j], self.core_land.at[(j ^ 1) // 2]
            )

    def fold(self, h, rows, landed):
        step = 32

        @pl.loop(0, rows.size // step)
        def _(i):
            at = pl.ds(pl.multiple_of(rows.start + i * step, step), step)
            self.sums[h // 2, at] = (
                self.sums[h // 2, at].astype(F32) + landed[at].astype(F32)
            ).astype(BF)

    def first(self, h):
        step = 32
        self.cores[h].wait_recv()

        @pl.loop(0, self.rows // step)
        def _(i):
            at = pl.ds(pl.multiple_of(i * step, step), step)
            self.sums[h // 2, at] = (
                self.part[h, at].astype(F32) + self.core_land[h // 2, at].astype(F32)
            ).astype(BF)

    def launch(self, k):
        half = self.rows // 2
        self.flight = []
        base = 0
        for i in range(k):
            base += 2 ** (len(self.masks) - 1 - i)
        for n, order in enumerate(orders(self.masks)):
            rows = pl.ds(n * half, half)
            rest = span(order[k + 1 :])
            for at, h in enumerate(rest):
                copy = self.net.to(
                    "shard",
                    order[k],
                    self.sums.at[(h ^ order[k]) // 2, rows],
                    self.land.at[base + at, rows],
                )
                self.flight.append((copy, h, rows, base + at))

    def prepare(self):
        both = orders(self.masks)
        sent = set()
        for order in both:
            sent |= {h ^ order[0] for h in span(order[1:])}
        every = span(self.masks)
        for h in sorted(sent):
            self.first(h)
        self.launch(0)
        for h in every:
            if h not in sent:
                self.first(h)

    def advance(self, k):
        flight = self.flight
        for copy, h, rows, at in flight:
            copy.wait_recv()
            if k < len(self.masks) - 1:
                self.fold(h, rows, self.land.at[at])
        if k < len(self.masks) - 1:
            self.launch(k + 1)

    def run(self):
        self.begin()
        self.prepare()
        for k in range(len(self.masks)):
            self.advance(k)

    def total(self, at):
        [(_, _, rows, slot)] = [f for f in self.flight if f[2].start == at[0]]
        return (self.sums[0, at[1]].astype(F32) + self.land[slot, at[1]].astype(F32))


def norm_rows(v):
    center = v - jnp.mean(v, axis=-1, keepdims=True)
    spread = jnp.mean(center * center, axis=-1, keepdims=True)
    inv = lax.rsqrt(spread + 1e-05)
    return center * inv, inv


def norm_back(grad, gain, n, inv):
    scaled = grad * gain
    return inv * (
        scaled
        - jnp.mean(scaled, axis=-1, keepdims=True)
        - n * jnp.mean(scaled * n, axis=-1, keepdims=True)
    )


FG, FS, OB, SG, SS, DB, LN = range(7)


def live_rows(length, start, rows):
    at = start + lax.broadcasted_iota(jnp.int32, (rows, 1), 0)
    return (at.astype(F32) < length).astype(F32)


def rep_gather(net, views, order):
    held = [0]
    for m in order:
        copies = [net.to("rep", m, views(h), views(h)) for h in held]
        held = held + [h ^ m for h in held]
        yield copies


def gather_kernel(
    sizes,
    x_ref,
    cot_ref,
    small_ref,
    q_ref,
    k_ref,
    v_ref,
    u_ref,
    nrm,
    mix,
    small_all,
    wq,
    wk,
    wv,
    wu,
    send,
    recv,
):
    group, reps = sizes
    me, rep = lax.axis_index("shard"), lax.axis_index("rep")
    net = Net(send, recv)
    masks, rmasks = shard_masks(group), pair_masks(reps)
    meet(range(1, group), rmasks)
    width = small_ref.shape[1]
    mine = pl.ds(pl.multiple_of(me * width, width), width)
    small = [
        net.to("shard", j, small_ref, small_all.at[:, mine]) for j in range(1, group)
    ]
    own_small = net.own(small_ref, small_all.at[:, mine])
    arrays = ((q_ref, wq), (k_ref, wk), (v_ref, wv), (u_ref, wu))
    chunk = q_ref.shape[0] // reps

    def piece(mask):
        return pl.ds(pl.multiple_of(flip(rep, mask) * chunk, chunk), chunk)

    moved = []
    for src, dst in arrays:
        n = dst.shape[2]

        def columns(j):
            return pl.ds(pl.multiple_of(flip(me, j) * n, n), n)

        moved.append(
            [
                net.to("shard", j, src.at[piece(0), columns(j)], dst.at[me, piece(0)])
                for j in range(1, group)
            ]
            + [net.own(src.at[piece(0), columns(0)], dst.at[me, piece(0)])]
        )
    for copy in small:
        copy.wait_recv()
    own_small.wait()
    length = small_all[LN : LN + 1, pl.ds(pl.multiple_of(me * width, width), 128)][:, :1]
    step = 16

    @pl.loop(0, x_ref.shape[0] // step)
    def _(i):
        at = pl.ds(pl.multiple_of(i * step, step), step)
        n, _ = norm_rows(x_ref[at].astype(F32))
        nrm[0, at] = (n * small_all[FG : FG + 1] + small_all[FS : FS + 1]).astype(BF)
        mix[0, at] = (cot_ref[at].astype(F32) * live_rows(length, i * step, step)).astype(BF)

    gathers = [Gather(net, nrm, masks), Gather(net, mix, masks)]
    for g in gathers:
        g.start()
    streams = []
    for i, ((_, dst), copies) in enumerate(zip(arrays, moved)):
        for copy in copies[:-1]:
            copy.wait_recv()
        copies[-1].wait()
        both = (rmasks, rmasks[::-1])
        lanes = dst.shape[2] // 2
        if lanes % 128:
            lanes, both = dst.shape[2], both[i % 2 :][:1]
        for n, order in enumerate(both):
            cols = pl.ds(n * lanes, lanes)
            streams.append(
                rep_gather(net, lambda h, d=dst, c=cols: d.at[:, piece(h), c], order)
            )
    flights = [next(s) for s in streams]
    for _ in range(len(masks)):
        for g in gathers:
            g.arrive()
            g.start()
    for _ in range(len(rmasks)):
        for i, s in enumerate(streams):
            for copy in flights[i]:
                copy.wait_recv()
            flights[i] = next(s, [])
    for g in gathers:
        g.end()
    net.finish()


def middle_kernel(sizes, part, x_ref, small, mid, second, *work):
    group, _ = sizes
    net = Net(*work[-2:])
    masks = shard_masks(group)
    meet([1] + masks, [])
    red = Reduce(net, part, work[:3], masks)
    red.run()
    step, half = 16, x_ref.shape[0] // 2
    for n in range(2):

        @pl.loop(0, half // step)
        def _(i):
            at = pl.ds(pl.multiple_of(n * half + i * step, step), step)
            m = x_ref[at].astype(F32) + (red.total((n * half, at)) + small[OB : OB + 1])
            mid[at] = m
            v, _ = norm_rows(m)
            second[0, at] = (v * small[SG : SG + 1] + small[SS : SS + 1]).astype(BF)

    Gather(net, second, masks).run()
    net.finish()


def branch_kernel(sizes, down, grad, mid, cot, small, out, gmid, sums, branch, *work):
    group, _ = sizes
    net = Net(*work[-2:])
    masks = shard_masks(group)
    meet([1] + masks, [])
    me = lax.axis_index("shard")
    width = small.shape[1] // group
    length = small[LN : LN + 1, pl.ds(pl.multiple_of(me * width, width), 128)][:, :1]
    red = Reduce(net, grad, work[:3], masks)
    late = Reduce(net, down, work[3:6], masks)
    red.begin()
    late.begin()
    red.prepare()
    for k in range(len(masks)):
        red.advance(k)
    step, half = 16, mid.shape[0] // 2
    sums[...] = jnp.zeros_like(sums)
    for n in range(2):

        @pl.loop(0, half // step)
        def _(i):
            at = pl.ds(pl.multiple_of(n * half + i * step, step), step)
            g = red.total((n * half, at))
            v, inv = norm_rows(mid[at])
            gout = cot[at].astype(F32) * live_rows(length, n * half + i * step, step)
            res = gout + norm_back(g, small[SG : SG + 1], v, inv)
            gmid[at] = res
            low = res.astype(BF)
            branch[0, at] = low
            sums[SG : SG + 1] += jnp.sum(g * v, axis=0, keepdims=True)
            sums[SS : SS + 1] += jnp.sum(g, axis=0, keepdims=True)
            sums[OB : OB + 1] += jnp.sum(low.astype(F32), axis=0, keepdims=True)
            sums[DB : DB + 1] += jnp.sum(gout, axis=0, keepdims=True)

    gather = Gather(net, branch, masks)
    gather.start()
    late.prepare()
    for k in range(len(masks)):
        gather.arrive()
        gather.start()
        late.advance(k)
    gather.end()
    for n in range(2):

        @pl.loop(0, half // step)
        def _(i):
            at = pl.ds(pl.multiple_of(n * half + i * step, step), step)
            v = mid[at] + (late.total((n * half, at)) + small[DB : DB + 1])
            out[at] = (v * live_rows(length, n * half + i * step, step)).astype(BF)

    net.finish()


class RepSum:
    def __init__(self, net, arr, order, sums, land, reps):
        self.net, self.arr, self.order = net, arr, order
        self.sums, self.land = sums, land
        self.chunk = arr.shape[1] // reps
        self.slots = {h: i for i, h in enumerate(span(order[1:]))}

    def view(self, mask):
        at = flip(lax.axis_index("rep"), mask) * self.chunk
        return self.arr.at[:, pl.ds(pl.multiple_of(at, self.chunk), self.chunk)]

    def launch(self, k):
        rest = span(self.order[k + 1 :])
        base = 0
        for i in range(k):
            base += 2 ** (len(self.order) - 1 - i)
        m = self.order[k]
        self.flight = []
        for at, h in enumerate(rest):
            src = self.view(h ^ m) if k == 0 else self.sums.at[self.slots[h ^ m]]
            copy = self.net.to("rep", m, src, self.land.at[base + at])
            self.flight.append((copy, h, base + at))

    def fold(self, k):
        flight = self.flight
        for copy, h, at in reversed(flight):
            copy.wait_recv()
            left = self.view(h) if k == 0 else self.sums.at[self.slots[h]]
            right, dst = self.land.at[at], self.sums.at[self.slots[h]]
            add_into(dst, left, right)


def add_into(dst, left, right):
    a, c, n = dst.shape
    step = 16 if n >= 1024 else min(c, 64)

    @pl.loop(0, a)
    def _(i):
        @pl.loop(0, c // step)
        def _(j):
            at = pl.ds(pl.multiple_of(j * step, step), step)
            dst[i, at] = (left[i, at].astype(F32) + right[i, at].astype(F32)).astype(BF)


def sum_shapes(shape, reps):
    a, rows, n = shape
    masks = pair_masks(reps)
    count = 2 ** len(masks)
    return [
        pltpu.VMEM((count // 2, a, rows // reps, n), BF),
        pltpu.VMEM((count - 1, a, rows // reps, n), BF),
    ]


def final_kernel(sizes, *refs):
    group, reps = sizes
    grad, x_ref, gmid, small, sums3, cols = refs[:6]
    arrays = refs[6:12]
    gin, smalls = refs[12:14]
    outs = refs[14:20]
    work = refs[20:]
    red_work = work[:3]
    pairs = [work[3 + 2 * i : 5 + 2 * i] for i in range(6)]
    sums, land, both, zland = work[15:19]
    net = Net(*work[-2:])
    masks, rmasks = shard_masks(group), pair_masks(reps)
    me, rep = lax.axis_index("shard"), lax.axis_index("rep")
    meet(range(1, group), range(1, reps))
    width = smalls.shape[1]
    flips = [rmasks, rmasks[::-1]]
    reds = [
        RepSum(net, a, flips[f], *p, reps)
        for a, p, f in zip(arrays, pairs, (0, 0, 1, 0, 1, 1))
    ]
    q, k, v, up, out, down = reds
    turn = [down, up, out, q, k, v]
    for red in turn:
        red.launch(0)
    first = Reduce(net, grad, red_work, masks)
    first.run()
    step, half = 16, x_ref.shape[0] // 2
    sums[...] = sums3[...]
    for n in range(2):

        @pl.loop(0, half // step)
        def _(i):
            at = pl.ds(pl.multiple_of(n * half + i * step, step), step)
            g = first.total((n * half, at))
            w, inv = norm_rows(x_ref[at].astype(F32))
            gin[at] = (gmid[at] + norm_back(g, small[FG : FG + 1], w, inv)).astype(BF)
            sums[FG : FG + 1] += jnp.sum(g * w, axis=0, keepdims=True)
            sums[FS : FS + 1] += jnp.sum(g, axis=0, keepdims=True)

    def mine(j):
        return pl.ds(pl.multiple_of(flip(me, j) * width, width), width)

    tiny = [net.to("shard", j, sums.at[:, mine(j)], land.at[me]) for j in range(1, group)]
    own = net.own(sums.at[:, mine(0)], land.at[me])
    for copy in tiny:
        copy.wait_recv()
    own.wait()
    total = land[0]
    for j in range(1, group):
        total = total + land[j]
    both[0:8] = total
    both[8:16] = cols[...]
    tiny = [net.to("rep", h, both, zland.at[rep]) for h in range(1, reps)]
    own = net.own(both, zland.at[rep])
    for step_at in range(len(rmasks)):
        for red in turn:
            red.fold(step_at)
            if step_at < len(rmasks) - 1:
                red.launch(step_at + 1)

    def rows(o, mask):
        c = o.shape[0] // reps
        return pl.ds(pl.multiple_of(flip(rep, mask) * c, c), c)

    moved = {}
    for i in (3, 4, 5, 0, 1, 2):
        red, o = reds[i], outs[i]
        done = red.sums.at[0]
        if i in (4, 5):
            moved[i] = [net.own(done.at[0], o.at[rows(o, 0)])]
            continue
        n = done.shape[2]

        def place(n=n):
            return pl.ds(pl.multiple_of(me * n, n), n)

        moved[i] = [
            net.to("shard", j, done.at[flip(me, j)], o.at[rows(o, 0), place()])
            for j in range(1, group)
        ] + [net.own(done.at[me], o.at[rows(o, 0), place()])]
    streams, flights = [], []
    for i in (5, 3, 4, 0, 1, 2):
        for copy in moved[i][:-1]:
            copy.wait_recv()
        moved[i][-1].wait()
        o = outs[i]
        lanes = o.shape[1] // 2
        for n, order in enumerate(flips):
            c = pl.ds(n * lanes, lanes)
            s = rep_gather(net, lambda h, o=o, c=c: o.at[rows(o, h), c], order)
            streams.append(s)
            flights.append(next(s))
    for copy in tiny:
        copy.wait_recv()
    own.wait()
    total = zland[0]
    for h in range(1, reps):
        total = total + zland[h]
    smalls[...] = total
    for _ in range(len(rmasks)):
        for i, s in enumerate(streams):
            for copy in flights[i]:
                copy.wait_recv()
            flights[i] = next(s, [])
    net.finish()


def call(body, number, sizes, outs, scratch, copies, args):
    return pl.pallas_call(
        functools.partial(body, sizes),
        out_shape=[jax.ShapeDtypeStruct(s, d) for s, d in outs],
        in_specs=[VM] * len(args),
        out_specs=[VM] * len(outs),
        scratch_shapes=list(scratch)
        + [pltpu.SemaphoreType.DMA((copies,)), pltpu.SemaphoreType.DMA((copies,))],
        compiler_params=pltpu.CompilerParams(
            collective_id=number, has_side_effects=True, vmem_limit_bytes=LIMIT
        ),
        name=body.__name__,
    )(*args)


def dot(a, b):
    return jnp.dot(a, b, preferred_element_type=F32)


def dot_nt(a, b):
    return jnp.einsum("tc,rc->tr", a, b, preferred_element_type=F32)


def dot_tn(a, b):
    return jnp.einsum("tr,tc->rc", a, b, preferred_element_type=F32)


def local(
    block_input,
    lengths,
    first_gain,
    first_shift,
    query_weight,
    query_bias,
    key_weight,
    value_weight,
    value_bias,
    out_weight,
    out_bias,
    second_gain,
    second_shift,
    up_weight,
    up_bias,
    down_weight,
    down_bias,
    cotangent,
):
    rows, width = block_input.shape[1], block_input.shape[2]
    hidden = up_weight.shape[1]
    group, reps = lax.axis_size("shard"), lax.axis_size("rep")
    sizes = (group, reps)
    g, f = width // group, hidden // group
    head = width // HEADS
    scale = 1.0 / math.sqrt(head)
    me = lax.axis_index("shard")
    small = jnp.stack(
        [
            first_gain.astype(F32),
            first_shift.astype(F32),
            out_bias.astype(F32),
            second_gain.astype(F32),
            second_shift.astype(F32),
            down_bias.astype(F32),
            jnp.full((g,), 1.0, F32) * lengths[0].astype(F32),
            jnp.zeros((g,), F32),
        ]
    )
    x, cot = block_input[0], cotangent[0]
    blocks = (group, rows, width)
    nrm, mix, small_all, wq, wk, wv, wu = call(
        gather_kernel,
        1,
        sizes,
        [
            (blocks, BF),
            (blocks, BF),
            ((8, width), F32),
            ((group, g, g), BF),
            ((group, g, g), BF),
            ((group, g, g), BF),
            ((group, g, f), BF),
        ],
        [],
        320,
        (x, cot, small, query_weight, key_weight, value_weight, up_weight),
    )
    flat = lambda a: a.reshape(-1, a.shape[-1])
    normed = flat(nrm)
    wq, wk, wv, wu = flat(wq), flat(wk), flat(wv), flat(wu)
    queries = (dot(normed, wq) + query_bias.astype(F32)).astype(BF)
    keys = dot(normed, wk).astype(BF)
    values = (dot(normed, wv) + value_bias.astype(F32)).astype(BF)
    shape = (group, rows, g // head, head)
    qh, kh, vh = (a.reshape(shape) for a in (queries, keys, values))
    lens = small_all[LN].reshape(group, g)[:, 0]
    order = jnp.bitwise_xor(jnp.arange(group, dtype=jnp.int32), me)
    lens = jnp.take(lens, order).astype(jnp.int32)
    pos = jnp.arange(rows, dtype=jnp.int32)
    valid = (pos[None, None, :] <= pos[None, :, None]) & (pos[None, None, :] < lens[:, None, None])
    scores = jnp.einsum("bqhd,bkhd->bhqk", qh, kh, preferred_element_type=F32) * scale
    scores = jnp.where(valid[:, None], scores, -1e30)
    top = jnp.max(scores, axis=-1, keepdims=True)
    expo = jnp.exp(scores - top)
    p = expo / jnp.sum(expo, axis=-1, keepdims=True)
    p_low = p.astype(BF)
    ctx = (
        jnp.einsum("bhqk,bkhd->bqhd", p_low, vh, preferred_element_type=F32)
        .astype(BF)
        .reshape(group * rows, g)
    )
    part = dot(ctx, out_weight).astype(BF).reshape(blocks)
    masks = shard_masks(group)
    work = reduce_shapes(group, rows, width, masks)
    mid, second = call(
        middle_kernel,
        2,
        sizes,
        [((rows, width), F32), (blocks, BF)],
        work,
        96,
        (part, x, small_all),
    )
    second = flat(second)
    mixed = flat(mix)
    upper = dot(second, wu) + up_bias.astype(F32)
    cdf = 0.5 * (1.0 + lax.erf(upper * (1.0 / math.sqrt(2.0))))
    pdf = jnp.exp(-0.5 * upper * upper) * (1.0 / math.sqrt(2.0 * math.pi))
    active = (upper * cdf).astype(BF)
    gup = (dot_nt(mixed, down_weight) * (cdf + upper * pdf)).astype(BF)
    gpart = dot_nt(gup, wu).astype(BF).reshape(blocks)
    dpart = dot(active, down_weight).astype(BF).reshape(blocks)
    out, gmid, sums3, branch = call(
        branch_kernel,
        3,
        sizes,
        [((rows, width), BF), ((rows, width), F32), ((8, width), F32), (blocks, BF)],
        work + work,
        160,
        (dpart, gpart, mid, cot, small_all),
    )
    branch = flat(branch)
    gctx = dot_nt(branch, out_weight).astype(BF).reshape(shape)
    gw = jnp.einsum("bqhd,bkhd->bhqk", gctx, vh, preferred_element_type=F32)
    inner = jnp.sum(p * gw, axis=-1, keepdims=True)
    gs = (p * (gw - inner)).astype(BF)
    join = lambda a: a.astype(BF).reshape(group * rows, g)
    gq = join(jnp.einsum("bhqk,bkhd->bqhd", gs, kh, preferred_element_type=F32) * scale)
    gk = join(jnp.einsum("bhqk,bqhd->bkhd", gs, qh, preferred_element_type=F32) * scale)
    gv = join(jnp.einsum("bhqk,bqhd->bkhd", p_low, gctx, preferred_element_type=F32))
    npart = (dot_nt(gq, wq) + dot_nt(gk, wk) + dot_nt(gv, wv)).astype(BF).reshape(blocks)
    total = lambda a: jnp.sum(a.astype(F32), axis=0)
    cols = jnp.concatenate(
        [
            total(gq)[None],
            total(gv)[None],
            total(gup).reshape(4, g),
            jnp.zeros((2, g), F32),
        ]
    )
    grads = (
        dot_tn(normed, gq).astype(BF).reshape(group, g, g),
        dot_tn(normed, gk).astype(BF).reshape(group, g, g),
        dot_tn(normed, gv).astype(BF).reshape(group, g, g),
        dot_tn(second, gup).astype(BF).reshape(group, g, f),
        dot_tn(ctx, branch).astype(BF).reshape(1, g, width),
        dot_tn(active, mixed).astype(BF).reshape(1, f, width),
    )
    scratch = list(work)
    for a in grads:
        scratch += sum_shapes(a.shape, reps)
    scratch += [
        pltpu.VMEM((8, width), F32),
        pltpu.VMEM((group, 8, g), F32),
        pltpu.VMEM((16, g), F32),
        pltpu.VMEM((reps, 16, g), F32),
    ]
    gin, smalls, *weights = call(
        final_kernel,
        4,
        sizes,
        [
            ((rows, width), BF),
            ((16, g), F32),
            ((g, width), BF),
            ((g, width), BF),
            ((g, width), BF),
            ((g, hidden), BF),
            ((g, width), BF),
            ((f, width), BF),
        ],
        scratch,
        320,
        (npart, x, gmid, small_all, sums3, cols) + grads,
    )
    dq, dk, dv, du, do, dd = (w.astype(F32) for w in weights)
    return (
        out[None],
        gin[None],
        smalls[FG],
        smalls[FS],
        dq,
        smalls[8],
        dk,
        dv,
        smalls[9],
        do,
        smalls[OB],
        smalls[SG],
        smalls[SS],
        du,
        smalls[10:14].reshape(-1),
        dd,
        smalls[DB],
    )


def solution(mesh):
    tokens = P(("rep", "shard"), None, None)
    vec, mat = P("shard"), P("shard", None)
    return jax.shard_map(
        local,
        mesh=mesh,
        in_specs=(
            tokens,
            P(("rep", "shard")),
            vec,
            vec,
            mat,
            vec,
            mat,
            mat,
            vec,
            mat,
            vec,
            vec,
            vec,
            mat,
            vec,
            mat,
            vec,
            tokens,
        ),
        out_specs=(
            tokens,
            tokens,
            vec,
            vec,
            mat,
            vec,
            mat,
            mat,
            vec,
            mat,
            vec,
            vec,
            vec,
            mat,
            vec,
            mat,
            vec,
        ),
        check_vma=False,
    )
```

```python
import functools
import math

import jax
import jax.numpy as jnp
from jax import lax
from jax.experimental import pallas as pl
from jax.experimental.pallas import tpu as pltpu
from jax.sharding import PartitionSpec as P

HEADS = 16
MESH = pl.DeviceIdType.MESH
BF = jnp.bfloat16
F32 = jnp.float32
VM = pl.BlockSpec(memory_space=pltpu.VMEM)
LIMIT = 60 * 2**20
SIZE = None


def flip(index, mask):
    bit = 1
    while bit <= mask:
        if mask & bit:
            index = index + bit - 2 * bit * ((index // bit) % 2)
        bit *= 2
    return index


def span(masks):
    out = [0]
    for m in masks:
        out = out + [h ^ m for h in out]
    return out


def pair_masks(size):
    masks, bit = [], 1
    while bit < size:
        masks.append(bit + bit // 2 if len(masks) % 2 and size >= 2 * bit else bit)
        bit *= 2
    return masks


def shard_masks(size):
    masks, bit = [], 2
    while bit < size:
        masks.append(bit if len(masks) < 2 else bit + bit // 2)
        bit *= 2
    return masks


def orders(masks):
    return [list(masks), list(masks[1:]) + list(masks[:1])]


class Net:
    def __init__(self, send, recv):
        self.send, self.recv, self.used, self.open = send, recv, 0, []

    def to(self, axis, mask, src, dst):
        k = self.used
        self.used += 1
        copy = pltpu.make_async_remote_copy(
            src_ref=src,
            dst_ref=dst,
            send_sem=self.send.at[k],
            recv_sem=self.recv.at[k],
            device_id={axis: flip(lax.axis_index(axis), mask)},
            device_id_type=MESH,
        )
        copy.start()
        self.open.append(copy)
        return copy

    def own(self, src, dst):
        k = self.used
        self.used += 1
        copy = pltpu.make_async_copy(src, dst, self.send.at[k])
        copy.start()
        return copy

    def finish(self):
        for copy in self.open:
            copy.wait_send()


def meet(shard_set, rep_set):
    barrier = pltpu.get_barrier_semaphore()
    for axis, masks in (("shard", shard_set), ("rep", rep_set)):
        for m in masks:
            pl.semaphore_signal(
                barrier,
                inc=1,
                device_id={axis: flip(lax.axis_index(axis), m)},
                device_id_type=MESH,
            )
    pl.semaphore_wait(barrier, len(shard_set) + len(rep_set))


class Gather:
    def __init__(self, net, buf, masks):
        self.net, self.buf = net, buf
        rows = buf.shape[1] // 2
        self.parts = [
            dict(rows=pl.ds(i * rows, rows), order=o, held=[0], new=[0], wait=[], step=0)
            for i, o in enumerate(orders(masks))
        ]
        self.cores = []
        self.steps = len(masks)

    def start(self, n):
        net, buf, part = self.net, self.buf, self.parts[n]
        fresh, rows = part["new"], part["rows"]
        if part["step"] < self.steps:
            m = part["order"][part["step"]]
            part["new"] = [h ^ m for h in part["held"]]
            part["wait"] = [
                net.to("shard", m, buf.at[h, rows], buf.at[h ^ m, rows]) for h in part["held"]
            ]
            part["held"] = part["held"] + part["new"]
        self.cores += [net.to("shard", 1, buf.at[h, rows], buf.at[h ^ 1, rows]) for h in fresh]
        part["step"] += 1

    def arrive(self, n):
        for copy in self.parts[n]["wait"]:
            copy.wait_recv()
        self.parts[n]["wait"] = []

    def both(self):
        for n in range(2):
            self.arrive(n)
            self.start(n)

    def end(self):
        for copy in self.cores:
            copy.wait_recv()

    def finish(self):
        for _ in range(self.steps):
            self.both()
        self.end()


def reduce_shapes(group, rows, width, masks):
    count = 2 ** len(masks) - 1
    return [
        pltpu.VMEM((group // 2, rows, width), BF),
        pltpu.VMEM((count, rows, width), BF),
    ]


class Reduce:
    def __init__(self, net, part, work, masks):
        self.net, self.part = net, part
        self.sums, self.land = work
        self.group, self.rows = part.shape[0], part.shape[1]
        self.cores = {}
        self.half = self.rows // 2
        self.steps = len(masks)
        self.orders = orders(masks)
        self.flight = [[], []]
        first = [o[0] for o in self.orders]
        self.sequence = sorted(
            span(masks), key=lambda h: -sum(self.sends(n, h) for n in range(2))
        )

    def sends(self, n, h):
        order = self.orders[n]
        return h not in span(order[1:])

    def begin(self):
        for h in self.sequence:
            self.cores[h] = self.net.to(
                "shard", 1, self.part.at[h ^ 1], self.sums.at[h // 2]
            )

    def add(self, h, start, count, other):
        step = min(count, 32)

        @pl.loop(0, count // step)
        def _(i):
            at = pl.ds(pl.multiple_of(start + i * step, step), step)
            self.sums[h // 2, at] = (
                self.sums[h // 2, at].astype(F32) + other[at].astype(F32)
            ).astype(BF)

    def send(self, n, k, h):
        order = self.orders[n]
        rest = span(order[k + 1 :])
        base = sum(2 ** (self.steps - 1 - i) for i in range(k))
        to = h ^ order[k]
        rows = pl.ds(n * self.half, self.half)
        slot = base + rest.index(to)
        copy = self.net.to(
            "shard", order[k], self.sums.at[h // 2, rows], self.land.at[slot, rows]
        )
        self.flight[n].append((copy, to, slot))

    def prepare(self):
        for h in self.sequence:
            self.cores[h].wait_recv()
            self.add(h, 0, self.rows, self.part.at[h])
            for n in range(2):
                if self.sends(n, h):
                    self.send(n, 0, h)

    def advance(self, n, k):
        flight, self.flight[n] = self.flight[n], []
        rest = span(self.orders[n][k + 2 :])
        flight.sort(key=lambda f: f[1] in rest)
        for copy, h, slot in flight:
            copy.wait_recv()
            if k < self.steps - 1:
                self.add(h, n * self.half, self.half, self.land.at[slot])
                if h not in rest:
                    self.send(n, k + 1, h)
            else:
                self.last = slot

    def run(self):
        self.begin()
        self.prepare()
        for k in range(self.steps - 1):
            for n in range(2):
                self.advance(n, k)

    def total(self, at):
        return self.sums[0, at].astype(F32) + self.land[self.last, at].astype(F32)


def norm_rows(v):
    center = v - jnp.mean(v, axis=-1, keepdims=True)
    spread = jnp.mean(center * center, axis=-1, keepdims=True)
    inv = lax.rsqrt(spread + 1e-05)
    return center * inv, inv


def norm_back(grad, gain, n, inv):
    scaled = grad * gain
    return inv * (
        scaled
        - jnp.mean(scaled, axis=-1, keepdims=True)
        - n * jnp.mean(scaled * n, axis=-1, keepdims=True)
    )


FG, FS, OB, SG, SS, DB, LN = range(7)


def live_rows(length, start, rows):
    at = start + lax.broadcasted_iota(jnp.int32, (rows, 1), 0)
    return (at.astype(F32) < length).astype(F32)


def by_rows(n, count, body):
    step = 16

    @pl.loop(0, count // 2 // step)
    def _(i):
        start = pl.multiple_of(n * (count // 2) + i * step, step)
        body(pl.ds(start, step), start)


def gather_kernel(
    sizes,
    x_ref,
    small_ref,
    q_ref,
    k_ref,
    v_ref,
    u_ref,
    nrm,
    small_all,
    wq,
    wk,
    wv,
    wu,
    send,
    recv,
):
    group, reps = sizes
    me, rep = lax.axis_index("shard"), lax.axis_index("rep")
    net = Net(send, recv)
    masks = shard_masks(group)
    meet(range(1, group), [])
    width = small_ref.shape[1]
    mine = pl.ds(pl.multiple_of(me * width, width), width)
    small = [
        net.to("shard", j, small_ref, small_all.at[:, mine]) for j in range(1, group)
    ]
    own_small = net.own(small_ref, small_all.at[:, mine])

    def scatter(src, dst, first, n):
        part = src.shape[1] // group

        def columns(j):
            return pl.ds(pl.multiple_of(flip(me, j) * part + first, n), n)

        return [
            net.to("shard", j, src.at[:, columns(j)], dst.at[me]) for j in range(1, group)
        ] + [net.own(src.at[:, columns(0)], dst.at[me])]

    moved = scatter(q_ref, wq, 0, width) + scatter(k_ref, wk, 0, width)
    for copy in small:
        copy.wait_recv()
    own_small.wait()
    gather = Gather(net, nrm, masks)
    for n in range(2):

        def one(at, start):
            v, _ = norm_rows(x_ref[at].astype(F32))
            nrm[0, at] = (v * small_all[FG : FG + 1] + small_all[FS : FS + 1]).astype(BF)

        by_rows(n, x_ref.shape[0], one)
        gather.start(n)
    moved += scatter(v_ref, wv, 0, width)
    quarter = wu.shape[2]
    moved += scatter(u_ref, wu, rep * quarter, quarter)
    gather.finish()
    for i, copy in enumerate(moved):
        if i % group == group - 1:
            copy.wait()
        else:
            copy.wait_recv()
    net.finish()


def middle_kernel(sizes, part, x_ref, cot_ref, small, mid, second, mix, *work):
    group, _ = sizes
    net = Net(*work[-2:])
    masks = shard_masks(group)
    meet([1] + masks, [])
    me = lax.axis_index("shard")
    width = small.shape[1] // group
    length = small[LN : LN + 1, pl.ds(pl.multiple_of(me * width, width), 128)][:, :1]
    rows = x_ref.shape[0]
    red = Reduce(net, part, work[:2], masks)
    red.begin()
    gmix = Gather(net, mix, masks)
    for n in range(2):

        def live(at, start):
            mix[0, at] = (cot_ref[at].astype(F32) * live_rows(length, start, 16)).astype(BF)

        by_rows(n, rows, live)
        gmix.start(n)
    red.prepare()
    for k in range(red.steps - 1):
        for n in range(2):
            red.advance(n, k)
    gather = Gather(net, second, masks)
    gmix.both()
    for n in range(2):
        red.advance(n, red.steps - 1)

        def norm(at, start):
            m = x_ref[at].astype(F32) + (red.total(at) + small[OB : OB + 1])
            mid[at] = m
            v, _ = norm_rows(m)
            second[0, at] = (v * small[SG : SG + 1] + small[SS : SS + 1]).astype(BF)

        by_rows(n, rows, norm)
        gather.start(n)
    for _ in range(gather.steps - 1):
        gmix.both()
        gather.both()
    gather.both()
    gmix.end()
    gather.end()
    net.finish()


def branch_kernel(
    sizes, down, grad, up, mid, cot, small, out, gmid, sums, branch, up_rows, *work
):
    group, _ = sizes
    net = Net(*work[-2:])
    masks = shard_masks(group)
    meet(range(1, group), [])
    me = lax.axis_index("shard")
    width = small.shape[1] // group
    rows = mid.shape[0]
    length = small[LN : LN + 1, pl.ds(pl.multiple_of(me * width, width), 128)][:, :1]
    red = Reduce(net, grad, work[:2], masks)
    red.run()
    late = Reduce(net, down, work[2:4], masks)
    late.begin()
    sums[...] = jnp.zeros_like(sums)
    gather = Gather(net, branch, masks)
    for n in range(2):
        red.advance(n, red.steps - 1)

        def back(at, start):
            g = red.total(at)
            v, inv = norm_rows(mid[at])
            gout = cot[at].astype(F32) * live_rows(length, start, 16)
            res = gout + norm_back(g, small[SG : SG + 1], v, inv)
            gmid[at] = res
            low = res.astype(BF)
            branch[0, at] = low
            sums[SG : SG + 1] += jnp.sum(g * v, axis=0, keepdims=True)
            sums[SS : SS + 1] += jnp.sum(g, axis=0, keepdims=True)
            sums[OB : OB + 1] += jnp.sum(low.astype(F32), axis=0, keepdims=True)
            sums[DB : DB + 1] += jnp.sum(gout, axis=0, keepdims=True)

        by_rows(n, rows, back)
        gather.start(n)
    wide = up.shape[2]
    each = mid.shape[1] // wide
    place = pl.ds(pl.multiple_of((me % each) * wide, wide), wide)
    tall = up.shape[1]
    down_to = pl.ds(pl.multiple_of((me // each) * tall, tall), tall)
    target = up_rows.at[down_to, place]
    moved = [net.to("shard", j, up.at[flip(me, j)], target) for j in range(1, group)]
    own = net.own(up.at[me], target)
    late.prepare()
    for k in range(gather.steps):
        gather.both()
        for n in range(2):
            late.advance(n, k)
    gather.end()
    for n in range(2):

        def close(at, start):
            v = mid[at] + (late.total(at) + small[DB : DB + 1])
            out[at] = (v * live_rows(length, start, 16)).astype(BF)

        by_rows(n, rows, close)
    for copy in moved:
        copy.wait_recv()
    own.wait()
    net.finish()


class Line:
    def __init__(self, own, land, out, tall, reps, sems):
        self.own, self.land, self.out = own, land, out
        self.rep, self.reps, self.sems = lax.axis_index("rep"), reps, sems
        self.count, self.size = land.shape[1], land.shape[2]
        self.tall, self.each = tall, tall // 2 // self.size
        self.skew = 2
        self.steps = self.count + 2 * self.skew * (reps - 1)

    def rows(self, way, i):
        row = (i // self.each) * self.tall + way * (self.tall // 2) + (i % self.each) * self.size
        return pl.ds(pl.multiple_of(row, self.size), self.size)

    def copy(self, src, dst, way, back, i, up):
        s, r = self.sems
        at = (2 * way + back) * self.count + i
        return pltpu.make_async_remote_copy(
            src_ref=src,
            dst_ref=dst,
            send_sem=s.at[at],
            recv_sem=r.at[at],
            device_id={"rep": self.rep + (1 if up else -1)},
            device_id_type=MESH,
        )

    def place(self, way):
        return self.rep if way == 0 else self.reps - 1 - self.rep

    def forth(self, way, t):
        at = self.place(way)
        i, last = t - self.skew * at, self.reps - 1

        @pl.when((i >= 0) & (i < self.count))
        def _():
            rows, land = self.rows(way, i), self.land.at[way, i]

            @pl.when(at == 0)
            def _():
                self.copy(self.own.at[rows], land, way, 0, i, way == 0).start()

            @pl.when(at != 0)
            def _():
                self.copy(self.own.at[rows], land, way, 0, i, way == 0).wait_recv()

            @pl.when((at != 0) & (at != last))
            def _():
                self.add(land, rows, land)
                self.copy(land, land, way, 0, i, way == 0).start()

            @pl.when(at == last)
            def _():
                out = self.out.at[rows]
                self.add(land, rows, out)
                self.copy(out, out, way, 1, i, way != 0).start()

    def add(self, land, rows, to):
        own, step = self.own.at[rows], 16

        @pl.loop(0, self.size // step)
        def _(n):
            at = pl.ds(pl.multiple_of(n * step, step), step)
            to[at] = (land[at].astype(F32) + own[at].astype(F32)).astype(BF)

    def back(self, way, t):
        at, last = self.place(way), self.reps - 1
        i = t - self.skew * (last + last - at)

        @pl.when((at != last) & (i >= 0) & (i < self.count))
        def _():
            out = self.out.at[self.rows(way, i)]
            self.copy(out, out, way, 1, i, way != 0).wait_recv()

            @pl.when(at != 0)
            def _():
                self.copy(out, out, way, 1, i, way != 0).start()

    def step(self, t):
        for way in (0, 1):
            self.forth(way, t)
        for way in (0, 1):
            self.back(way, t)

    def finish(self):
        last = self.reps - 1
        for way in (0, 1):
            at = self.place(way)

            @pl.loop(0, self.count)
            def _(i):
                out = self.out.at[self.rows(way, i)]

                @pl.when(at != last)
                def _():
                    self.copy(out, out, way, 0, i, way == 0).wait_send()

                @pl.when(at != 0)
                def _():
                    self.copy(out, out, way, 1, i, way != 0).wait_send()


def final_kernel(sizes, *refs):
    group, reps = sizes
    grad, x_ref, gmid, small, sums3, cols = refs[:6]
    arrays = refs[6:10]
    up_rows = refs[10]
    gin, smalls = refs[11:13]
    whole = refs[13]
    work = refs[14:]
    sums, land, both, zland, mine_all, line_land = work[2:8]
    net = Net(*work[-2:])
    masks = shard_masks(group)
    me, rep = lax.axis_index("shard"), lax.axis_index("rep")
    meet(range(1, group), range(1, reps))
    width, rows = smalls.shape[1], x_ref.shape[0]
    place = pl.ds(pl.multiple_of(me * width, width), width)
    tall = arrays[3].shape[0]
    wide = up_rows.shape[0]
    moved = [[net.own(up_rows, mine_all.at[0:wide]), net.own(arrays[3], mine_all.at[pl.ds(wide, tall)])]]
    for i, src in enumerate(arrays[:3]):
        dst = mine_all.at[pl.ds(wide + (i + 1) * tall, tall)]
        moved.append(
            [
                net.to("shard", j, src.at[flip(me, j)], dst.at[:, place])
                for j in range(1, group)
            ]
            + [net.own(src.at[me], dst.at[:, place])]
        )
    line = Line(mine_all, line_land, whole, tall, reps, work[-4:-2])
    red = Reduce(net, grad, work[:2], masks)

    def tasks():
        red.begin()
        yield
        red.prepare()
        for k in range(red.steps - 1):
            for n in range(2):
                yield
                red.advance(n, k)
        sums[...] = sums3[...]
        for n in range(2):
            yield
            red.advance(n, red.steps - 1)

            def back(at, start):
                g = red.total(at)
                w, inv = norm_rows(x_ref[at].astype(F32))
                gin[at] = (gmid[at] + norm_back(g, small[FG : FG + 1], w, inv)).astype(BF)
                sums[FG : FG + 1] += jnp.sum(g * w, axis=0, keepdims=True)
                sums[FS : FS + 1] += jnp.sum(g, axis=0, keepdims=True)

            by_rows(n, rows, back)

        def mine(j):
            return pl.ds(pl.multiple_of(flip(me, j) * width, width), width)

        tiny = [net.to("shard", j, sums.at[:, mine(j)], land.at[me]) for j in range(1, group)]
        own = net.own(sums.at[:, mine(0)], land.at[me])
        yield
        yield
        for copy in tiny:
            copy.wait_recv()
        own.wait()
        total = land[0]
        for j in range(1, group):
            total = total + land[j]
        both[0:8] = total
        both[8:16] = cols[...]
        tiny = [net.to("rep", h, both, zland.at[rep]) for h in range(1, reps)]
        own = net.own(both, zland.at[rep])
        yield
        yield
        yield
        for copy in tiny:
            copy.wait_recv()
        own.wait()
        total = zland[0]
        for h in range(1, reps):
            total = total + zland[h]
        smalls[...] = total

    todo = tasks()
    next(todo)
    for t in range(line.steps):
        i = t // line.each - wide // tall
        if t == 0:
            for copy in moved[0]:
                copy.wait()
        elif t < line.count and t % line.each == 0 and i > 0:
            for copy in moved[i][:-1]:
                copy.wait_recv()
            moved[i][-1].wait()
        line.step(t)
        if t >= 15 and t % 4 == 3:
            next(todo, None)
    for _ in todo:
        pass
    line.finish()
    net.finish()


def call(body, number, sizes, outs, scratch, copies, args):
    return pl.pallas_call(
        functools.partial(body, sizes),
        out_shape=[jax.ShapeDtypeStruct(s, d) for s, d in outs],
        in_specs=[VM] * len(args),
        out_specs=[VM] * len(outs),
        scratch_shapes=list(scratch)
        + [pltpu.SemaphoreType.DMA((copies,)), pltpu.SemaphoreType.DMA((copies,))],
        compiler_params=pltpu.CompilerParams(
            collective_id=number, has_side_effects=True, vmem_limit_bytes=LIMIT
        ),
        name=body.__name__,
    )(*args)


def dot(a, b):
    return jnp.dot(a, b, preferred_element_type=F32)


def dot_nt(a, b):
    return jnp.einsum("tc,rc->tr", a, b, preferred_element_type=F32)


def dot_tn(a, b):
    return jnp.einsum("tr,tc->rc", a, b, preferred_element_type=F32)


def local(
    block_input,
    lengths,
    first_gain,
    first_shift,
    query_weight,
    query_bias,
    key_weight,
    value_weight,
    value_bias,
    out_weight,
    out_bias,
    second_gain,
    second_shift,
    up_weight,
    up_bias,
    down_weight,
    down_bias,
    cotangent,
):
    rows, width = block_input.shape[1], block_input.shape[2]
    hidden = up_weight.shape[1]
    group, reps = lax.axis_size("shard"), lax.axis_size("rep")
    sizes = (group, reps)
    g, f = width // group, hidden // group
    head = width // HEADS
    scale = 1.0 / math.sqrt(head)
    me = lax.axis_index("shard")
    small = jnp.stack(
        [
            first_gain.astype(F32),
            first_shift.astype(F32),
            out_bias.astype(F32),
            second_gain.astype(F32),
            second_shift.astype(F32),
            down_bias.astype(F32),
            jnp.full((g,), 1.0, F32) * lengths[0].astype(F32),
            jnp.zeros((g,), F32),
        ]
    )
    x, cot = block_input[0], cotangent[0]
    blocks = (group, rows, width)
    parts = reps if f // reps % 128 == 0 else 1
    nrm, small_all, wq, wk, wv, wu = call(
        gather_kernel,
        1,
        sizes,
        [
            (blocks, BF),
            ((8, width), F32),
            ((group, g, g), BF),
            ((group, g, g), BF),
            ((group, g, g), BF),
            ((group, g, f // parts), BF),
        ],
        [],
        200,
        (x, small, query_weight, key_weight, value_weight, up_weight),
    )
    flat = lambda a: a.reshape(-1, a.shape[-1])
    normed = flat(nrm)
    wq, wk, wv, wu = flat(wq), flat(wk), flat(wv), flat(wu)
    if parts > 1:
        wu = lax.all_gather(wu, "rep", axis=0).transpose(1, 0, 2).reshape(width, f)
    queries = (dot(normed, wq) + query_bias.astype(F32)).astype(BF)
    keys = dot(normed, wk).astype(BF)
    values = (dot(normed, wv) + value_bias.astype(F32)).astype(BF)
    shape = (group, rows, g // head, head)
    qh, kh, vh = (a.reshape(shape) for a in (queries, keys, values))
    lens = small_all[LN].reshape(group, g)[:, 0]
    order = jnp.bitwise_xor(jnp.arange(group, dtype=jnp.int32), me)
    lens = jnp.take(lens, order).astype(jnp.int32)
    pos = jnp.arange(rows, dtype=jnp.int32)
    valid = (pos[None, None, :] <= pos[None, :, None]) & (pos[None, None, :] < lens[:, None, None])
    scores = jnp.einsum("bqhd,bkhd->bhqk", qh, kh, preferred_element_type=F32) * scale
    scores = jnp.where(valid[:, None], scores, -1e30)
    top = jnp.max(scores, axis=-1, keepdims=True)
    expo = jnp.exp(scores - top)
    p = expo / jnp.sum(expo, axis=-1, keepdims=True)
    p_low = p.astype(BF)
    ctx = (
        jnp.einsum("bhqk,bkhd->bqhd", p_low, vh, preferred_element_type=F32)
        .astype(BF)
        .reshape(group * rows, g)
    )
    part = dot(ctx, out_weight).astype(BF).reshape(blocks)
    masks = shard_masks(group)
    work = reduce_shapes(group, rows, width, masks)
    mid, second, mix = call(
        middle_kernel,
        2,
        sizes,
        [((rows, width), F32), (blocks, BF), (blocks, BF)],
        work,
        160,
        (part, x, cot, small_all),
    )
    second = flat(second)
    mixed = flat(mix)
    upper = dot(second, wu) + up_bias.astype(F32)
    cdf = 0.5 * (1.0 + lax.erf(upper * (1.0 / math.sqrt(2.0))))
    pdf = jnp.exp(-0.5 * upper * upper) * (1.0 / math.sqrt(2.0 * math.pi))
    active = (upper * cdf).astype(BF)
    gup = (dot_nt(mixed, down_weight) * (cdf + upper * pdf)).astype(BF)
    gpart = dot_nt(gup, wu).astype(BF).reshape(blocks)
    dpart = dot(active, down_weight).astype(BF).reshape(blocks)
    down_grad = lax.psum(dot_tn(active, mixed).astype(BF), "rep")
    up_part = dot_tn(second, gup).astype(BF).reshape(group, g, f)
    out, gmid, sums3, branch, up_rows = call(
        branch_kernel,
        3,
        sizes,
        [
            ((rows, width), BF),
            ((rows, width), F32),
            ((8, width), F32),
            (blocks, BF),
            ((hidden // width * g, width), BF),
        ],
        work + work,
        200,
        (dpart, gpart, up_part, mid, cot, small_all),
    )
    up_rows, down_grad = lax.optimization_barrier((up_rows, down_grad))
    branch = flat(branch)
    gctx = dot_nt(branch, out_weight).astype(BF).reshape(shape)
    gw = jnp.einsum("bqhd,bkhd->bhqk", gctx, vh, preferred_element_type=F32)
    inner = jnp.sum(p * gw, axis=-1, keepdims=True)
    gs = (p * (gw - inner)).astype(BF)
    join = lambda a: a.astype(BF).reshape(group * rows, g)
    gq = join(jnp.einsum("bhqk,bkhd->bqhd", gs, kh, preferred_element_type=F32) * scale)
    gk = join(jnp.einsum("bhqk,bqhd->bkhd", gs, qh, preferred_element_type=F32) * scale)
    gv = join(jnp.einsum("bhqk,bqhd->bkhd", p_low, gctx, preferred_element_type=F32))
    npart = (dot_nt(gq, wq) + dot_nt(gk, wk) + dot_nt(gv, wv)).astype(BF).reshape(blocks)
    total = lambda a: jnp.sum(a.astype(F32), axis=0)
    cols = jnp.concatenate(
        [
            total(gq)[None],
            total(gv)[None],
            total(gup).reshape(4, g),
            jnp.zeros((2, g), F32),
        ]
    )
    grads = (
        dot_tn(normed, gq).astype(BF).reshape(group, g, g),
        dot_tn(normed, gk).astype(BF).reshape(group, g, g),
        dot_tn(normed, gv).astype(BF).reshape(group, g, g),
        dot_tn(ctx, branch).astype(BF),
    )
    piece = 16
    blocks_up = hidden // width
    tall_all = (4 + blocks_up) * g
    count = (4 + blocks_up) * (g // 2 // piece)
    scratch = (
        list(work)
        + [
            pltpu.VMEM((8, width), F32),
            pltpu.VMEM((group, 8, g), F32),
            pltpu.VMEM((16, g), F32),
            pltpu.VMEM((reps, 16, g), F32),
            pltpu.VMEM((tall_all, width), BF),
            pltpu.VMEM((2, count, piece, width), BF),
        ]
        + [pltpu.SemaphoreType.DMA((4 * count,))] * 2
    )
    gin, smalls, whole = call(
        final_kernel,
        4,
        sizes,
        [((rows, width), BF), ((16, g), F32), ((tall_all, width), BF)],
        scratch,
        200,
        (npart, x, gmid, small_all, sums3, cols) + grads + (up_rows,),
    )
    do, dq, dk, dv = (
        whole[(i + blocks_up) * g : (i + blocks_up + 1) * g].astype(F32) for i in range(4)
    )
    du = whole[: blocks_up * g].reshape(blocks_up, g, width).transpose(1, 0, 2)
    du = du.reshape(g, hidden).astype(F32)
    dd = down_grad.astype(F32)
    return (
        out[None],
        gin[None],
        smalls[FG],
        smalls[FS],
        dq,
        smalls[8],
        dk,
        dv,
        smalls[9],
        do,
        smalls[OB],
        smalls[SG],
        smalls[SS],
        du,
        smalls[10:14].reshape(-1),
        dd,
        smalls[DB],
    )


def solution(mesh):
    tokens = P(("rep", "shard"), None, None)
    vec, mat = P("shard"), P("shard", None)
    return jax.shard_map(
        local,
        mesh=mesh,
        in_specs=(
            tokens,
            P(("rep", "shard")),
            vec,
            vec,
            mat,
            vec,
            mat,
            mat,
            vec,
            mat,
            vec,
            vec,
            vec,
            mat,
            vec,
            mat,
            vec,
            tokens,
        ),
        out_specs=(
            tokens,
            tokens,
            vec,
            vec,
            mat,
            vec,
            mat,
            mat,
            vec,
            mat,
            vec,
            vec,
            vec,
            mat,
            vec,
            mat,
            vec,
        ),
        check_vma=False,
    )
```

```python
import functools
import math

import jax
import jax.numpy as jnp
from jax import lax
from jax.experimental import pallas as pl
from jax.experimental.pallas import tpu as pltpu
from jax.sharding import PartitionSpec as P

HEADS = 16
MESH = pl.DeviceIdType.MESH
BF = jnp.bfloat16
F32 = jnp.float32
VM = pl.BlockSpec(memory_space=pltpu.VMEM)
ANY = pl.BlockSpec(memory_space=pl.ANY)
LIMIT = 63 * 2**20


def flip(index, mask):
    bit = 1
    while bit <= mask:
        if mask & bit:
            index = index + bit - 2 * bit * ((index // bit) % 2)
        bit *= 2
    return index


def span(masks):
    out = [0]
    for m in masks:
        out = out + [h ^ m for h in out]
    return out


def pair_masks(size):
    masks, bit = [], 1
    while bit < size:
        masks.append(bit + bit // 2 if len(masks) % 2 and size >= 2 * bit else bit)
        bit *= 2
    return masks


def shard_masks(size):
    masks, bit = [], 2
    while bit < size:
        masks.append(bit if len(masks) < 2 else bit + bit // 2)
        bit *= 2
    return masks


def orders(masks):
    return [list(masks), list(masks[1:]) + list(masks[:1])]


class Net:
    def __init__(self, send, recv):
        self.send, self.recv, self.used, self.open = send, recv, 0, []

    def to(self, axis, mask, src, dst):
        k = self.used
        self.used += 1
        copy = pltpu.make_async_remote_copy(
            src_ref=src,
            dst_ref=dst,
            send_sem=self.send.at[k],
            recv_sem=self.recv.at[k],
            device_id={axis: flip(lax.axis_index(axis), mask)},
            device_id_type=MESH,
        )
        copy.start()
        self.open.append(copy)
        return copy

    def own(self, src, dst):
        k = self.used
        self.used += 1
        copy = pltpu.make_async_copy(src, dst, self.send.at[k])
        copy.start()
        return copy

    def settle(self, count=None):
        for copy in self.open[:count]:
            copy.wait_send()
        self.open = self.open[len(self.open) if count is None else count :]

    finish = settle


def meet(shard_set, rep_set):
    barrier = pltpu.get_barrier_semaphore()
    for axis, masks in (("shard", shard_set), ("rep", rep_set)):
        for m in masks:
            pl.semaphore_signal(
                barrier,
                inc=1,
                device_id={axis: flip(lax.axis_index(axis), m)},
                device_id_type=MESH,
            )
    pl.semaphore_wait(barrier, len(shard_set) + len(rep_set))


class Gather:
    def __init__(self, net, buf, masks):
        self.net, self.buf = net, buf
        rows = buf.shape[1] // 2
        self.parts = [
            dict(rows=pl.ds(i * rows, rows), order=o, held=[0], new=[0], wait=[], step=0)
            for i, o in enumerate(orders(masks))
        ]
        self.cores = []
        self.steps = len(masks)

    def start(self, n):
        net, buf, part = self.net, self.buf, self.parts[n]
        fresh, rows = part["new"], part["rows"]
        if part["step"] < self.steps:
            m = part["order"][part["step"]]
            part["new"] = [h ^ m for h in part["held"]]
            part["wait"] = [
                net.to("shard", m, buf.at[h, rows], buf.at[h ^ m, rows]) for h in part["held"]
            ]
            part["held"] = part["held"] + part["new"]
        self.cores += [net.to("shard", 1, buf.at[h, rows], buf.at[h ^ 1, rows]) for h in fresh]
        part["step"] += 1

    def arrive(self, n):
        for copy in self.parts[n]["wait"]:
            copy.wait_recv()
        self.parts[n]["wait"] = []

    def both(self):
        for n in range(2):
            self.arrive(n)
            self.start(n)

    def end(self):
        for copy in self.cores:
            copy.wait_recv()

    def finish(self):
        for _ in range(self.steps):
            self.both()
        self.end()


def reduce_shapes(group, rows, width, masks):
    count = 2 ** len(masks) - 1
    return [
        pltpu.VMEM((group // 2, rows, width), BF),
        pltpu.VMEM((count, rows, width), BF),
    ]


class Reduce:
    def __init__(self, net, part, work, masks):
        self.net, self.part = net, part
        self.sums, self.land = work
        self.group, self.rows = part.shape[0], part.shape[1]
        self.cores = {}
        self.half = self.rows // 2
        self.steps = len(masks)
        self.orders = orders(masks)
        self.flight = [[], []]
        first = [o[0] for o in self.orders]
        self.sequence = sorted(
            span(masks), key=lambda h: -sum(self.sends(n, h) for n in range(2))
        )

    def sends(self, n, h):
        order = self.orders[n]
        return h not in span(order[1:])

    def begin(self):
        for h in self.sequence:
            self.cores[h] = self.net.to(
                "shard", 1, self.part.at[h ^ 1], self.sums.at[h // 2]
            )

    def add(self, h, start, count, other):
        step = min(count, 32)

        @pl.loop(0, count // step)
        def _(i):
            at = pl.ds(pl.multiple_of(start + i * step, step), step)
            self.sums[h // 2, at] = (
                self.sums[h // 2, at].astype(F32) + other[at].astype(F32)
            ).astype(BF)

    def send(self, n, k, h):
        order = self.orders[n]
        rest = span(order[k + 1 :])
        base = sum(2 ** (self.steps - 1 - i) for i in range(k))
        to = h ^ order[k]
        rows = pl.ds(n * self.half, self.half)
        slot = base + rest.index(to)
        copy = self.net.to(
            "shard", order[k], self.sums.at[h // 2, rows], self.land.at[slot, rows]
        )
        self.flight[n].append((copy, to, slot))

    def prepare(self):
        for h in self.sequence:
            self.cores[h].wait_recv()
            self.add(h, 0, self.rows, self.part.at[h])
            for n in range(2):
                if self.sends(n, h):
                    self.send(n, 0, h)

    def advance(self, n, k):
        flight, self.flight[n] = self.flight[n], []
        rest = span(self.orders[n][k + 2 :])
        flight.sort(key=lambda f: f[1] in rest)
        for copy, h, slot in flight:
            copy.wait_recv()
            if k < self.steps - 1:
                self.add(h, n * self.half, self.half, self.land.at[slot])
                if h not in rest:
                    self.send(n, k + 1, h)
            else:
                self.last = slot

    def run(self):
        self.begin()
        self.prepare()
        for k in range(self.steps - 1):
            for n in range(2):
                self.advance(n, k)

    def total(self, at):
        return self.sums[0, at].astype(F32) + self.land[self.last, at].astype(F32)


def norm_rows(v):
    center = v - jnp.mean(v, axis=-1, keepdims=True)
    spread = jnp.mean(center * center, axis=-1, keepdims=True)
    inv = lax.rsqrt(spread + 1e-05)
    return center * inv, inv


def norm_back(grad, gain, n, inv):
    scaled = grad * gain
    return inv * (
        scaled
        - jnp.mean(scaled, axis=-1, keepdims=True)
        - n * jnp.mean(scaled * n, axis=-1, keepdims=True)
    )


FG, FS, OB, SG, SS, DB, LN = range(7)


def live_rows(length, start, rows):
    at = start + lax.broadcasted_iota(jnp.int32, (rows, 1), 0)
    return (at.astype(F32) < length).astype(F32)


def by_rows(n, count, body):
    step = 16

    @pl.loop(0, count // 2 // step)
    def _(i):
        start = pl.multiple_of(n * (count // 2) + i * step, step)
        body(pl.ds(start, step), start)


def gather_kernel(
    sizes,
    x_ref,
    small_ref,
    q_ref,
    k_ref,
    v_ref,
    u_ref,
    nrm,
    small_all,
    wq,
    wk,
    wv,
    wu,
    send,
    recv,
):
    group, reps = sizes
    me, rep = lax.axis_index("shard"), lax.axis_index("rep")
    net = Net(send, recv)
    masks = shard_masks(group)
    meet(range(1, group), [])
    width = small_ref.shape[1]
    mine = pl.ds(pl.multiple_of(me * width, width), width)
    small = [
        net.to("shard", j, small_ref, small_all.at[:, mine]) for j in range(1, group)
    ]
    own_small = net.own(small_ref, small_all.at[:, mine])

    def scatter(src, dst, first, n):
        part = src.shape[1] // group

        def columns(j):
            return pl.ds(pl.multiple_of(flip(me, j) * part + first, n), n)

        return [
            net.to("shard", j, src.at[:, columns(j)], dst.at[me]) for j in range(1, group)
        ] + [net.own(src.at[:, columns(0)], dst.at[me])]

    moved = scatter(q_ref, wq, 0, width) + scatter(k_ref, wk, 0, width)
    for copy in small:
        copy.wait_recv()
    own_small.wait()
    gather = Gather(net, nrm, masks)
    for n in range(2):

        def one(at, start):
            v, _ = norm_rows(x_ref[at].astype(F32))
            nrm[0, at] = (v * small_all[FG : FG + 1] + small_all[FS : FS + 1]).astype(BF)

        by_rows(n, x_ref.shape[0], one)
        gather.start(n)
    moved += scatter(v_ref, wv, 0, width)
    quarter = wu.shape[2]
    moved += scatter(u_ref, wu, rep * quarter, quarter)
    gather.finish()
    for i, copy in enumerate(moved):
        if i % group == group - 1:
            copy.wait()
        else:
            copy.wait_recv()
    net.finish()


def middle_kernel(sizes, part, x_ref, cot_ref, small, mid, second, mix, *work):
    group, _ = sizes
    net = Net(*work[-2:])
    masks = shard_masks(group)
    meet([1] + masks, [])
    me = lax.axis_index("shard")
    width = small.shape[1] // group
    length = small[LN : LN + 1, pl.ds(pl.multiple_of(me * width, width), 128)][:, :1]
    rows = x_ref.shape[0]
    red = Reduce(net, part, work[:2], masks)
    red.begin()
    gmix = Gather(net, mix, masks)
    for n in range(2):

        def live(at, start):
            mix[0, at] = (cot_ref[at].astype(F32) * live_rows(length, start, 16)).astype(BF)

        by_rows(n, rows, live)
        gmix.start(n)
    red.prepare()
    for k in range(red.steps - 1):
        for n in range(2):
            red.advance(n, k)
    gather = Gather(net, second, masks)
    gmix.both()
    for n in range(2):
        red.advance(n, red.steps - 1)

        def norm(at, start):
            m = x_ref[at].astype(F32) + (red.total(at) + small[OB : OB + 1])
            mid[at] = m
            v, _ = norm_rows(m)
            second[0, at] = (v * small[SG : SG + 1] + small[SS : SS + 1]).astype(BF)

        by_rows(n, rows, norm)
        gather.start(n)
    for _ in range(gather.steps - 1):
        gmix.both()
        gather.both()
    gather.both()
    gmix.end()
    gather.end()
    net.finish()


class Line:
    def __init__(self, own, land, out, tall, reps, sems, kept):
        self.kept = kept
        self.own, self.land, self.out = own, land, out
        self.rep, self.reps, self.sems = lax.axis_index("rep"), reps, sems
        self.count, self.size = land.shape[1], land.shape[2]
        self.tall, self.each = tall, tall // 2 // self.size
        self.skew = 2
        self.steps = self.count + 2 * self.skew * (reps - 1)

    def rows(self, way, i):
        row = (i // self.each) * self.tall + way * (self.tall // 2) + (i % self.each) * self.size
        return pl.ds(pl.multiple_of(row, self.size), self.size)

    def copy(self, src, dst, way, back, i, up):
        s, r = self.sems
        at = (2 * way + back) * self.count + i
        return pltpu.make_async_remote_copy(
            src_ref=src,
            dst_ref=dst,
            send_sem=s.at[at],
            recv_sem=r.at[at],
            device_id={"rep": self.rep + (1 if up else -1)},
            device_id_type=MESH,
        )

    def place(self, way):
        return self.rep if way == 0 else self.reps - 1 - self.rep

    def forth(self, way, t):
        at = self.place(way)
        i, last = t - self.skew * at, self.reps - 1

        @pl.when((i >= 0) & (i < self.count))
        def _():
            rows, land = self.rows(way, i), self.land.at[way, i]

            @pl.when(at == 0)
            def _():
                self.copy(self.own.at[rows], land, way, 0, i, way == 0).start()

            @pl.when(at != 0)
            def _():
                self.copy(self.own.at[rows], land, way, 0, i, way == 0).wait_recv()

            @pl.when((at != 0) & (at != last))
            def _():
                self.add(land, rows, land)
                self.copy(land, land, way, 0, i, way == 0).start()

            @pl.when(at == last)
            def _():
                self.add(land, rows, land)
                self.copy(land, self.out.at[rows], way, 1, i, way != 0).start()
                self.keep(way, i).start()

    def add(self, land, rows, to):
        own, step = self.own.at[rows], 16

        @pl.loop(0, self.size // step)
        def _(n):
            at = pl.ds(pl.multiple_of(n * step, step), step)
            to[at] = (land[at].astype(F32) + own[at].astype(F32)).astype(BF)

    def keep(self, way, i):
        return pltpu.make_async_copy(
            self.land.at[way, i],
            self.out.at[self.rows(way, i)],
            self.kept.at[way * self.count + i],
        )

    def back(self, way, t):
        at, last = self.place(way), self.reps - 1
        i = t - self.skew * (last + last - at)

        @pl.when((at != last) & (i >= 0) & (i < self.count))
        def _():
            out = self.out.at[self.rows(way, i)]
            self.copy(out, out, way, 1, i, way != 0).wait_recv()

            @pl.when(at != 0)
            def _():
                self.copy(out, out, way, 1, i, way != 0).start()

    def step(self, t):
        for way in (0, 1):
            self.forth(way, t)
        for way in (0, 1):
            self.back(way, t)

    def finish(self):
        last = self.reps - 1
        for way in (0, 1):
            at = self.place(way)

            @pl.loop(0, self.count)
            def _(i):
                out = self.out.at[self.rows(way, i)]

                @pl.when(at != last)
                def _():
                    self.copy(out, out, way, 0, i, way == 0).wait_send()

                @pl.when(at != 0)
                def _():
                    self.copy(out, out, way, 1, i, way != 0).wait_send()

                @pl.when(at == last)
                def _():
                    self.keep(way, i).wait()


def final_kernel(sizes, head, *refs):
    group, reps = sizes
    (
        gpart,
        dpart,
        up_part,
        down_grad,
        mid,
        cot,
        x_ref,
        small,
        q,
        k,
        v,
        p_ref,
        ctx,
        nrm,
        wq,
        wk,
        wv,
        wo,
        cols,
    ) = refs[:19]
    out, gin, smalls, whole = refs[19:23]
    work = refs[23:]
    gmid, sums, land, both, zland, own_all, line_land = work[4:11]
    part, branch, g3, dw, nbuf, wbuf, loads = work[11:18]
    line_sems, kept = work[18:20], work[20]
    net = Net(*work[-2:])
    masks = shard_masks(group)
    me, rep = lax.axis_index("shard"), lax.axis_index("rep")
    width, rows, model = smalls.shape[1], x_ref.shape[0], x_ref.shape[1]
    heads = width // head
    scale = 1.0 / math.sqrt(head)
    tall = width
    down_rows, wide = down_grad.shape[0], up_part.shape[2]
    up_base = down_rows
    out_base = up_base + tall * (wide * group // model)
    loaded = [
        net.own(gpart, part),
        net.own(down_grad, own_all.at[pl.ds(0, down_rows)]),
    ]
    meet(range(1, group), range(1, reps))
    length = small[LN : LN + 1, pl.ds(pl.multiple_of(me * width, width), 128)][:, :1]
    line = Line(own_all, line_land, whole, tall, reps, line_sems, kept)
    for copy in loaded:
        copy.wait()
    arrivals = {}

    def place(j):
        return pl.ds(pl.multiple_of(flip(me, j) * width, width), width)

    def tasks():
        red = Reduce(net, part, work[:2], masks)
        red.begin()
        yield 3
        red.prepare()
        each = model // wide
        target = own_all.at[
            pl.ds(pl.multiple_of(up_base + (me // each) * tall, tall), tall),
            pl.ds(pl.multiple_of((me % each) * wide, wide), wide),
        ]
        arrivals[up_base] = [
            net.to("shard", j, up_part.at[flip(me, j)], target) for j in range(1, group)
        ] + [net.own(up_part.at[me], target)]
        yield 22
        for s in range(red.steps - 1):
            for n in range(2):
                red.advance(n, s)
        yield 28
        for n in range(2):
            red.advance(n, red.steps - 1)
        net.settle()
        sums[...] = jnp.zeros_like(sums)
        gather = Gather(net, branch, masks)
        for n in range(2):

            def back(at, start):
                g = red.total(at)
                w, inv = norm_rows(mid[at])
                gout = cot[at].astype(F32) * live_rows(length, start, 16)
                res = gout + norm_back(g, small[SG : SG + 1], w, inv)
                gmid[at] = res
                low = res.astype(BF)
                branch[0, at] = low
                sums[SG : SG + 1] += jnp.sum(g * w, axis=0, keepdims=True)
                sums[SS : SS + 1] += jnp.sum(g, axis=0, keepdims=True)
                sums[OB : OB + 1] += jnp.sum(low.astype(F32), axis=0, keepdims=True)
                sums[DB : DB + 1] += jnp.sum(gout, axis=0, keepdims=True)

            by_rows(n, rows, back)
            gather.start(n)
        for s in range(gather.steps):
            yield 33 + 5 * s
            gather.both()
        yield 33 + 5 * gather.steps
        gather.end()
        early = len(net.open)
        for b in range(group):
            at = pl.ds(b * rows, rows)
            gc = dot_nt(branch[b], wo[...]).astype(BF)
            for h in range(heads):
                lane = pl.ds(h * head, head)
                qh, kh, vh = q[at, lane], k[at, lane], v[at, lane]
                gch = gc[:, h * head : (h + 1) * head]
                p = p_ref[b, h]
                gw = dot_nt(gch, vh)
                inner = jnp.sum(p * gw, axis=-1, keepdims=True)
                gs = (p * (gw - inner)).astype(BF)
                g3[b, :, pl.ds(h * head, head)] = (dot(gs, kh) * scale).astype(BF)
                g3[b, :, pl.ds(width + h * head, head)] = (dot_tn(gs, qh) * scale).astype(BF)
                g3[b, :, pl.ds(2 * width + h * head, head)] = dot_tn(p.astype(BF), gch).astype(BF)
            yield 0
        n_col = 512
        for c in range(0, model, n_col):
            lane = pl.ds(c, n_col)
            full = branch[:, :, lane].reshape(group * rows, n_col)
            own_all[pl.ds(out_base, tall), lane] = dot_tn(ctx[...], full).astype(BF)
            yield 0
        arrivals[out_base] = []
        grads = g3[...].reshape(group * rows, 3 * width)
        total = jnp.sum(grads.astype(F32), axis=0, keepdims=True)
        both[8:9] = total[:, :width]
        both[9:10] = total[:, 2 * width :]
        both[10:16] = cols[...]

        def normed_of(j):
            return pltpu.make_async_copy(nrm.at[:, :, place(j)], nbuf.at[j % 2], loads.at[0, j % 2])

        normed_of(0).start()
        for i in range(3):
            arrivals[out_base + (i + 1) * tall] = []
        for j in range(group):
            if j + 1 < group:
                normed_of(j + 1).start()
            normed_of(j).wait()
            left = nbuf[j % 2].reshape(group * rows, width)
            right = g3[...].reshape(group * rows, 3 * width)
            dw[j] = dot_tn(left, right).astype(BF)
            for i in range(3):
                src = dw.at[j, :, pl.ds(i * width, width)]
                base = out_base + (i + 1) * tall
                dst = own_all.at[pl.ds(base, tall), place(0)]
                copy = net.to("shard", j, src, dst) if j else net.own(src, dst)
                arrivals[base].insert(len(arrivals[base]) if j == 0 else 0, copy)
            yield 0

        def weight_of(a):
            return [
                pltpu.make_async_copy(w.at[a], wbuf.at[a % 2, i], loads.at[1 + i, a % 2])
                for i, w in enumerate((wq, wk, wv))
            ]

        for copy in weight_of(0):
            copy.start()
        for a in range(group):
            if a + 1 < group:
                for copy in weight_of(a + 1):
                    copy.start()
            for copy in weight_of(a):
                copy.wait()
            left = g3[...].reshape(group * rows, 3 * width)
            res = dot_nt(left[:, :width], wbuf[a % 2, 0])
            res = res + dot_nt(left[:, width : 2 * width], wbuf[a % 2, 1])
            res = res + dot_nt(left[:, 2 * width :], wbuf[a % 2, 2])
            part[:, :, pl.ds(a * width, width)] = res.astype(BF).reshape(group, rows, width)
            yield 0
        red = Reduce(net, part, work[:2], masks)
        red.begin()
        net.settle(early)
        own = net.own(dpart, branch)
        yield 62
        own.wait()
        late = Reduce(net, branch, work[2:4], masks)
        late.begin()
        yield 66
        red.prepare()
        for s in range(red.steps - 1):
            yield 74 + 4 * s
            for n in range(2):
                red.advance(n, s)
        yield 79
        for n in range(2):
            red.advance(n, red.steps - 1)

            def first(at, start):
                g = red.total(at)
                w, inv = norm_rows(x_ref[at].astype(F32))
                gin[at] = (gmid[at] + norm_back(g, small[FG : FG + 1], w, inv)).astype(BF)
                sums[FG : FG + 1] += jnp.sum(g * w, axis=0, keepdims=True)
                sums[FS : FS + 1] += jnp.sum(g, axis=0, keepdims=True)

            by_rows(n, rows, first)
        tiny = [net.to("shard", j, sums.at[:, place(j)], land.at[me]) for j in range(1, group)]
        own = net.own(sums.at[:, place(0)], land.at[me])
        yield 81
        late.prepare()
        yield 83
        for copy in tiny:
            copy.wait_recv()
        own.wait()
        total = land[0]
        for j in range(1, group):
            total = total + land[j]
        both[0:8] = total
        tiny = [net.to("rep", h, both, zland.at[rep]) for h in range(1, reps)]
        own = net.own(both, zland.at[rep])
        for s in range(late.steps - 1):
            yield 89 + 4 * s
            for n in range(2):
                late.advance(n, s)
        yield 93
        for n in range(2):
            late.advance(n, late.steps - 1)

            def close(at, start):
                m = mid[at] + (late.total(at) + small[DB : DB + 1])
                out[at] = (m * live_rows(length, start, 16)).astype(BF)

            by_rows(n, rows, close)
        yield 96
        for copy in tiny:
            copy.wait_recv()
        own.wait()
        total = zland[0]
        for h in range(1, reps):
            total = total + zland[h]
        smalls[...] = total

    todo = tasks()
    resume = next(todo)
    for t in range(line.steps):
        base = t // line.each * tall
        if t < line.count and t % line.each == 0 and (base == up_base or base >= out_base):
            while base not in arrivals:
                resume = next(todo, None)
            for copy in arrivals.get(base, []):
                if copy is arrivals[base][-1]:
                    copy.wait()
                else:
                    copy.wait_recv()
        line.step(t)
        if resume is not None and t >= resume:
            resume = next(todo, None)
    for _ in todo:
        pass
    line.finish()
    net.finish()


def call(body, number, sizes, outs, scratch, copies, args, far=(), far_outs=()):
    return pl.pallas_call(
        functools.partial(body, *sizes),
        out_shape=[jax.ShapeDtypeStruct(s, d) for s, d in outs],
        in_specs=[ANY if i in far else VM for i in range(len(args))],
        out_specs=[ANY if i in far_outs else VM for i in range(len(outs))],
        scratch_shapes=list(scratch)
        + [pltpu.SemaphoreType.DMA((copies,)), pltpu.SemaphoreType.DMA((copies,))],
        compiler_params=pltpu.CompilerParams(
            collective_id=number, has_side_effects=True, vmem_limit_bytes=LIMIT
        ),
        name=body.__name__,
    )(*args)


def dot(a, b):
    return jnp.dot(a, b, preferred_element_type=F32)


def dot_nt(a, b):
    return jnp.einsum("tc,rc->tr", a, b, preferred_element_type=F32)


def dot_tn(a, b):
    return jnp.einsum("tr,tc->rc", a, b, preferred_element_type=F32)


def local(
    block_input,
    lengths,
    first_gain,
    first_shift,
    query_weight,
    query_bias,
    key_weight,
    value_weight,
    value_bias,
    out_weight,
    out_bias,
    second_gain,
    second_shift,
    up_weight,
    up_bias,
    down_weight,
    down_bias,
    cotangent,
):
    rows, width = block_input.shape[1], block_input.shape[2]
    hidden = up_weight.shape[1]
    group, reps = lax.axis_size("shard"), lax.axis_size("rep")
    sizes = (group, reps)
    g, f = width // group, hidden // group
    head = width // HEADS
    scale = 1.0 / math.sqrt(head)
    me = lax.axis_index("shard")
    small = jnp.stack(
        [
            first_gain.astype(F32),
            first_shift.astype(F32),
            out_bias.astype(F32),
            second_gain.astype(F32),
            second_shift.astype(F32),
            down_bias.astype(F32),
            jnp.full((g,), 1.0, F32) * lengths[0].astype(F32),
            jnp.zeros((g,), F32),
        ]
    )
    x, cot = block_input[0], cotangent[0]
    blocks = (group, rows, width)
    parts = reps if f // reps % 128 == 0 else 1
    nrm, small_all, wq, wk, wv, wu = call(
        gather_kernel,
        1,
        (sizes,),
        [
            (blocks, BF),
            ((8, width), F32),
            ((group, g, g), BF),
            ((group, g, g), BF),
            ((group, g, g), BF),
            ((group, g, f // parts), BF),
        ],
        [],
        200,
        (x, small, query_weight, key_weight, value_weight, up_weight),
    )
    flat = lambda a: a.reshape(-1, a.shape[-1])
    normed = flat(nrm)
    wq, wk, wv, wu = flat(wq), flat(wk), flat(wv), flat(wu)
    if parts > 1:
        wu = lax.all_gather(wu, "rep", axis=0).transpose(1, 0, 2).reshape(width, f)
    queries = (dot(normed, wq) + query_bias.astype(F32)).astype(BF)
    keys = dot(normed, wk).astype(BF)
    values = (dot(normed, wv) + value_bias.astype(F32)).astype(BF)
    shape = (group, rows, g // head, head)
    qh, kh, vh = (a.reshape(shape) for a in (queries, keys, values))
    lens = small_all[LN].reshape(group, g)[:, 0]
    order = jnp.bitwise_xor(jnp.arange(group, dtype=jnp.int32), me)
    lens = jnp.take(lens, order).astype(jnp.int32)
    pos = jnp.arange(rows, dtype=jnp.int32)
    valid = (pos[None, None, :] <= pos[None, :, None]) & (pos[None, None, :] < lens[:, None, None])
    scores = jnp.einsum("bqhd,bkhd->bhqk", qh, kh, preferred_element_type=F32) * scale
    scores = jnp.where(valid[:, None], scores, -1e30)
    top = jnp.max(scores, axis=-1, keepdims=True)
    expo = jnp.exp(scores - top)
    p = expo / jnp.sum(expo, axis=-1, keepdims=True)
    p_low = p.astype(BF)
    ctx = (
        jnp.einsum("bhqk,bkhd->bqhd", p_low, vh, preferred_element_type=F32)
        .astype(BF)
        .reshape(group * rows, g)
    )
    part = dot(ctx, out_weight).astype(BF).reshape(blocks)
    masks = shard_masks(group)
    work = reduce_shapes(group, rows, width, masks)
    mid, second, mix = call(
        middle_kernel,
        2,
        (sizes,),
        [((rows, width), F32), (blocks, BF), (blocks, BF)],
        work,
        160,
        (part, x, cot, small_all),
    )
    second = flat(second)
    mixed = flat(mix)
    upper = dot(second, wu) + up_bias.astype(F32)
    cdf = 0.5 * (1.0 + lax.erf(upper * (1.0 / math.sqrt(2.0))))
    pdf = jnp.exp(-0.5 * upper * upper) * (1.0 / math.sqrt(2.0 * math.pi))
    active = (upper * cdf).astype(BF)
    gup = (dot_nt(mixed, down_weight) * (cdf + upper * pdf)).astype(BF)
    gpart = dot_nt(gup, wu).astype(BF).reshape(blocks)
    dpart = dot(active, down_weight).astype(BF).reshape(blocks)
    down_grad = dot_tn(active, mixed).astype(BF)
    up_part = dot_tn(second, gup).astype(BF).reshape(group, g, f)
    cols = jnp.concatenate(
        [jnp.sum(gup.astype(F32), axis=0).reshape(4, g), jnp.zeros((2, g), F32)]
    )
    blocks_up = hidden // width
    tall_all = f + (4 + blocks_up) * g
    piece = 16
    count = tall_all // 2 // piece
    scratch = (
        work
        + work
        + [
            pltpu.VMEM((rows, width), F32),
            pltpu.VMEM((8, width), F32),
            pltpu.VMEM((group, 8, g), F32),
            pltpu.VMEM((16, g), F32),
            pltpu.VMEM((reps, 16, g), F32),
            pltpu.VMEM((tall_all, width), BF),
            pltpu.VMEM((2, count, piece, width), BF),
            pltpu.VMEM(blocks, BF),
            pltpu.VMEM(blocks, BF),
            pltpu.VMEM((group, rows, 3 * g), BF),
            pltpu.VMEM((group, g, 3 * g), BF),
            pltpu.VMEM((2, group, rows, g), BF),
            pltpu.VMEM((2, 3, g, g), BF),
            pltpu.SemaphoreType.DMA((4, 2)),
        ]
        + [pltpu.SemaphoreType.DMA((4 * count,))] * 2
        + [pltpu.SemaphoreType.DMA((2 * count,))]
    )
    out, gin, smalls, whole = call(
        final_kernel,
        3,
        (sizes, head),
        [
            ((rows, width), BF),
            ((rows, width), BF),
            ((16, g), F32),
            ((tall_all, width), BF),
        ],
        scratch,
        320,
        (
            gpart,
            dpart,
            up_part,
            down_grad,
            mid,
            cot,
            x,
            small_all,
            queries,
            keys,
            values,
            p,
            ctx,
            nrm,
            wq.reshape(group, g, g),
            wk.reshape(group, g, g),
            wv.reshape(group, g, g),
            out_weight,
            cols,
        ),
        (0, 1, 2, 3, 13, 14, 15, 16),
        (3,),
    )
    dd = whole[:f].astype(F32)
    du = whole[f : f + blocks_up * g].reshape(blocks_up, g, width).transpose(1, 0, 2)
    du = du.reshape(g, hidden).astype(F32)
    skip = f + blocks_up * g
    do, dq, dk, dv = (whole[skip + i * g : skip + (i + 1) * g].astype(F32) for i in range(4))
    return (
        out[None],
        gin[None],
        smalls[FG],
        smalls[FS],
        dq,
        smalls[8],
        dk,
        dv,
        smalls[9],
        do,
        smalls[OB],
        smalls[SG],
        smalls[SS],
        du,
        smalls[10:14].reshape(-1),
        dd,
        smalls[DB],
    )


def solution(mesh):
    tokens = P(("rep", "shard"), None, None)
    vec, mat = P("shard"), P("shard", None)
    return jax.shard_map(
        local,
        mesh=mesh,
        in_specs=(
            tokens,
            P(("rep", "shard")),
            vec,
            vec,
            mat,
            vec,
            mat,
            mat,
            vec,
            mat,
            vec,
            vec,
            vec,
            mat,
            vec,
            mat,
            vec,
            tokens,
        ),
        out_specs=(
            tokens,
            tokens,
            vec,
            vec,
            mat,
            vec,
            mat,
            mat,
            vec,
            mat,
            vec,
            vec,
            vec,
            mat,
            vec,
            mat,
            vec,
        ),
        check_vma=False,
    )
```

```python
import functools
import math

import jax
import jax.numpy as jnp
from jax import lax
from jax.experimental import pallas as pl
from jax.experimental.pallas import tpu as pltpu
from jax.sharding import PartitionSpec as P

HEADS = 16
MESH = pl.DeviceIdType.MESH
BF = jnp.bfloat16
F32 = jnp.float32
VM = pl.BlockSpec(memory_space=pltpu.VMEM)
SCALAR = pl.BlockSpec(memory_space=pltpu.SMEM)
ANY = pl.BlockSpec(memory_space=pl.ANY)
LIMIT = 63 * 2**20


def flip(index, mask):
    bit = 1
    while bit <= mask:
        if mask & bit:
            index = index + bit - 2 * bit * ((index // bit) % 2)
        bit *= 2
    return index


def span(masks):
    out = [0]
    for m in masks:
        out = out + [h ^ m for h in out]
    return out


def pair_masks(size):
    masks, bit = [], 1
    while bit < size:
        masks.append(bit + bit // 2 if len(masks) % 2 and size >= 2 * bit else bit)
        bit *= 2
    return masks


def shard_masks(size):
    masks, bit = [], 2
    while bit < size:
        masks.append(bit if len(masks) < 2 else bit + bit // 2)
        bit *= 2
    return masks


def orders(masks):
    return [list(masks), list(masks[1:]) + list(masks[:1])]


class Net:
    def __init__(self, send, recv):
        self.send, self.recv, self.used, self.open = send, recv, 0, []

    def to(self, axis, mask, src, dst):
        k = self.used
        self.used += 1
        copy = pltpu.make_async_remote_copy(
            src_ref=src,
            dst_ref=dst,
            send_sem=self.send.at[k],
            recv_sem=self.recv.at[k],
            device_id={axis: flip(lax.axis_index(axis), mask)},
            device_id_type=MESH,
        )
        copy.start()
        self.open.append(copy)
        return copy

    def own(self, src, dst):
        k = self.used
        self.used += 1
        copy = pltpu.make_async_copy(src, dst, self.send.at[k])
        copy.start()
        return copy

    def settle(self, count=None):
        for copy in self.open[:count]:
            copy.wait_send()
        self.open = self.open[len(self.open) if count is None else count :]

    finish = settle


def meet(shard_set, rep_set):
    barrier = pltpu.get_barrier_semaphore()
    for axis, masks in (("shard", shard_set), ("rep", rep_set)):
        for m in masks:
            pl.semaphore_signal(
                barrier,
                inc=1,
                device_id={axis: flip(lax.axis_index(axis), m)},
                device_id_type=MESH,
            )
    pl.semaphore_wait(barrier, len(shard_set) + len(rep_set))


class Gather:
    def __init__(self, net, buf, masks):
        self.net, self.buf = net, buf
        rows = buf.shape[1] // 2
        self.parts = [
            dict(rows=pl.ds(i * rows, rows), order=o, held=[0], new=[0], wait=[], step=0)
            for i, o in enumerate(orders(masks))
        ]
        self.cores = []
        self.steps = len(masks)

    def start(self, n):
        net, buf, part = self.net, self.buf, self.parts[n]
        fresh, rows = part["new"], part["rows"]
        if part["step"] < self.steps:
            m = part["order"][part["step"]]
            part["new"] = [h ^ m for h in part["held"]]
            part["wait"] = [
                net.to("shard", m, buf.at[h, rows], buf.at[h ^ m, rows]) for h in part["held"]
            ]
            part["held"] = part["held"] + part["new"]
        self.cores += [net.to("shard", 1, buf.at[h, rows], buf.at[h ^ 1, rows]) for h in fresh]
        part["step"] += 1

    def arrive(self, n):
        for copy in self.parts[n]["wait"]:
            copy.wait_recv()
        self.parts[n]["wait"] = []

    def both(self):
        for n in range(2):
            self.arrive(n)
            self.start(n)

    def end(self):
        for copy in self.cores:
            copy.wait_recv()

    def finish(self):
        for _ in range(self.steps):
            self.both()
        self.end()


def reduce_shapes(group, rows, width, masks):
    count = 2 ** len(masks) - 1
    return [
        pltpu.VMEM((group // 2, rows, width), BF),
        pltpu.VMEM((count, rows, width), BF),
    ]


class Reduce:
    def __init__(self, net, part, work, masks):
        self.net, self.part = net, part
        self.sums, self.land = work
        self.group, self.rows = part.shape[0], part.shape[1]
        self.cores = {}
        self.half = self.rows // 2
        self.steps = len(masks)
        self.orders = orders(masks)
        self.flight = [[], []]
        first = [o[0] for o in self.orders]
        self.sequence = sorted(
            span(masks), key=lambda h: -sum(self.sends(n, h) for n in range(2))
        )

    def sends(self, n, h):
        order = self.orders[n]
        return h not in span(order[1:])

    def begin_one(self, h):
        self.cores[h] = self.net.to("shard", 1, self.part.at[h ^ 1], self.sums.at[h // 2])

    def begin(self):
        for h in self.sequence:
            self.begin_one(h)

    def add(self, h, start, count, other):
        step = min(count, 32)

        @pl.loop(0, count // step)
        def _(i):
            at = pl.ds(pl.multiple_of(start + i * step, step), step)
            self.sums[h // 2, at] = (
                self.sums[h // 2, at].astype(F32) + other[at].astype(F32)
            ).astype(BF)

    def send(self, n, k, h):
        order = self.orders[n]
        rest = span(order[k + 1 :])
        base = sum(2 ** (self.steps - 1 - i) for i in range(k))
        to = h ^ order[k]
        rows = pl.ds(n * self.half, self.half)
        slot = base + rest.index(to)
        copy = self.net.to(
            "shard", order[k], self.sums.at[h // 2, rows], self.land.at[slot, rows]
        )
        self.flight[n].append((copy, to, slot))

    def prepare_one(self, h):
        self.cores[h].wait_recv()
        self.add(h, 0, self.rows, self.part.at[h])
        for n in range(2):
            if self.sends(n, h):
                self.send(n, 0, h)

    def prepare(self):
        for h in self.sequence:
            self.prepare_one(h)

    def advance(self, n, k):
        flight, self.flight[n] = self.flight[n], []
        rest = span(self.orders[n][k + 2 :])
        flight.sort(key=lambda f: f[1] in rest)
        for copy, h, slot in flight:
            copy.wait_recv()
            if k < self.steps - 1:
                self.add(h, n * self.half, self.half, self.land.at[slot])
                if h not in rest:
                    self.send(n, k + 1, h)
            else:
                self.last = slot

    def run(self):
        self.begin()
        self.prepare()
        for k in range(self.steps - 1):
            for n in range(2):
                self.advance(n, k)

    def total(self, at):
        return self.sums[0, at].astype(F32) + self.land[self.last, at].astype(F32)


def norm_rows(v):
    center = v - jnp.mean(v, axis=-1, keepdims=True)
    spread = jnp.mean(center * center, axis=-1, keepdims=True)
    inv = lax.rsqrt(spread + 1e-05)
    return center * inv, inv


def norm_back(grad, gain, n, inv):
    scaled = grad * gain
    return inv * (
        scaled
        - jnp.mean(scaled, axis=-1, keepdims=True)
        - n * jnp.mean(scaled * n, axis=-1, keepdims=True)
    )


FG, FS, OB, SG, SS, DB, LN = range(7)


def live_rows(length, start, rows):
    at = start + lax.broadcasted_iota(jnp.int32, (rows, 1), 0)
    return (at.astype(F32) < length).astype(F32)


def by_rows(n, count, body):
    step = 16

    @pl.loop(0, count // 2 // step)
    def _(i):
        start = pl.multiple_of(n * (count // 2) + i * step, step)
        body(pl.ds(start, step), start)


class Spread:
    def __init__(self, buf, columns, reps, sems):
        self.buf, self.columns, self.reps, self.sems = buf, columns, reps, sems
        self.rep = lax.axis_index("rep")

    def copy(self, hop, way, member):
        s, r = self.sems
        n = self.columns
        view = self.buf.at[:, :, pl.ds(pl.multiple_of(member * n, n), n)]
        at = 2 * (hop - 1) + way
        return pltpu.make_async_remote_copy(
            src_ref=view,
            dst_ref=view,
            send_sem=s.at[at],
            recv_sem=r.at[at],
            device_id={"rep": self.rep + (1 - 2 * way)},
            device_id_type=MESH,
        )

    def each(self, hop, sent, act):
        rep, last = self.rep, self.reps - 1
        for way in (0, 1):
            sign = 1 - 2 * way
            if sent:
                member = rep - sign * (hop - 1)
                to = rep + sign
                here = (to >= 0) & (to <= last)
            else:
                member = rep - sign * hop
                here = True

            @pl.when((member >= 0) & (member <= last) & here)
            def _():
                act(self.copy(hop, way, member))

    def start(self, hop):
        self.each(hop, True, lambda c: c.start())

    def arrive(self, hop):
        self.each(hop, False, lambda c: c.wait_recv())

    def finish(self):
        for hop in range(1, self.reps):
            self.each(hop, True, lambda c: c.wait_send())


def forward_kernel(sizes, head, *refs):
    group, reps = sizes
    length_ref, x_ref, cot_ref, vectors, q_ref, k_ref, v_ref, u_ref, wo = refs[:9]
    nrm, small_all, wq, wk, wv, wu, queries, keys, values, p_ref, ctx, mid, second, mix = refs[9:23]
    work = refs[23:]
    part, small_ref = work[2:4]
    spread_sems = work[4:6]
    me, rep = lax.axis_index("shard"), lax.axis_index("rep")
    net = Net(*work[-2:])
    masks = shard_masks(group)
    width, rows, model = vectors.shape[1], x_ref.shape[0], x_ref.shape[1]
    heads = width // head
    scale = 1.0 / math.sqrt(head)
    live = length_ref[0].astype(F32)
    small_ref[0:6] = vectors[0:6]
    small_ref[LN : LN + 1] = jnp.full((1, width), 1.0, F32) * live
    small_ref[LN + 1 :] = jnp.zeros((1, width), F32)
    meet(range(1, group), range(1, reps))
    mine = pl.ds(pl.multiple_of(me * width, width), width)
    small = [
        net.to("shard", j, small_ref, small_all.at[:, mine]) for j in range(1, group)
    ]
    own_small = net.own(small_ref, small_all.at[:, mine])

    def scatter(src, dst, first, n):
        share = src.shape[1] // group

        def columns(j):
            return pl.ds(pl.multiple_of(flip(me, j) * share + first, n), n)

        return [net.to("shard", j, src.at[:, columns(j)], dst) for j in range(1, group)] + [
            net.own(src.at[:, columns(0)], dst)
        ]

    def arrive(copies):
        for copy in copies[:-1]:
            copy.wait_recv()
        copies[-1].wait()

    whole = wu.shape[2]
    share = whole // reps if whole // reps % 128 == 0 else whole
    first = rep * share if share < whole else 0
    lanes = pl.ds(pl.multiple_of(first, share), share)
    ups = scatter(u_ref, wu.at[me, :, lanes], first, share)
    spread = Spread(wu, share, reps if share < whole else 1, spread_sems)
    moved = [scatter(s, d.at[me], 0, width) for s, d in ((q_ref, wq), (k_ref, wk), (v_ref, wv))]
    arrive(small + [own_small])
    gather = Gather(net, nrm, masks)
    for n in range(2):

        def one(at, start):
            v, _ = norm_rows(x_ref[at].astype(F32))
            nrm[0, at] = (v * small_all[FG : FG + 1] + small_all[FS : FS + 1]).astype(BF)
            mix[0, at] = (cot_ref[at].astype(F32) * live_rows(live, start, 16)).astype(BF)

        by_rows(n, rows, one)
        gather.start(n)
    arrive(ups)
    if spread.reps > 1:
        spread.start(1)
    for _ in range(gather.steps - 1):
        gather.both()
    gather.both()
    gather.end()
    for copies, weight, low, row in zip(
        moved, (wq, wk, wv), (queries, keys, values), (6, None, 7)
    ):
        arrive(copies)
        for b in range(0, group, 2):
            left = nrm[b : b + 2].reshape(2 * rows, model)
            res = dot(left, weight[...].reshape(model, width))
            if row is not None:
                res = res + vectors[row : row + 1]
            low[pl.ds(b * rows, 2 * rows)] = res.astype(BF)
    gmix = Gather(net, mix, masks)
    red = Reduce(net, part, work[:2], masks)
    order = [h ^ 1 for h in red.sequence] + red.sequence
    row_at = lax.broadcasted_iota(jnp.int32, (rows, rows), 0)
    col_at = lax.broadcasted_iota(jnp.int32, (rows, rows), 1)

    def side(n):
        if n == 0:
            for i in range(2):
                gmix.start(i)
        if n == 0 and spread.reps > 1:
            spread.arrive(1)
            if spread.reps > 2:
                spread.start(2)
        if n in (3, 6) and gmix.parts[0]["step"] <= gmix.steps:
            gmix.both()

    for n, b in enumerate(order):
        side(n)
        at = pl.ds(b * rows, rows)
        count = small_all[LN : LN + 1, pl.ds(pl.multiple_of(flip(me, b) * width, width), 128)]
        valid = (col_at <= row_at) & (col_at.astype(F32) < count[:, :1])
        for h in range(heads):
            lane = pl.ds(h * head, head)
            scores = dot_nt(queries[at, lane], keys[at, lane]) * scale
            scores = jnp.where(valid, scores, -1e30)
            expo = jnp.exp(scores - jnp.max(scores, axis=-1, keepdims=True))
            p = expo / jnp.sum(expo, axis=-1, keepdims=True)
            p_ref[b, h] = p
            ctx[at, lane] = dot(p.astype(BF), values[at, lane]).astype(BF)
        for c in range(0, model, 1024):
            lane = pl.ds(c, 1024)
            part[b, :, lane] = dot(ctx[at], wo[:, lane]).astype(BF)
        if b % 2:
            red.begin_one(b ^ 1)
        else:
            red.prepare_one(b)
    for k in range(red.steps - 1):
        for n in range(2):
            red.advance(n, k)
    gather = Gather(net, second, masks)
    for n in range(2):
        red.advance(n, red.steps - 1)

        def norm(at, start):
            m = x_ref[at].astype(F32) + (red.total(at) + small_all[OB : OB + 1])
            mid[at] = m
            v, _ = norm_rows(m)
            second[0, at] = (v * small_all[SG : SG + 1] + small_all[SS : SS + 1]).astype(BF)

        by_rows(n, rows, norm)
        gather.start(n)
    hop = 2
    while gmix.parts[0]["step"] <= gmix.steps:
        gmix.both()
    for _ in range(gather.steps):
        if hop < spread.reps:
            spread.arrive(hop)
            hop += 1
            if hop < spread.reps:
                spread.start(hop)
        gather.both()
    while hop < spread.reps:
        spread.arrive(hop)
        hop += 1
        if hop < spread.reps:
            spread.start(hop)
    gmix.end()
    gather.end()
    if spread.reps > 1:
        spread.finish()
    net.finish()


class Line:
    def __init__(self, own, land, out, tall, reps, sems, kept):
        self.kept = kept
        self.own, self.land, self.out = own, land, out
        self.rep, self.reps, self.sems = lax.axis_index("rep"), reps, sems
        self.count, self.size = land.shape[1], land.shape[2]
        self.tall, self.each = tall, tall // 2 // self.size
        self.skew = 2
        self.steps = self.count + 2 * self.skew * (reps - 1)

    def rows(self, way, i):
        row = (i // self.each) * self.tall + way * (self.tall // 2) + (i % self.each) * self.size
        return pl.ds(pl.multiple_of(row, self.size), self.size)

    def copy(self, src, dst, way, back, i, up):
        s, r = self.sems
        at = (2 * way + back) * self.count + i
        return pltpu.make_async_remote_copy(
            src_ref=src,
            dst_ref=dst,
            send_sem=s.at[at],
            recv_sem=r.at[at],
            device_id={"rep": self.rep + (1 if up else -1)},
            device_id_type=MESH,
        )

    def place(self, way):
        return self.rep if way == 0 else self.reps - 1 - self.rep

    def forth(self, way, t):
        at = self.place(way)
        i, last = t - self.skew * at, self.reps - 1

        @pl.when((i >= 0) & (i < self.count))
        def _():
            rows, land = self.rows(way, i), self.land.at[way, i]

            @pl.when(at == 0)
            def _():
                self.copy(self.own.at[rows], land, way, 0, i, way == 0).start()

            @pl.when(at != 0)
            def _():
                self.copy(self.own.at[rows], land, way, 0, i, way == 0).wait_recv()

            @pl.when((at != 0) & (at != last))
            def _():
                self.add(land, rows, land)
                self.copy(land, land, way, 0, i, way == 0).start()

            @pl.when(at == last)
            def _():
                self.add(land, rows, land)
                self.copy(land, self.out.at[rows], way, 1, i, way != 0).start()
                self.keep(way, i).start()

    def add(self, land, rows, to):
        own, step = self.own.at[rows], 16

        @pl.loop(0, self.size // step)
        def _(n):
            at = pl.ds(pl.multiple_of(n * step, step), step)
            to[at] = (land[at].astype(F32) + own[at].astype(F32)).astype(BF)

    def keep(self, way, i):
        return pltpu.make_async_copy(
            self.land.at[way, i],
            self.out.at[self.rows(way, i)],
            self.kept.at[way * self.count + i],
        )

    def back(self, way, t):
        at, last = self.place(way), self.reps - 1
        i = t - self.skew * (last + last - at)

        @pl.when((at != last) & (i >= 0) & (i < self.count))
        def _():
            out = self.out.at[self.rows(way, i)]
            self.copy(out, out, way, 1, i, way != 0).wait_recv()

            @pl.when(at != 0)
            def _():
                self.copy(out, out, way, 1, i, way != 0).start()

    def step(self, t):
        for way in (0, 1):
            self.forth(way, t)
        for way in (0, 1):
            self.back(way, t)

    def finish(self):
        last = self.reps - 1
        for way in (0, 1):
            at = self.place(way)

            @pl.loop(0, self.count)
            def _(i):
                out = self.out.at[self.rows(way, i)]

                @pl.when(at != last)
                def _():
                    self.copy(out, out, way, 0, i, way == 0).wait_send()

                @pl.when(at != 0)
                def _():
                    self.copy(out, out, way, 1, i, way != 0).wait_send()

                @pl.when(at == last)
                def _():
                    self.keep(way, i).wait()


def final_kernel(sizes, head, *refs):
    group, reps = sizes
    (
        gpart,
        dpart,
        up_part,
        down_grad,
        mid,
        cot,
        x_ref,
        small,
        q,
        k,
        v,
        p_ref,
        ctx,
        nrm,
        wq,
        wk,
        wv,
        wo,
        cols,
    ) = refs[:19]
    out, gin, smalls, whole = refs[19:23]
    work = refs[23:]
    gmid, sums, land, both, zland, own_all, line_land = work[4:11]
    part, branch, g3, dw, nbuf, wbuf, loads = work[11:18]
    line_sems, kept = work[18:20], work[20]
    net = Net(*work[-2:])
    masks = shard_masks(group)
    me, rep = lax.axis_index("shard"), lax.axis_index("rep")
    width, rows, model = smalls.shape[1], x_ref.shape[0], x_ref.shape[1]
    heads = width // head
    scale = 1.0 / math.sqrt(head)
    tall = width
    down_rows, wide = down_grad.shape[0], up_part.shape[2]
    up_base = down_rows
    out_base = up_base + tall * (wide * group // model)
    loaded = [
        net.own(gpart, part),
        net.own(down_grad, own_all.at[pl.ds(0, down_rows)]),
    ]
    meet(range(1, group), range(1, reps))
    length = small[LN : LN + 1, pl.ds(pl.multiple_of(me * width, width), 128)][:, :1]
    line = Line(own_all, line_land, whole, tall, reps, line_sems, kept)
    for copy in loaded:
        copy.wait()
    arrivals = {}

    def place(j):
        return pl.ds(pl.multiple_of(flip(me, j) * width, width), width)

    def tasks():
        red = Reduce(net, part, work[:2], masks)
        red.begin()
        yield 3
        red.prepare()
        each = model // wide
        target = own_all.at[
            pl.ds(pl.multiple_of(up_base + (me // each) * tall, tall), tall),
            pl.ds(pl.multiple_of((me % each) * wide, wide), wide),
        ]
        arrivals[up_base] = [
            net.to("shard", j, up_part.at[flip(me, j)], target) for j in range(1, group)
        ] + [net.own(up_part.at[me], target)]
        yield 22
        for s in range(red.steps - 1):
            for n in range(2):
                red.advance(n, s)
        yield 28
        for n in range(2):
            red.advance(n, red.steps - 1)
        net.settle()
        sums[...] = jnp.zeros_like(sums)
        gather = Gather(net, branch, masks)
        for n in range(2):

            def back(at, start):
                g = red.total(at)
                w, inv = norm_rows(mid[at])
                gout = cot[at].astype(F32) * live_rows(length, start, 16)
                res = gout + norm_back(g, small[SG : SG + 1], w, inv)
                gmid[at] = res
                low = res.astype(BF)
                branch[0, at] = low
                sums[SG : SG + 1] += jnp.sum(g * w, axis=0, keepdims=True)
                sums[SS : SS + 1] += jnp.sum(g, axis=0, keepdims=True)
                sums[OB : OB + 1] += jnp.sum(low.astype(F32), axis=0, keepdims=True)
                sums[DB : DB + 1] += jnp.sum(gout, axis=0, keepdims=True)

            by_rows(n, rows, back)
            gather.start(n)
        for s in range(gather.steps):
            yield 33 + 5 * s
            gather.both()
        yield 33 + 5 * gather.steps
        gather.end()
        early = len(net.open)
        for b in range(group):
            at = pl.ds(b * rows, rows)
            gc = dot_nt(branch[b], wo[...]).astype(BF)
            for h in range(heads):
                lane = pl.ds(h * head, head)
                qh, kh, vh = q[at, lane], k[at, lane], v[at, lane]
                gch = gc[:, h * head : (h + 1) * head]
                p = p_ref[b, h]
                gw = dot_nt(gch, vh)
                inner = jnp.sum(p * gw, axis=-1, keepdims=True)
                gs = (p * (gw - inner)).astype(BF)
                g3[b, :, pl.ds(h * head, head)] = (dot(gs, kh) * scale).astype(BF)
                g3[b, :, pl.ds(width + h * head, head)] = (dot_tn(gs, qh) * scale).astype(BF)
                g3[b, :, pl.ds(2 * width + h * head, head)] = dot_tn(p.astype(BF), gch).astype(BF)
            yield 0
        n_col = 512
        for c in range(0, model, n_col):
            lane = pl.ds(c, n_col)
            full = branch[:, :, lane].reshape(group * rows, n_col)
            own_all[pl.ds(out_base, tall), lane] = dot_tn(ctx[...], full).astype(BF)
            yield 0
        arrivals[out_base] = []
        grads = g3[...].reshape(group * rows, 3 * width)
        total = jnp.sum(grads.astype(F32), axis=0, keepdims=True)
        both[8:9] = total[:, :width]
        both[9:10] = total[:, 2 * width :]
        both[10:16] = cols[...]

        def normed_of(j):
            return pltpu.make_async_copy(nrm.at[:, :, place(j)], nbuf.at[j % 2], loads.at[0, j % 2])

        normed_of(0).start()
        for i in range(3):
            arrivals[out_base + (i + 1) * tall] = []
        for j in range(group):
            if j + 1 < group:
                normed_of(j + 1).start()
            normed_of(j).wait()
            left = nbuf[j % 2].reshape(group * rows, width)
            right = g3[...].reshape(group * rows, 3 * width)
            dw[j] = dot_tn(left, right).astype(BF)
            for i in range(3):
                src = dw.at[j, :, pl.ds(i * width, width)]
                base = out_base + (i + 1) * tall
                dst = own_all.at[pl.ds(base, tall), place(0)]
                copy = net.to("shard", j, src, dst) if j else net.own(src, dst)
                arrivals[base].insert(len(arrivals[base]) if j == 0 else 0, copy)
            yield 0

        def weight_of(a):
            return [
                pltpu.make_async_copy(w.at[a], wbuf.at[a % 2, i], loads.at[1 + i, a % 2])
                for i, w in enumerate((wq, wk, wv))
            ]

        for copy in weight_of(0):
            copy.start()
        for a in range(group):
            if a + 1 < group:
                for copy in weight_of(a + 1):
                    copy.start()
            for copy in weight_of(a):
                copy.wait()
            left = g3[...].reshape(group * rows, 3 * width)
            res = dot_nt(left[:, :width], wbuf[a % 2, 0])
            res = res + dot_nt(left[:, width : 2 * width], wbuf[a % 2, 1])
            res = res + dot_nt(left[:, 2 * width :], wbuf[a % 2, 2])
            part[:, :, pl.ds(a * width, width)] = res.astype(BF).reshape(group, rows, width)
            yield 0
        red = Reduce(net, part, work[:2], masks)
        red.begin()
        net.settle(early)
        own = net.own(dpart, branch)
        yield 62
        own.wait()
        late = Reduce(net, branch, work[2:4], masks)
        late.begin()
        yield 66
        red.prepare()
        for s in range(red.steps - 1):
            yield 74 + 4 * s
            for n in range(2):
                red.advance(n, s)
        yield 79
        for n in range(2):
            red.advance(n, red.steps - 1)

            def first(at, start):
                g = red.total(at)
                w, inv = norm_rows(x_ref[at].astype(F32))
                gin[at] = (gmid[at] + norm_back(g, small[FG : FG + 1], w, inv)).astype(BF)
                sums[FG : FG + 1] += jnp.sum(g * w, axis=0, keepdims=True)
                sums[FS : FS + 1] += jnp.sum(g, axis=0, keepdims=True)

            by_rows(n, rows, first)
        tiny = [net.to("shard", j, sums.at[:, place(j)], land.at[me]) for j in range(1, group)]
        own = net.own(sums.at[:, place(0)], land.at[me])
        yield 81
        late.prepare()
        yield 83
        for copy in tiny:
            copy.wait_recv()
        own.wait()
        total = land[0]
        for j in range(1, group):
            total = total + land[j]
        both[0:8] = total
        tiny = [net.to("rep", h, both, zland.at[rep]) for h in range(1, reps)]
        own = net.own(both, zland.at[rep])
        for s in range(late.steps - 1):
            yield 89 + 4 * s
            for n in range(2):
                late.advance(n, s)
        yield 93
        for n in range(2):
            late.advance(n, late.steps - 1)

            def close(at, start):
                m = mid[at] + (late.total(at) + small[DB : DB + 1])
                out[at] = (m * live_rows(length, start, 16)).astype(BF)

            by_rows(n, rows, close)
        yield 96
        for copy in tiny:
            copy.wait_recv()
        own.wait()
        total = zland[0]
        for h in range(1, reps):
            total = total + zland[h]
        smalls[...] = total

    todo = tasks()
    resume = next(todo)
    for t in range(line.steps):
        base = t // line.each * tall
        if t < line.count and t % line.each == 0 and (base == up_base or base >= out_base):
            while base not in arrivals:
                resume = next(todo, None)
            for copy in arrivals.get(base, []):
                if copy is arrivals[base][-1]:
                    copy.wait()
                else:
                    copy.wait_recv()
        line.step(t)
        if resume is not None and t >= resume:
            resume = next(todo, None)
    for _ in todo:
        pass
    line.finish()
    net.finish()


def call(body, number, sizes, outs, scratch, copies, args, far=(), far_outs=(), scalars=()):
    return pl.pallas_call(
        functools.partial(body, *sizes),
        out_shape=[jax.ShapeDtypeStruct(s, d) for s, d in outs],
        in_specs=[
            ANY if i in far else SCALAR if i in scalars else VM for i in range(len(args))
        ],
        out_specs=[ANY if i in far_outs else VM for i in range(len(outs))],
        scratch_shapes=list(scratch)
        + [pltpu.SemaphoreType.DMA((copies,)), pltpu.SemaphoreType.DMA((copies,))],
        compiler_params=pltpu.CompilerParams(
            collective_id=number, has_side_effects=True, vmem_limit_bytes=LIMIT
        ),
        name=body.__name__,
    )(*args)


def dot(a, b):
    return jnp.dot(a, b, preferred_element_type=F32)


def dot_nt(a, b):
    return jnp.einsum("tc,rc->tr", a, b, preferred_element_type=F32)


def dot_tn(a, b):
    return jnp.einsum("tr,tc->rc", a, b, preferred_element_type=F32)


def local(
    block_input,
    lengths,
    first_gain,
    first_shift,
    query_weight,
    query_bias,
    key_weight,
    value_weight,
    value_bias,
    out_weight,
    out_bias,
    second_gain,
    second_shift,
    up_weight,
    up_bias,
    down_weight,
    down_bias,
    cotangent,
):
    rows, width = block_input.shape[1], block_input.shape[2]
    hidden = up_weight.shape[1]
    group, reps = lax.axis_size("shard"), lax.axis_size("rep")
    sizes = (group, reps)
    g, f = width // group, hidden // group
    head = width // HEADS
    scale = 1.0 / math.sqrt(head)
    me = lax.axis_index("shard")
    vectors = jnp.concatenate(
        [
            first_gain,
            first_shift,
            out_bias,
            second_gain,
            second_shift,
            down_bias,
            query_bias,
            value_bias,
        ]
    )
    vectors = vectors.reshape(8, g).astype(F32)
    x, cot = block_input[0], cotangent[0]
    blocks = (group, rows, width)
    masks = shard_masks(group)
    work = reduce_shapes(group, rows, width, masks)
    tokens, column = group * rows, ((group, g, g), BF)
    nrm, small_all, wq, wk, wv, wu, queries, keys, values, p, ctx, mid, second, mix = call(
        forward_kernel,
        1,
        (sizes, head),
        [
            (blocks, BF),
            ((8, width), F32),
            column,
            column,
            column,
            ((group, g, f), BF),
            ((tokens, g), BF),
            ((tokens, g), BF),
            ((tokens, g), BF),
            ((group, g // head, rows, rows), F32),
            ((tokens, g), BF),
            ((rows, width), F32),
            (blocks, BF),
            (blocks, BF),
        ],
        work
        + [pltpu.VMEM(blocks, BF), pltpu.VMEM((8, g), F32)]
        + [pltpu.SemaphoreType.DMA((2 * reps,))] * 2,
        320,
        (
            lengths,
            x,
            cot,
            vectors,
            query_weight,
            key_weight,
            value_weight,
            up_weight,
            out_weight,
        ),
        (4, 5, 6, 7),
        (),
        (0,),
    )
    flat = lambda a: a.reshape(-1, a.shape[-1])
    wu = flat(wu)
    second = flat(second)
    mixed = flat(mix)
    upper = dot(second, wu) + up_bias.astype(F32)
    cdf = 0.5 * (1.0 + lax.erf(upper * (1.0 / math.sqrt(2.0))))
    pdf = jnp.exp(-0.5 * upper * upper) * (1.0 / math.sqrt(2.0 * math.pi))
    active = (upper * cdf).astype(BF)
    gup = (dot_nt(mixed, down_weight) * (cdf + upper * pdf)).astype(BF)
    gpart = dot_nt(gup, wu).astype(BF).reshape(blocks)
    dpart = dot(active, down_weight).astype(BF).reshape(blocks)
    down_grad = dot_tn(active, mixed).astype(BF)
    up_part = dot_tn(second, gup).astype(BF).reshape(group, g, f)
    cols = jnp.concatenate(
        [jnp.sum(gup.astype(F32), axis=0).reshape(4, g), jnp.zeros((2, g), F32)]
    )
    blocks_up = hidden // width
    tall_all = f + (4 + blocks_up) * g
    piece = 16
    count = tall_all // 2 // piece
    scratch = (
        work
        + work
        + [
            pltpu.VMEM((rows, width), F32),
            pltpu.VMEM((8, width), F32),
            pltpu.VMEM((group, 8, g), F32),
            pltpu.VMEM((16, g), F32),
            pltpu.VMEM((reps, 16, g), F32),
            pltpu.VMEM((tall_all, width), BF),
            pltpu.VMEM((2, count, piece, width), BF),
            pltpu.VMEM(blocks, BF),
            pltpu.VMEM(blocks, BF),
            pltpu.VMEM((group, rows, 3 * g), BF),
            pltpu.VMEM((group, g, 3 * g), BF),
            pltpu.VMEM((2, group, rows, g), BF),
            pltpu.VMEM((2, 3, g, g), BF),
            pltpu.SemaphoreType.DMA((4, 2)),
        ]
        + [pltpu.SemaphoreType.DMA((4 * count,))] * 2
        + [pltpu.SemaphoreType.DMA((2 * count,))]
    )
    out, gin, smalls, whole = call(
        final_kernel,
        2,
        (sizes, head),
        [
            ((rows, width), BF),
            ((rows, width), BF),
            ((16, g), F32),
            ((tall_all, width), BF),
        ],
        scratch,
        320,
        (
            gpart,
            dpart,
            up_part,
            down_grad,
            mid,
            cot,
            x,
            small_all,
            queries,
            keys,
            values,
            p,
            ctx,
            nrm,
            wq,
            wk,
            wv,
            out_weight,
            cols,
        ),
        (0, 1, 2, 3, 13, 14, 15, 16),
        (3,),
    )
    dd = whole[:f].astype(F32)
    du = whole[f : f + blocks_up * g].reshape(blocks_up, g, width).transpose(1, 0, 2)
    du = du.reshape(g, hidden).astype(F32)
    skip = f + blocks_up * g
    do, dq, dk, dv = (whole[skip + i * g : skip + (i + 1) * g].astype(F32) for i in range(4))
    return (
        out[None],
        gin[None],
        smalls[FG],
        smalls[FS],
        dq,
        smalls[8],
        dk,
        dv,
        smalls[9],
        do,
        smalls[OB],
        smalls[SG],
        smalls[SS],
        du,
        smalls[10:14].reshape(-1),
        dd,
        smalls[DB],
    )


def solution(mesh):
    tokens = P(("rep", "shard"), None, None)
    vec, mat = P("shard"), P("shard", None)
    return jax.shard_map(
        local,
        mesh=mesh,
        in_specs=(
            tokens,
            P(("rep", "shard")),
            vec,
            vec,
            mat,
            vec,
            mat,
            mat,
            vec,
            mat,
            vec,
            vec,
            vec,
            mat,
            vec,
            mat,
            vec,
            tokens,
        ),
        out_specs=(
            tokens,
            tokens,
            vec,
            vec,
            mat,
            vec,
            mat,
            mat,
            vec,
            mat,
            vec,
            vec,
            vec,
            mat,
            vec,
            mat,
            vec,
        ),
        check_vma=False,
    )
```

```python
import functools
import math

import jax
import jax.numpy as jnp
from jax import lax
from jax.experimental import pallas as pl
from jax.experimental.pallas import tpu as pltpu
from jax.sharding import PartitionSpec as P

HEADS = 16
MESH = pl.DeviceIdType.MESH
BF = jnp.bfloat16
F32 = jnp.float32
VM = pl.BlockSpec(memory_space=pltpu.VMEM)
SCALAR = pl.BlockSpec(memory_space=pltpu.SMEM)
ANY = pl.BlockSpec(memory_space=pl.ANY)
LIMIT = 63 * 2**20


def flip(index, mask):
    bit = 1
    while bit <= mask:
        if mask & bit:
            index = index + bit - 2 * bit * ((index // bit) % 2)
        bit *= 2
    return index


def span(masks):
    out = [0]
    for m in masks:
        out = out + [h ^ m for h in out]
    return out


def pair_masks(size):
    masks, bit = [], 1
    while bit < size:
        masks.append(bit + bit // 2 if len(masks) % 2 and size >= 2 * bit else bit)
        bit *= 2
    return masks


def shard_masks(size):
    masks, bit = [], 2
    while bit < size:
        masks.append(bit if len(masks) < 2 else bit + bit // 2)
        bit *= 2
    return masks


def orders(masks):
    return [list(masks), list(masks[1:]) + list(masks[:1])]


class Net:
    def __init__(self, send, recv):
        self.send, self.recv, self.used, self.open = send, recv, 0, []

    def to(self, axis, mask, src, dst):
        k = self.used
        self.used += 1
        copy = pltpu.make_async_remote_copy(
            src_ref=src,
            dst_ref=dst,
            send_sem=self.send.at[k],
            recv_sem=self.recv.at[k],
            device_id={axis: flip(lax.axis_index(axis), mask)},
            device_id_type=MESH,
        )
        copy.start()
        self.open.append(copy)
        return copy

    def own(self, src, dst):
        k = self.used
        self.used += 1
        copy = pltpu.make_async_copy(src, dst, self.send.at[k])
        copy.start()
        return copy

    def settle(self, count=None):
        for copy in self.open[:count]:
            copy.wait_send()
        self.open = self.open[len(self.open) if count is None else count :]

    finish = settle


def meet(shard_set, rep_set):
    barrier = pltpu.get_barrier_semaphore()
    for axis, masks in (("shard", shard_set), ("rep", rep_set)):
        for m in masks:
            pl.semaphore_signal(
                barrier,
                inc=1,
                device_id={axis: flip(lax.axis_index(axis), m)},
                device_id_type=MESH,
            )
    pl.semaphore_wait(barrier, len(shard_set) + len(rep_set))


class Gather:
    def __init__(self, net, buf, masks):
        self.net, self.buf = net, buf
        rows = buf.shape[1] // 2
        self.parts = [
            dict(rows=pl.ds(i * rows, rows), order=o, held=[0], new=[0], wait=[], step=0)
            for i, o in enumerate(orders(masks))
        ]
        self.cores = []
        self.steps = len(masks)

    def start(self, n):
        net, buf, part = self.net, self.buf, self.parts[n]
        fresh, rows = part["new"], part["rows"]
        if part["step"] < self.steps:
            m = part["order"][part["step"]]
            part["new"] = [h ^ m for h in part["held"]]
            part["wait"] = [
                net.to("shard", m, buf.at[h, rows], buf.at[h ^ m, rows]) for h in part["held"]
            ]
            part["held"] = part["held"] + part["new"]
        self.cores += [net.to("shard", 1, buf.at[h, rows], buf.at[h ^ 1, rows]) for h in fresh]
        part["step"] += 1

    def arrive(self, n):
        for copy in self.parts[n]["wait"]:
            copy.wait_recv()
        self.parts[n]["wait"] = []

    def both(self):
        for n in range(2):
            self.arrive(n)
            self.start(n)

    def end(self):
        for copy in self.cores:
            copy.wait_recv()

    def finish(self):
        for _ in range(self.steps):
            self.both()
        self.end()


def reduce_shapes(group, rows, width, masks):
    count = 2 ** len(masks) - 1
    return [
        pltpu.VMEM((group // 2, rows, width), BF),
        pltpu.VMEM((count, rows, width), BF),
    ]


class Reduce:
    def __init__(self, net, part, work, masks):
        self.net, self.part = net, part
        self.sums, self.land = work
        self.group, self.rows = part.shape[0], part.shape[1]
        self.cores = {}
        self.half = self.rows // 2
        self.steps = len(masks)
        self.orders = orders(masks)
        self.flight = [[], []]
        self.sequence = sorted(
            span(masks), key=lambda h: -sum(self.sends(n, h) for n in range(2))
        )

    def sends(self, n, h):
        order = self.orders[n]
        return h not in span(order[1:])

    def begin_one(self, h):
        self.cores[h] = self.net.to("shard", 1, self.part.at[h ^ 1], self.sums.at[h // 2])

    def begin(self):
        for h in self.sequence:
            self.begin_one(h)

    def add(self, h, start, count, other):
        step = min(count, 32)

        @pl.loop(0, count // step)
        def _(i):
            at = pl.ds(pl.multiple_of(start + i * step, step), step)
            self.sums[h // 2, at] = (
                self.sums[h // 2, at].astype(F32) + other[at].astype(F32)
            ).astype(BF)

    def send(self, n, k, h):
        order = self.orders[n]
        rest = span(order[k + 1 :])
        base = sum(2 ** (self.steps - 1 - i) for i in range(k))
        to = h ^ order[k]
        rows = pl.ds(n * self.half, self.half)
        slot = base + rest.index(to)
        copy = self.net.to(
            "shard", order[k], self.sums.at[h // 2, rows], self.land.at[slot, rows]
        )
        self.flight[n].append((copy, to, slot))

    def prepare_one(self, h):
        self.cores[h].wait_recv()
        self.add(h, 0, self.rows, self.part.at[h])
        for n in range(2):
            if self.sends(n, h):
                self.send(n, 0, h)

    def prepare(self):
        for h in self.sequence:
            self.prepare_one(h)

    def advance(self, n, k):
        flight, self.flight[n] = self.flight[n], []
        rest = span(self.orders[n][k + 2 :])
        flight.sort(key=lambda f: f[1] in rest)
        for copy, h, slot in flight:
            copy.wait_recv()
            if k < self.steps - 1:
                self.add(h, n * self.half, self.half, self.land.at[slot])
                if h not in rest:
                    self.send(n, k + 1, h)
            else:
                self.last = slot

    def run(self):
        self.begin()
        self.prepare()
        for k in range(self.steps - 1):
            for n in range(2):
                self.advance(n, k)

    def total(self, at):
        return self.sums[0, at].astype(F32) + self.land[self.last, at].astype(F32)


def norm_rows(v):
    center = v - jnp.mean(v, axis=-1, keepdims=True)
    spread = jnp.mean(center * center, axis=-1, keepdims=True)
    inv = lax.rsqrt(spread + 1e-05)
    return center * inv, inv


def norm_back(grad, gain, n, inv):
    scaled = grad * gain
    return inv * (
        scaled
        - jnp.mean(scaled, axis=-1, keepdims=True)
        - n * jnp.mean(scaled * n, axis=-1, keepdims=True)
    )


FG, FS, OB, SG, SS, DB, LN = range(7)


def live_rows(length, start, rows):
    at = start + lax.broadcasted_iota(jnp.int32, (rows, 1), 0)
    return (at.astype(F32) < length).astype(F32)


def by_rows(n, count, body):
    step = 16

    @pl.loop(0, count // 2 // step)
    def _(i):
        start = pl.multiple_of(n * (count // 2) + i * step, step)
        body(pl.ds(start, step), start)


class Spread:
    def __init__(self, buf, columns, reps, sems):
        self.buf, self.columns, self.reps, self.sems = buf, columns, reps, sems
        self.rep = lax.axis_index("rep")

    def copy(self, hop, way, member):
        s, r = self.sems
        n = self.columns
        view = self.buf.at[:, :, pl.ds(pl.multiple_of(member * n, n), n)]
        at = 2 * (hop - 1) + way
        return pltpu.make_async_remote_copy(
            src_ref=view,
            dst_ref=view,
            send_sem=s.at[at],
            recv_sem=r.at[at],
            device_id={"rep": self.rep + (1 - 2 * way)},
            device_id_type=MESH,
        )

    def each(self, hop, sent, act):
        rep, last = self.rep, self.reps - 1
        for way in (0, 1):
            sign = 1 - 2 * way
            if sent:
                member = rep - sign * (hop - 1)
                to = rep + sign
                here = (to >= 0) & (to <= last)
            else:
                member = rep - sign * hop
                here = True

            @pl.when((member >= 0) & (member <= last) & here)
            def _():
                act(self.copy(hop, way, member))

    def start(self, hop):
        self.each(hop, True, lambda c: c.start())

    def arrive(self, hop):
        self.each(hop, False, lambda c: c.wait_recv())

    def finish(self):
        for hop in range(1, self.reps):
            self.each(hop, True, lambda c: c.wait_send())


def forward_kernel(sizes, head, *refs):
    group, reps = sizes
    length_ref, x_ref, cot_ref, vectors, q_ref, k_ref, v_ref, u_ref, wo = refs[:9]
    nrm, small_all, wq, wk, wv, wu, queries, keys, values, p_ref, ctx, mid, second, mix = refs[9:23]
    work = refs[23:]
    part, small_ref = work[2:4]
    spread_sems = work[4:6]
    me, rep = lax.axis_index("shard"), lax.axis_index("rep")
    net = Net(*work[-2:])
    masks = shard_masks(group)
    width, rows, model = vectors.shape[1], x_ref.shape[0], x_ref.shape[1]
    heads = width // head
    scale = 1.0 / math.sqrt(head)
    live = length_ref[0].astype(F32)
    small_ref[0:6] = vectors[0:6]
    small_ref[LN : LN + 1] = jnp.full((1, width), 1.0, F32) * live
    small_ref[LN + 1 :] = jnp.zeros((1, width), F32)
    meet(range(1, group), range(1, reps))
    mine = pl.ds(pl.multiple_of(me * width, width), width)
    small = [
        net.to("shard", j, small_ref, small_all.at[:, mine]) for j in range(1, group)
    ]
    own_small = net.own(small_ref, small_all.at[:, mine])

    def scatter(src, dst, first, n):
        share = src.shape[1] // group

        def columns(j):
            return pl.ds(pl.multiple_of(flip(me, j) * share + first, n), n)

        return [net.to("shard", j, src.at[:, columns(j)], dst) for j in range(1, group)] + [
            net.own(src.at[:, columns(0)], dst)
        ]

    def arrive(copies):
        for copy in copies[:-1]:
            copy.wait_recv()
        copies[-1].wait()

    whole = wu.shape[2]
    share = whole // reps if whole // reps % 128 == 0 else whole
    first = rep * share if share < whole else 0
    lanes = pl.ds(pl.multiple_of(first, share), share)
    ups = scatter(u_ref, wu.at[me, :, lanes], first, share)
    spread = Spread(wu, share, reps if share < whole else 1, spread_sems)
    moved = [scatter(s, d.at[me], 0, width) for s, d in ((q_ref, wq), (k_ref, wk), (v_ref, wv))]
    arrive(small + [own_small])
    gather = Gather(net, nrm, masks)
    for n in range(2):

        def one(at, start):
            v, _ = norm_rows(x_ref[at].astype(F32))
            nrm[0, at] = (v * small_all[FG : FG + 1] + small_all[FS : FS + 1]).astype(BF)
            mix[0, at] = (cot_ref[at].astype(F32) * live_rows(live, start, 16)).astype(BF)

        by_rows(n, rows, one)
        gather.start(n)
    arrive(ups)
    if spread.reps > 1:
        spread.start(1)
    for _ in range(gather.steps - 1):
        gather.both()
    gather.both()
    gather.end()
    for copies, weight, low, row in zip(
        moved, (wq, wk, wv), (queries, keys, values), (6, None, 7)
    ):
        arrive(copies)
        for b in range(0, group, 2):
            left = nrm[b : b + 2].reshape(2 * rows, model)
            res = dot(left, weight[...].reshape(model, width))
            if row is not None:
                res = res + vectors[row : row + 1]
            low[pl.ds(b * rows, 2 * rows)] = res.astype(BF)
    gmix = Gather(net, mix, masks)
    red = Reduce(net, part, work[:2], masks)
    order = [h ^ 1 for h in red.sequence] + red.sequence
    row_at = lax.broadcasted_iota(jnp.int32, (rows, rows), 0)
    col_at = lax.broadcasted_iota(jnp.int32, (rows, rows), 1)

    def side(n):
        if n == 0:
            for i in range(2):
                gmix.start(i)
        if n == 0 and spread.reps > 1:
            spread.arrive(1)
            if spread.reps > 2:
                spread.start(2)
        if n in (3, 6) and gmix.parts[0]["step"] <= gmix.steps:
            gmix.both()

    for n, b in enumerate(order):
        side(n)
        at = pl.ds(b * rows, rows)
        count = small_all[LN : LN + 1, pl.ds(pl.multiple_of(flip(me, b) * width, width), 128)]
        valid = (col_at <= row_at) & (col_at.astype(F32) < count[:, :1])
        for h in range(heads):
            lane = pl.ds(h * head, head)
            scores = dot_nt(queries[at, lane], keys[at, lane]) * scale
            scores = jnp.where(valid, scores, -1e30)
            expo = jnp.exp(scores - jnp.max(scores, axis=-1, keepdims=True))
            p = expo / jnp.sum(expo, axis=-1, keepdims=True)
            p_ref[b, h] = p
            ctx[at, lane] = dot(p.astype(BF), values[at, lane]).astype(BF)
        for c in range(0, model, 1024):
            lane = pl.ds(c, 1024)
            part[b, :, lane] = dot(ctx[at], wo[:, lane]).astype(BF)
        if b % 2:
            red.begin_one(b ^ 1)
        else:
            red.prepare_one(b)
    for k in range(red.steps - 1):
        for n in range(2):
            red.advance(n, k)
    gather = Gather(net, second, masks)
    for n in range(2):
        red.advance(n, red.steps - 1)

        def norm(at, start):
            m = x_ref[at].astype(F32) + (red.total(at) + small_all[OB : OB + 1])
            mid[at] = m
            v, _ = norm_rows(m)
            second[0, at] = (v * small_all[SG : SG + 1] + small_all[SS : SS + 1]).astype(BF)

        by_rows(n, rows, norm)
        gather.start(n)
    hop = 2
    while gmix.parts[0]["step"] <= gmix.steps:
        gmix.both()
    for _ in range(gather.steps):
        if hop < spread.reps:
            spread.arrive(hop)
            hop += 1
            if hop < spread.reps:
                spread.start(hop)
        gather.both()
    while hop < spread.reps:
        spread.arrive(hop)
        hop += 1
        if hop < spread.reps:
            spread.start(hop)
    gmix.end()
    gather.end()
    if spread.reps > 1:
        spread.finish()
    net.finish()


class Line:
    def __init__(self, own, land, out, tall, reps, sems, kept):
        self.kept = kept
        self.own, self.land, self.out = own, land, out
        self.rep, self.reps, self.sems = lax.axis_index("rep"), reps, sems
        self.count, self.size = land.shape[1], land.shape[2]
        self.tall, self.each = tall, tall // 2 // self.size
        self.skew = 2
        self.steps = self.count + 2 * self.skew * (reps - 1)

    def rows(self, way, i):
        row = (i // self.each) * self.tall + way * (self.tall // 2) + (i % self.each) * self.size
        return pl.ds(pl.multiple_of(row, self.size), self.size)

    def copy(self, src, dst, way, back, i, up):
        s, r = self.sems
        at = (2 * way + back) * self.count + i
        return pltpu.make_async_remote_copy(
            src_ref=src,
            dst_ref=dst,
            send_sem=s.at[at],
            recv_sem=r.at[at],
            device_id={"rep": self.rep + (1 if up else -1)},
            device_id_type=MESH,
        )

    def place(self, way):
        return self.rep if way == 0 else self.reps - 1 - self.rep

    def forth(self, way, t):
        at = self.place(way)
        i, last = t - self.skew * at, self.reps - 1

        @pl.when((i >= 0) & (i < self.count))
        def _():
            rows, land = self.rows(way, i), self.land.at[way, i]

            @pl.when(at == 0)
            def _():
                self.copy(self.own.at[rows], land, way, 0, i, way == 0).start()

            @pl.when(at != 0)
            def _():
                self.copy(self.own.at[rows], land, way, 0, i, way == 0).wait_recv()

            @pl.when((at != 0) & (at != last))
            def _():
                self.add(land, rows, land)
                self.copy(land, land, way, 0, i, way == 0).start()

            @pl.when(at == last)
            def _():
                self.add(land, rows, land)
                self.copy(land, self.out.at[rows], way, 1, i, way != 0).start()
                self.keep(way, i).start()

    def add(self, land, rows, to):
        own, step = self.own.at[rows], 16

        @pl.loop(0, self.size // step)
        def _(n):
            at = pl.ds(pl.multiple_of(n * step, step), step)
            to[at] = (land[at].astype(F32) + own[at].astype(F32)).astype(BF)

    def keep(self, way, i):
        return pltpu.make_async_copy(
            self.land.at[way, i],
            self.out.at[self.rows(way, i)],
            self.kept.at[way * self.count + i],
        )

    def back(self, way, t):
        at, last = self.place(way), self.reps - 1
        i = t - self.skew * (last + last - at)

        @pl.when((at != last) & (i >= 0) & (i < self.count))
        def _():
            out = self.out.at[self.rows(way, i)]
            self.copy(out, out, way, 1, i, way != 0).wait_recv()

            @pl.when(at != 0)
            def _():
                self.copy(out, out, way, 1, i, way != 0).start()

    def step(self, t):
        for way in (0, 1):
            self.forth(way, t)
        for way in (0, 1):
            self.back(way, t)

    def finish(self):
        last = self.reps - 1
        for way in (0, 1):
            at = self.place(way)

            @pl.loop(0, self.count)
            def _(i):
                out = self.out.at[self.rows(way, i)]

                @pl.when(at != last)
                def _():
                    self.copy(out, out, way, 0, i, way == 0).wait_send()

                @pl.when(at != 0)
                def _():
                    self.copy(out, out, way, 1, i, way != 0).wait_send()

                @pl.when(at == last)
                def _():
                    self.keep(way, i).wait()


def final_kernel(sizes, head, *refs):
    group, reps = sizes
    (
        gup,
        active,
        second,
        wu,
        wd,
        down_grad,
        mid,
        cot,
        x_ref,
        small,
        q,
        k,
        v,
        p_ref,
        ctx,
        nrm,
        wq,
        wk,
        wv,
        wo,
        cols,
    ) = refs[:21]
    out, gin, smalls, whole = refs[21:25]
    work = refs[25:]
    gmid, sums, land, both, zland, own_all, line_land = work[4:11]
    part, branch, g3, dw, nbuf, wbuf, ubuf, dbuf, loads = work[11:20]
    line_sems, kept = work[20:22], work[22]
    net = Net(*work[-2:])
    masks = shard_masks(group)
    me, rep = lax.axis_index("shard"), lax.axis_index("rep")
    width, rows, model = smalls.shape[1], x_ref.shape[0], x_ref.shape[1]
    heads = width // head
    scale = 1.0 / math.sqrt(head)
    tall = width
    down_rows, wide = down_grad.shape[0], gup.shape[1]
    up_base = down_rows
    out_base = up_base + tall * (wide * group // model)
    loaded = [net.own(down_grad, own_all.at[pl.ds(0, down_rows)])]
    meet(range(1, group), range(1, reps))
    length = small[LN : LN + 1, pl.ds(pl.multiple_of(me * width, width), 128)][:, :1]
    line = Line(own_all, line_land, whole, tall, reps, line_sems, kept)
    for copy in loaded:
        copy.wait()
    arrivals, kept_here = {}, {}

    def place(j):
        return pl.ds(pl.multiple_of(flip(me, j) * width, width), width)

    class stream:
        def __init__(self, source, buf, row):
            self.source, self.buf, self.row = source, buf, row

        def copy(self, a):
            return pltpu.make_async_copy(
                self.source(a), self.buf.at[a % 2], loads.at[self.row, a % 2]
            )

        def begin(self):
            self.copy(0).start()

        def take(self, a):
            if a + 1 < group:
                self.copy(a + 1).start()
            self.copy(a).wait()
            return self.buf[a % 2]

    def tasks():
        each = model // wide
        target = own_all.at[
            pl.ds(pl.multiple_of(up_base + (me // each) * tall, tall), tall),
            pl.ds(pl.multiple_of((me % each) * wide, wide), wide),
        ]
        second_of = stream(lambda j: second.at[:, :, place(j)], nbuf, 0)
        second_of.begin()
        ups = []
        for j in range(group):
            left = second_of.take(j).reshape(group * rows, width)
            at = pl.ds(out_base + j // each * tall, tall), pl.ds(j % each * wide, wide)
            own_all[at[0], at[1]] = dot_tn(left, gup[...]).astype(BF)
            src = own_all.at[at[0], at[1]]
            if j:
                ups.append(net.to("shard", j, src, target))
            else:
                kept_here[up_base] = [net.own(src, target)]
            yield 0
        arrivals[up_base] = ups
        up_of = stream(lambda a: wu.at[a], ubuf, 4)
        up_of.begin()
        for a in range(group):
            block = up_of.take(a)
            part[:, :, pl.ds(a * width, width)] = (
                dot_nt(gup[...], block).astype(BF).reshape(group, rows, width)
            )
            yield 0
        red = Reduce(net, part, work[:2], masks)
        red.begin()
        yield 18
        red.prepare()
        yield 23
        for s in range(red.steps - 1):
            for n in range(2):
                red.advance(n, s)
        yield 26
        for n in range(2):
            red.advance(n, red.steps - 1)
        for copy in kept_here.pop(up_base, []):
            copy.wait()
        net.settle()
        sums[...] = jnp.zeros_like(sums)
        gather = Gather(net, branch, masks)
        for n in range(2):

            def back(at, start):
                g = red.total(at)
                w, inv = norm_rows(mid[at])
                gout = cot[at].astype(F32) * live_rows(length, start, 16)
                res = gout + norm_back(g, small[SG : SG + 1], w, inv)
                gmid[at] = res
                low = res.astype(BF)
                branch[0, at] = low
                sums[SG : SG + 1] += jnp.sum(g * w, axis=0, keepdims=True)
                sums[SS : SS + 1] += jnp.sum(g, axis=0, keepdims=True)
                sums[OB : OB + 1] += jnp.sum(low.astype(F32), axis=0, keepdims=True)
                sums[DB : DB + 1] += jnp.sum(gout, axis=0, keepdims=True)

            by_rows(n, rows, back)
            gather.start(n)
        for s in range(gather.steps):
            yield 30 + 4 * s
            gather.both()
        yield 30 + 4 * gather.steps
        gather.end()
        early = len(net.open)
        for b in range(group):
            at = pl.ds(b * rows, rows)
            gc = dot_nt(branch[b], wo[...]).astype(BF)
            for h in range(heads):
                lane = pl.ds(h * head, head)
                qh, kh, vh = q[at, lane], k[at, lane], v[at, lane]
                gch = gc[:, h * head : (h + 1) * head]
                p = p_ref[b, h]
                gw = dot_nt(gch, vh)
                inner = jnp.sum(p * gw, axis=-1, keepdims=True)
                gs = (p * (gw - inner)).astype(BF)
                g3[b, :, pl.ds(h * head, head)] = (dot(gs, kh) * scale).astype(BF)
                g3[b, :, pl.ds(width + h * head, head)] = (dot_tn(gs, qh) * scale).astype(BF)
                g3[b, :, pl.ds(2 * width + h * head, head)] = dot_tn(p.astype(BF), gch).astype(BF)
            yield 0
        n_col = 512
        for c in range(0, model, n_col):
            lane = pl.ds(c, n_col)
            full = branch[:, :, lane].reshape(group * rows, n_col)
            own_all[pl.ds(out_base, tall), lane] = dot_tn(ctx[...], full).astype(BF)
            yield 0
        arrivals[out_base] = []
        grads = g3[...].reshape(group * rows, 3 * width)
        total = jnp.sum(grads.astype(F32), axis=0, keepdims=True)
        both[8:9] = total[:, :width]
        both[9:10] = total[:, 2 * width :]
        both[10:16] = cols[...]

        def normed_of(j):
            return pltpu.make_async_copy(nrm.at[:, :, place(j)], nbuf.at[j % 2], loads.at[0, j % 2])

        normed_of(0).start()
        grown = {out_base + (i + 1) * tall: [] for i in range(3)}
        for j in range(group):
            if j + 1 < group:
                normed_of(j + 1).start()
            normed_of(j).wait()
            left = nbuf[j % 2].reshape(group * rows, width)
            right = g3[...].reshape(group * rows, 3 * width)
            dw[j] = dot_tn(left, right).astype(BF)
            for i in range(3):
                src = dw.at[j, :, pl.ds(i * width, width)]
                base = out_base + (i + 1) * tall
                dst = own_all.at[pl.ds(base, tall), place(0)]
                if j:
                    grown[base].append(net.to("shard", j, src, dst))
                else:
                    kept_here[base] = [net.own(src, dst)]
            yield 0
        arrivals.update(grown)

        def weight_of(a):
            return [
                pltpu.make_async_copy(w.at[a], wbuf.at[a % 2, i], loads.at[1 + i, a % 2])
                for i, w in enumerate((wq, wk, wv))
            ]

        net.settle(early)
        for copy in weight_of(0):
            copy.start()
        for a in range(group):
            if a + 1 < group:
                for copy in weight_of(a + 1):
                    copy.start()
            for copy in weight_of(a):
                copy.wait()
            left = g3[...].reshape(group * rows, 3 * width)
            res = dot_nt(left[:, :width], wbuf[a % 2, 0])
            res = res + dot_nt(left[:, width : 2 * width], wbuf[a % 2, 1])
            res = res + dot_nt(left[:, 2 * width :], wbuf[a % 2, 2])
            part[:, :, pl.ds(a * width, width)] = res.astype(BF).reshape(group, rows, width)
            yield 0
        red = Reduce(net, part, work[:2], masks)
        red.begin()
        yield 0
        down_of = stream(lambda a: wd.at[:, pl.ds(a * width, width)], dbuf, 4)
        down_of.begin()
        for a in range(group):
            block = down_of.take(a)
            branch[:, :, pl.ds(a * width, width)] = (
                dot(active[...], block).astype(BF).reshape(group, rows, width)
            )
            if a % 2:
                yield 0
        late = Reduce(net, branch, work[2:4], masks)
        late.begin()
        yield 69
        red.prepare()
        for s in range(red.steps - 1):
            yield 75 + 4 * s
            for n in range(2):
                red.advance(n, s)
        yield 80
        for n in range(2):
            red.advance(n, red.steps - 1)

            def first(at, start):
                g = red.total(at)
                w, inv = norm_rows(x_ref[at].astype(F32))
                gin[at] = (gmid[at] + norm_back(g, small[FG : FG + 1], w, inv)).astype(BF)
                sums[FG : FG + 1] += jnp.sum(g * w, axis=0, keepdims=True)
                sums[FS : FS + 1] += jnp.sum(g, axis=0, keepdims=True)

            by_rows(n, rows, first)
        tiny = [net.to("shard", j, sums.at[:, place(j)], land.at[me]) for j in range(1, group)]
        own = net.own(sums.at[:, place(0)], land.at[me])
        yield 83
        late.prepare()
        yield 85
        for copy in tiny:
            copy.wait_recv()
        own.wait()
        total = land[0]
        for j in range(1, group):
            total = total + land[j]
        both[0:8] = total
        tiny = [net.to("rep", h, both, zland.at[rep]) for h in range(1, reps)]
        own = net.own(both, zland.at[rep])
        for s in range(late.steps - 1):
            yield 90 + 4 * s
            for n in range(2):
                late.advance(n, s)
        yield 94
        for n in range(2):
            late.advance(n, late.steps - 1)

            def close(at, start):
                m = mid[at] + (late.total(at) + small[DB : DB + 1])
                out[at] = (m * live_rows(length, start, 16)).astype(BF)

            by_rows(n, rows, close)
        yield 97
        for copy in tiny:
            copy.wait_recv()
        own.wait()
        total = zland[0]
        for h in range(1, reps):
            total = total + zland[h]
        smalls[...] = total

    todo = tasks()
    resume = next(todo)
    for t in range(line.steps):
        base = t // line.each * tall
        if t < line.count and t % line.each == 0 and (base == up_base or base >= out_base):
            while base not in arrivals:
                resume = next(todo, None)
            for copy in arrivals[base]:
                copy.wait_recv()
            for copy in kept_here.pop(base, []):
                copy.wait()
        line.step(t)
        if resume is not None and t >= resume:
            resume = next(todo, None)
    for _ in todo:
        pass
    line.finish()
    net.finish()


def call(body, number, sizes, outs, scratch, copies, args, far=(), far_outs=(), scalars=()):
    return pl.pallas_call(
        functools.partial(body, *sizes),
        out_shape=[jax.ShapeDtypeStruct(s, d) for s, d in outs],
        in_specs=[
            ANY if i in far else SCALAR if i in scalars else VM for i in range(len(args))
        ],
        out_specs=[ANY if i in far_outs else VM for i in range(len(outs))],
        scratch_shapes=list(scratch)
        + [pltpu.SemaphoreType.DMA((copies,)), pltpu.SemaphoreType.DMA((copies,))],
        compiler_params=pltpu.CompilerParams(
            collective_id=number, has_side_effects=True, vmem_limit_bytes=LIMIT
        ),
        name=body.__name__,
    )(*args)


def dot(a, b):
    return jnp.dot(a, b, preferred_element_type=F32)


def dot_nt(a, b):
    return jnp.einsum("tc,rc->tr", a, b, preferred_element_type=F32)


def dot_tn(a, b):
    return jnp.einsum("tr,tc->rc", a, b, preferred_element_type=F32)


def local(
    block_input,
    lengths,
    first_gain,
    first_shift,
    query_weight,
    query_bias,
    key_weight,
    value_weight,
    value_bias,
    out_weight,
    out_bias,
    second_gain,
    second_shift,
    up_weight,
    up_bias,
    down_weight,
    down_bias,
    cotangent,
):
    rows, width = block_input.shape[1], block_input.shape[2]
    hidden = up_weight.shape[1]
    group, reps = lax.axis_size("shard"), lax.axis_size("rep")
    sizes = (group, reps)
    g, f = width // group, hidden // group
    head = width // HEADS
    scale = 1.0 / math.sqrt(head)
    me = lax.axis_index("shard")
    vectors = jnp.concatenate(
        [
            first_gain,
            first_shift,
            out_bias,
            second_gain,
            second_shift,
            down_bias,
            query_bias,
            value_bias,
        ]
    )
    vectors = vectors.reshape(8, g).astype(F32)
    x, cot = block_input[0], cotangent[0]
    blocks = (group, rows, width)
    masks = shard_masks(group)
    work = reduce_shapes(group, rows, width, masks)
    tokens, column = group * rows, ((group, g, g), BF)
    nrm, small_all, wq, wk, wv, wu, queries, keys, values, p, ctx, mid, second, mix = call(
        forward_kernel,
        1,
        (sizes, head),
        [
            (blocks, BF),
            ((8, width), F32),
            column,
            column,
            column,
            ((group, g, f), BF),
            ((tokens, g), BF),
            ((tokens, g), BF),
            ((tokens, g), BF),
            ((group, g // head, rows, rows), F32),
            ((tokens, g), BF),
            ((rows, width), F32),
            (blocks, BF),
            (blocks, BF),
        ],
        work
        + [pltpu.VMEM(blocks, BF), pltpu.VMEM((8, g), F32)]
        + [pltpu.SemaphoreType.DMA((2 * reps,))] * 2,
        320,
        (
            lengths,
            x,
            cot,
            vectors,
            query_weight,
            key_weight,
            value_weight,
            up_weight,
            out_weight,
        ),
        (4, 5, 6, 7),
        (),
        (0,),
    )
    flat = lambda a: a.reshape(-1, a.shape[-1])
    wu = flat(wu)
    second = flat(second)
    mixed = flat(mix)
    upper = dot(second, wu) + up_bias.astype(F32)
    cdf = 0.5 * (1.0 + lax.erf(upper * (1.0 / math.sqrt(2.0))))
    pdf = jnp.exp(-0.5 * upper * upper) * (1.0 / math.sqrt(2.0 * math.pi))
    active = (upper * cdf).astype(BF)
    gup = (dot_nt(mixed, down_weight) * (cdf + upper * pdf)).astype(BF)
    down_grad = dot_tn(active, mixed).astype(BF)
    cols = jnp.concatenate(
        [jnp.sum(gup.astype(F32), axis=0).reshape(4, g), jnp.zeros((2, g), F32)]
    )
    blocks_up = hidden // width
    tall_all = f + (4 + blocks_up) * g
    piece = 16
    count = tall_all // 2 // piece
    scratch = (
        work
        + work
        + [
            pltpu.VMEM((rows, width), F32),
            pltpu.VMEM((8, width), F32),
            pltpu.VMEM((group, 8, g), F32),
            pltpu.VMEM((16, g), F32),
            pltpu.VMEM((reps, 16, g), F32),
            pltpu.VMEM((tall_all, width), BF),
            pltpu.VMEM((2, count, piece, width), BF),
            pltpu.VMEM(blocks, BF),
            pltpu.VMEM(blocks, BF),
            pltpu.VMEM((group, rows, 3 * g), BF),
            pltpu.VMEM((group, g, 3 * g), BF),
            pltpu.VMEM((2, group, rows, g), BF),
            pltpu.VMEM((2, 3, g, g), BF),
            pltpu.VMEM((2, g, f), BF),
            pltpu.VMEM((2, f, g), BF),
            pltpu.SemaphoreType.DMA((5, 2)),
        ]
        + [pltpu.SemaphoreType.DMA((4 * count,))] * 2
        + [pltpu.SemaphoreType.DMA((2 * count,))]
    )
    out, gin, smalls, whole = call(
        final_kernel,
        2,
        (sizes, head),
        [
            ((rows, width), BF),
            ((rows, width), BF),
            ((16, g), F32),
            ((tall_all, width), BF),
        ],
        scratch,
        320,
        (
            gup,
            active,
            second.reshape(blocks),
            wu.reshape(group, g, f),
            down_weight,
            down_grad,
            mid,
            cot,
            x,
            small_all,
            queries,
            keys,
            values,
            p,
            ctx,
            nrm,
            wq,
            wk,
            wv,
            out_weight,
            cols,
        ),
        (2, 3, 4, 5, 15, 16, 17, 18),
        (3,),
    )
    dd = whole[:f].astype(F32)
    ups = [whole[f + i * g : f + (i + 1) * g] for i in range(blocks_up)]
    du = jnp.concatenate(ups, axis=1).astype(F32)
    skip = f + blocks_up * g
    do, dq, dk, dv = (whole[skip + i * g : skip + (i + 1) * g].astype(F32) for i in range(4))
    return (
        out[None],
        gin[None],
        smalls[FG],
        smalls[FS],
        dq,
        smalls[8],
        dk,
        dv,
        smalls[9],
        do,
        smalls[OB],
        smalls[SG],
        smalls[SS],
        du,
        smalls[10:14].reshape(-1),
        dd,
        smalls[DB],
    )


def solution(mesh):
    tokens = P(("rep", "shard"), None, None)
    vec, mat = P("shard"), P("shard", None)
    return jax.shard_map(
        local,
        mesh=mesh,
        in_specs=(
            tokens,
            P(("rep", "shard")),
            vec,
            vec,
            mat,
            vec,
            mat,
            mat,
            vec,
            mat,
            vec,
            vec,
            vec,
            mat,
            vec,
            mat,
            vec,
            tokens,
        ),
        out_specs=(
            tokens,
            tokens,
            vec,
            vec,
            mat,
            vec,
            mat,
            mat,
            vec,
            mat,
            vec,
            vec,
            vec,
            mat,
            vec,
            mat,
            vec,
        ),
        check_vma=False,
    )
```

```python
import functools
import math

import jax
import jax.numpy as jnp
from jax import lax
from jax.experimental import pallas as pl
from jax.experimental.pallas import tpu as pltpu
from jax.sharding import PartitionSpec as P

HEADS = 16
MESH = pl.DeviceIdType.MESH
BF = jnp.bfloat16
F32 = jnp.float32
VM = pl.BlockSpec(memory_space=pltpu.VMEM)
SCALAR = pl.BlockSpec(memory_space=pltpu.SMEM)
ANY = pl.BlockSpec(memory_space=pl.ANY)
LIMIT = 63 * 2**20


def flip(index, mask):
    bit = 1
    while bit <= mask:
        if mask & bit:
            index = index + bit - 2 * bit * ((index // bit) % 2)
        bit *= 2
    return index


def span(masks):
    out = [0]
    for m in masks:
        out = out + [h ^ m for h in out]
    return out


def pair_masks(size):
    masks, bit = [], 1
    while bit < size:
        masks.append(bit + bit // 2 if len(masks) % 2 and size >= 2 * bit else bit)
        bit *= 2
    return masks


def shard_masks(size):
    masks, bit = [], 2
    while bit < size:
        masks.append(bit if len(masks) < 2 else bit + bit // 2)
        bit *= 2
    return masks


def orders(masks):
    return [list(masks), list(masks[1:]) + list(masks[:1])]


class Net:
    def __init__(self, send, recv):
        self.send, self.recv, self.used, self.open = send, recv, 0, []

    def to(self, axis, mask, src, dst):
        k = self.used
        self.used += 1
        copy = pltpu.make_async_remote_copy(
            src_ref=src,
            dst_ref=dst,
            send_sem=self.send.at[k],
            recv_sem=self.recv.at[k],
            device_id={axis: flip(lax.axis_index(axis), mask)},
            device_id_type=MESH,
        )
        copy.start()
        self.open.append(copy)
        return copy

    def own(self, src, dst):
        k = self.used
        self.used += 1
        copy = pltpu.make_async_copy(src, dst, self.send.at[k])
        copy.start()
        return copy

    def settle(self, count=None):
        for copy in self.open[:count]:
            copy.wait_send()
        self.open = self.open[len(self.open) if count is None else count :]

    finish = settle


def meet(shard_set, rep_set):
    barrier = pltpu.get_barrier_semaphore()
    for axis, masks in (("shard", shard_set), ("rep", rep_set)):
        for m in masks:
            pl.semaphore_signal(
                barrier,
                inc=1,
                device_id={axis: flip(lax.axis_index(axis), m)},
                device_id_type=MESH,
            )
    pl.semaphore_wait(barrier, len(shard_set) + len(rep_set))


class Gather:
    def __init__(self, net, buf, masks):
        self.net, self.buf = net, buf
        rows = buf.shape[1] // 2
        self.parts = [
            dict(rows=pl.ds(i * rows, rows), order=o, held=[0], new=[0], wait=[], step=0)
            for i, o in enumerate(orders(masks))
        ]
        self.cores = []
        self.steps = len(masks)

    def start(self, n):
        net, buf, part = self.net, self.buf, self.parts[n]
        fresh, rows = part["new"], part["rows"]
        if part["step"] < self.steps:
            m = part["order"][part["step"]]
            part["new"] = [h ^ m for h in part["held"]]
            part["wait"] = [
                net.to("shard", m, buf.at[h, rows], buf.at[h ^ m, rows]) for h in part["held"]
            ]
            part["held"] = part["held"] + part["new"]
        self.cores += [net.to("shard", 1, buf.at[h, rows], buf.at[h ^ 1, rows]) for h in fresh]
        part["step"] += 1

    def arrive(self, n):
        for copy in self.parts[n]["wait"]:
            copy.wait_recv()
        self.parts[n]["wait"] = []

    def both(self):
        for n in range(2):
            self.arrive(n)
            self.start(n)

    def end(self):
        for copy in self.cores:
            copy.wait_recv()

    def finish(self):
        for _ in range(self.steps):
            self.both()
        self.end()


def reduce_shapes(group, rows, width, masks):
    count = 2 ** len(masks) - 1
    return [
        pltpu.VMEM((group // 2, rows, width), BF),
        pltpu.VMEM((count, rows, width), BF),
    ]


class Reduce:
    def __init__(self, net, part, work, masks):
        self.net, self.part = net, part
        self.sums, self.land = work
        self.group, self.rows = part.shape[0], part.shape[1]
        self.cores = {}
        self.half = self.rows // 2
        self.steps = len(masks)
        self.orders = orders(masks)
        self.flight = [[], []]
        self.sequence = sorted(
            span(masks), key=lambda h: -sum(self.sends(n, h) for n in range(2))
        )

    def sends(self, n, h):
        order = self.orders[n]
        return h not in span(order[1:])

    def begin_one(self, h):
        self.cores[h] = self.net.to("shard", 1, self.part.at[h ^ 1], self.sums.at[h // 2])

    def begin(self):
        for h in self.sequence:
            self.begin_one(h)

    def add(self, h, start, count, other):
        step = min(count, 32)

        @pl.loop(0, count // step)
        def _(i):
            at = pl.ds(pl.multiple_of(start + i * step, step), step)
            self.sums[h // 2, at] = (
                self.sums[h // 2, at].astype(F32) + other[at].astype(F32)
            ).astype(BF)

    def send(self, n, k, h):
        order = self.orders[n]
        rest = span(order[k + 1 :])
        base = sum(2 ** (self.steps - 1 - i) for i in range(k))
        to = h ^ order[k]
        rows = pl.ds(n * self.half, self.half)
        slot = base + rest.index(to)
        copy = self.net.to(
            "shard", order[k], self.sums.at[h // 2, rows], self.land.at[slot, rows]
        )
        self.flight[n].append((copy, to, slot))

    def prepare_one(self, h):
        self.cores[h].wait_recv()
        self.add(h, 0, self.rows, self.part.at[h])
        for n in range(2):
            if self.sends(n, h):
                self.send(n, 0, h)

    def prepare(self):
        for h in self.sequence:
            self.prepare_one(h)

    def advance(self, n, k):
        flight, self.flight[n] = self.flight[n], []
        rest = span(self.orders[n][k + 2 :])
        flight.sort(key=lambda f: f[1] in rest)
        for copy, h, slot in flight:
            copy.wait_recv()
            if k < self.steps - 1:
                self.add(h, n * self.half, self.half, self.land.at[slot])
                if h not in rest:
                    self.send(n, k + 1, h)
            else:
                self.last = slot

    def run(self):
        self.begin()
        self.prepare()
        for k in range(self.steps - 1):
            for n in range(2):
                self.advance(n, k)

    def total(self, at):
        return self.sums[0, at].astype(F32) + self.land[self.last, at].astype(F32)


def norm_rows(v):
    center = v - jnp.mean(v, axis=-1, keepdims=True)
    spread = jnp.mean(center * center, axis=-1, keepdims=True)
    inv = lax.rsqrt(spread + 1e-05)
    return center * inv, inv


def norm_back(grad, gain, n, inv):
    scaled = grad * gain
    return inv * (
        scaled
        - jnp.mean(scaled, axis=-1, keepdims=True)
        - n * jnp.mean(scaled * n, axis=-1, keepdims=True)
    )


FG, FS, OB, SG, SS, DB, LN = range(7)


def live_rows(length, start, rows):
    at = start + lax.broadcasted_iota(jnp.int32, (rows, 1), 0)
    return (at.astype(F32) < length).astype(F32)


def by_rows(n, count, body):
    step = 16

    @pl.loop(0, count // 2 // step)
    def _(i):
        start = pl.multiple_of(n * (count // 2) + i * step, step)
        body(pl.ds(start, step), start)


class Spread:
    def __init__(self, buf, columns, reps, sems):
        self.buf, self.columns, self.reps, self.sems = buf, columns, reps, sems
        self.rep = lax.axis_index("rep")

    def copy(self, hop, way, member):
        s, r = self.sems
        n = self.columns
        view = self.buf.at[:, :, pl.ds(pl.multiple_of(member * n, n), n)]
        at = 2 * (hop - 1) + way
        return pltpu.make_async_remote_copy(
            src_ref=view,
            dst_ref=view,
            send_sem=s.at[at],
            recv_sem=r.at[at],
            device_id={"rep": self.rep + (1 - 2 * way)},
            device_id_type=MESH,
        )

    def each(self, hop, sent, act):
        rep, last = self.rep, self.reps - 1
        for way in (0, 1):
            sign = 1 - 2 * way
            if sent:
                member = rep - sign * (hop - 1)
                to = rep + sign
                here = (to >= 0) & (to <= last)
            else:
                member = rep - sign * hop
                here = True

            @pl.when((member >= 0) & (member <= last) & here)
            def _():
                act(self.copy(hop, way, member))

    def start(self, hop):
        self.each(hop, True, lambda c: c.start())

    def arrive(self, hop):
        self.each(hop, False, lambda c: c.wait_recv())

    def finish(self):
        for hop in range(1, self.reps):
            self.each(hop, True, lambda c: c.wait_send())


def forward_kernel(sizes, head, *refs):
    group, reps = sizes
    length_ref, x_ref, cot_ref, q_ref, k_ref, v_ref, u_ref, wo, vectors = refs[:9]
    refs = refs[9:]
    (nrm_out, small_all, wq_out, wk_out, wv_out, wu, queries, keys, values, p_ref, ctx) = refs[:11]
    mid, second, mix = refs[11:14]
    work = refs[14:]
    part, small_ref = work[2:4]
    spread_sems = work[4:6]
    nrm, wq, wk, wv = work[6:10]
    me, rep = lax.axis_index("shard"), lax.axis_index("rep")
    net = Net(*work[-2:])
    masks = shard_masks(group)
    width, rows, model = vectors.shape[1], x_ref.shape[0], x_ref.shape[1]
    heads = width // head
    scale = 1.0 / math.sqrt(head)
    live = length_ref[0].astype(F32)
    small_ref[0:6] = vectors[0:6]
    small_ref[LN : LN + 1] = jnp.full((1, width), 1.0, F32) * live
    small_ref[LN + 1 :] = jnp.zeros((1, width), F32)
    meet(range(1, group), range(1, reps))
    mine = pl.ds(pl.multiple_of(me * width, width), width)
    small = [
        net.to("shard", j, small_ref, small_all.at[:, mine]) for j in range(1, group)
    ]
    own_small = net.own(small_ref, small_all.at[:, mine])

    def scatter(src, dst, first, n):
        share = src.shape[1] // group

        def columns(j):
            return pl.ds(pl.multiple_of(flip(me, j) * share + first, n), n)

        return [net.to("shard", j, src.at[:, columns(j)], dst) for j in range(1, group)] + [
            net.own(src.at[:, columns(0)], dst)
        ]

    def arrive(copies):
        for copy in copies[:-1]:
            copy.wait_recv()
        copies[-1].wait()

    whole = wu.shape[2]
    share = whole // reps if whole // reps % 128 == 0 else whole
    first = rep * share if share < whole else 0
    lanes = pl.ds(pl.multiple_of(first, share), share)
    ups = scatter(u_ref, wu.at[me, :, lanes], first, share)
    spread = Spread(wu, share, reps if share < whole else 1, spread_sems)
    moved = [scatter(s, d.at[me], 0, width) for s, d in ((q_ref, wq), (k_ref, wk), (v_ref, wv))]
    arrive(small + [own_small])
    gather = Gather(net, nrm, masks)
    for n in range(2):

        def one(at, start):
            v, _ = norm_rows(x_ref[at].astype(F32))
            nrm[0, at] = (v * small_all[FG : FG + 1] + small_all[FS : FS + 1]).astype(BF)
            mix[0, at] = (cot_ref[at].astype(F32) * live_rows(live, start, 16)).astype(BF)

        by_rows(n, rows, one)
        gather.start(n)
    arrive(ups)
    if spread.reps > 1:
        spread.start(1)
    for _ in range(gather.steps - 1):
        gather.both()
    gather.both()
    gather.end()
    for copies, weight, low, row in zip(
        moved, (wq, wk, wv), (queries, keys, values), (6, None, 7)
    ):
        arrive(copies)
        for b in range(0, group, 2):
            left = nrm[b : b + 2].reshape(2 * rows, model)
            res = dot(left, weight[...].reshape(model, width))
            if row is not None:
                res = res + vectors[row : row + 1]
            low[pl.ds(b * rows, 2 * rows)] = res.astype(BF)
    leaving = [
        net.own(a, b)
        for a, b in ((nrm, nrm_out), (wq, wq_out), (wk, wk_out), (wv, wv_out))
    ]
    gmix = Gather(net, mix, masks)
    red = Reduce(net, part, work[:2], masks)
    order = [h ^ 1 for h in red.sequence] + red.sequence
    row_at = lax.broadcasted_iota(jnp.int32, (rows, rows), 0)
    col_at = lax.broadcasted_iota(jnp.int32, (rows, rows), 1)

    def side(n):
        if n == 0:
            for i in range(2):
                gmix.start(i)
        if n == 0 and spread.reps > 1:
            spread.arrive(1)
            if spread.reps > 2:
                spread.start(2)
        if n in (3, 6) and gmix.parts[0]["step"] <= gmix.steps:
            gmix.both()

    for n, b in enumerate(order):
        side(n)
        at = pl.ds(b * rows, rows)
        count = small_all[LN : LN + 1, pl.ds(pl.multiple_of(flip(me, b) * width, width), 128)]
        valid = (col_at <= row_at) & (col_at.astype(F32) < count[:, :1])
        for h in range(heads):
            lane = pl.ds(h * head, head)
            scores = dot_nt(queries[at, lane], keys[at, lane]) * scale
            scores = jnp.where(valid, scores, -1e30)
            expo = jnp.exp(scores - jnp.max(scores, axis=-1, keepdims=True))
            p = expo / jnp.sum(expo, axis=-1, keepdims=True)
            p_ref[b, h] = p
            ctx[at, lane] = dot(p.astype(BF), values[at, lane]).astype(BF)
        for c in range(0, model, 1024):
            lane = pl.ds(c, 1024)
            part[b, :, lane] = dot(ctx[at], wo[:, lane]).astype(BF)
        if b % 2:
            red.begin_one(b ^ 1)
        else:
            red.prepare_one(b)
    for k in range(red.steps - 1):
        for n in range(2):
            red.advance(n, k)
    gather = Gather(net, second, masks)
    for n in range(2):
        red.advance(n, red.steps - 1)

        def norm(at, start):
            m = x_ref[at].astype(F32) + (red.total(at) + small_all[OB : OB + 1])
            mid[at] = m
            v, _ = norm_rows(m)
            second[0, at] = (v * small_all[SG : SG + 1] + small_all[SS : SS + 1]).astype(BF)

        by_rows(n, rows, norm)
        gather.start(n)
    hop = 2
    while gmix.parts[0]["step"] <= gmix.steps:
        gmix.both()
    for _ in range(gather.steps):
        if hop < spread.reps:
            spread.arrive(hop)
            hop += 1
            if hop < spread.reps:
                spread.start(hop)
        gather.both()
    while hop < spread.reps:
        spread.arrive(hop)
        hop += 1
        if hop < spread.reps:
            spread.start(hop)
    gmix.end()
    gather.end()
    if spread.reps > 1:
        spread.finish()
    for copy in leaving:
        copy.wait()
    net.finish()


class Line:
    def __init__(self, own, land, out, tall, reps, sems, kept):
        self.kept = kept
        self.own, self.land, self.out = own, land, out
        self.rep, self.reps, self.sems = lax.axis_index("rep"), reps, sems
        self.count, self.size = land.shape[1], land.shape[2]
        self.tall, self.each = tall, tall // 2 // self.size
        self.skew = 2
        self.steps = self.count + 2 * self.skew * (reps - 1)

    def rows(self, way, i):
        row = (i // self.each) * self.tall + way * (self.tall // 2) + (i % self.each) * self.size
        return pl.ds(pl.multiple_of(row, self.size), self.size)

    def copy(self, src, dst, way, back, i, up):
        s, r = self.sems
        at = (2 * way + back) * self.count + i
        return pltpu.make_async_remote_copy(
            src_ref=src,
            dst_ref=dst,
            send_sem=s.at[at],
            recv_sem=r.at[at],
            device_id={"rep": self.rep + (1 if up else -1)},
            device_id_type=MESH,
        )

    def place(self, way):
        return self.rep if way == 0 else self.reps - 1 - self.rep

    def forth(self, way, t):
        at = self.place(way)
        i, last = t - self.skew * at, self.reps - 1

        @pl.when((i >= 0) & (i < self.count))
        def _():
            rows, land = self.rows(way, i), self.land.at[way, i]

            @pl.when(at == 0)
            def _():
                self.copy(self.own.at[rows], land, way, 0, i, way == 0).start()

            @pl.when(at != 0)
            def _():
                self.copy(self.own.at[rows], land, way, 0, i, way == 0).wait_recv()

            @pl.when((at != 0) & (at != last))
            def _():
                self.add(land, rows, land)
                self.copy(land, land, way, 0, i, way == 0).start()

            @pl.when(at == last)
            def _():
                self.add(land, rows, land)
                self.copy(land, self.out.at[rows], way, 1, i, way != 0).start()
                self.keep(way, i).start()

    def add(self, land, rows, to):
        own, step = self.own.at[rows], 16

        @pl.loop(0, self.size // step)
        def _(n):
            at = pl.ds(pl.multiple_of(n * step, step), step)
            to[at] = (land[at].astype(F32) + own[at].astype(F32)).astype(BF)

    def keep(self, way, i):
        return pltpu.make_async_copy(
            self.land.at[way, i],
            self.out.at[self.rows(way, i)],
            self.kept.at[way * self.count + i],
        )

    def back(self, way, t):
        at, last = self.place(way), self.reps - 1
        i = t - self.skew * (last + last - at)

        @pl.when((at != last) & (i >= 0) & (i < self.count))
        def _():
            out = self.out.at[self.rows(way, i)]
            self.copy(out, out, way, 1, i, way != 0).wait_recv()

            @pl.when(at != 0)
            def _():
                self.copy(out, out, way, 1, i, way != 0).start()

    def step(self, t):
        for way in (0, 1):
            self.forth(way, t)
        for way in (0, 1):
            self.back(way, t)

    def finish(self):
        last = self.reps - 1
        for way in (0, 1):
            at = self.place(way)

            @pl.loop(0, self.count)
            def _(i):
                out = self.out.at[self.rows(way, i)]

                @pl.when(at != last)
                def _():
                    self.copy(out, out, way, 0, i, way == 0).wait_send()

                @pl.when(at != 0)
                def _():
                    self.copy(out, out, way, 1, i, way != 0).wait_send()

                @pl.when(at == last)
                def _():
                    self.keep(way, i).wait()


def final_kernel(sizes, head, *refs):
    group, reps = sizes
    (
        gup,
        active,
        second,
        wu,
        wd,
        down_grad,
        mid,
        cot,
        x_ref,
        small,
        q,
        k,
        v,
        p_ref,
        ctx,
        nrm,
        wq,
        wk,
        wv,
        wo,
        cols,
    ) = refs[:21]
    out, gin, smalls, whole = refs[21:25]
    work = refs[25:]
    gmid, sums, land, both, zland, own_all, line_land = work[4:11]
    part, branch, g3, dw, nbuf, wbuf, ubuf, dbuf, loads = work[11:20]
    line_sems, kept = work[20:22], work[22]
    net = Net(*work[-2:])
    masks = shard_masks(group)
    me, rep = lax.axis_index("shard"), lax.axis_index("rep")
    width, rows, model = smalls.shape[1], x_ref.shape[0], x_ref.shape[1]
    heads = width // head
    scale = 1.0 / math.sqrt(head)
    tall = width
    down_rows, wide = down_grad.shape[0], gup.shape[1]
    up_base = down_rows
    out_base = up_base + tall * (wide * group // model)
    loaded = [net.own(down_grad, own_all.at[pl.ds(0, down_rows)])]
    meet(range(1, group), range(1, reps))
    length = small[LN : LN + 1, pl.ds(pl.multiple_of(me * width, width), 128)][:, :1]
    line = Line(own_all, line_land, whole, tall, reps, line_sems, kept)
    for copy in loaded:
        copy.wait()
    arrivals, kept_here = {}, {}

    def place(j):
        return pl.ds(pl.multiple_of(flip(me, j) * width, width), width)

    class stream:
        def __init__(self, source, buf, row):
            self.source, self.buf, self.row = source, buf, row

        def copy(self, a):
            return pltpu.make_async_copy(
                self.source(a), self.buf.at[a % 2], loads.at[self.row, a % 2]
            )

        def begin(self):
            self.copy(0).start()

        def take(self, a):
            if a + 1 < group:
                self.copy(a + 1).start()
            self.copy(a).wait()
            return self.buf[a % 2]

    def tasks():
        each = model // wide
        target = own_all.at[
            pl.ds(pl.multiple_of(up_base + (me // each) * tall, tall), tall),
            pl.ds(pl.multiple_of((me % each) * wide, wide), wide),
        ]
        second_of = stream(lambda j: second.at[:, :, place(j)], nbuf, 0)
        second_of.begin()
        ups = []
        for j in range(group):
            left = second_of.take(j).reshape(group * rows, width)
            at = pl.ds(out_base + j // each * tall, tall), pl.ds(j % each * wide, wide)
            own_all[at[0], at[1]] = dot_tn(left, gup[...]).astype(BF)
            src = own_all.at[at[0], at[1]]
            if j:
                ups.append(net.to("shard", j, src, target))
            else:
                kept_here[up_base] = [net.own(src, target)]
            yield 0
        arrivals[up_base] = ups
        up_of = stream(lambda a: wu.at[a], ubuf, 4)
        up_of.begin()
        for a in range(group):
            block = up_of.take(a)
            part[:, :, pl.ds(a * width, width)] = (
                dot_nt(gup[...], block).astype(BF).reshape(group, rows, width)
            )
            yield 0
        red = Reduce(net, part, work[:2], masks)
        red.begin()
        yield 18
        red.prepare()
        yield 23
        for s in range(red.steps - 1):
            for n in range(2):
                red.advance(n, s)
        yield 26
        for n in range(2):
            red.advance(n, red.steps - 1)
        for copy in kept_here.pop(up_base, []):
            copy.wait()
        net.settle()
        sums[...] = jnp.zeros_like(sums)
        gather = Gather(net, branch, masks)
        for n in range(2):

            def back(at, start):
                g = red.total(at)
                w, inv = norm_rows(mid[at])
                gout = cot[at].astype(F32) * live_rows(length, start, 16)
                res = gout + norm_back(g, small[SG : SG + 1], w, inv)
                gmid[at] = res
                low = res.astype(BF)
                branch[0, at] = low
                sums[SG : SG + 1] += jnp.sum(g * w, axis=0, keepdims=True)
                sums[SS : SS + 1] += jnp.sum(g, axis=0, keepdims=True)
                sums[OB : OB + 1] += jnp.sum(low.astype(F32), axis=0, keepdims=True)
                sums[DB : DB + 1] += jnp.sum(gout, axis=0, keepdims=True)

            by_rows(n, rows, back)
            gather.start(n)
        for s in range(gather.steps):
            yield 30 + 4 * s
            gather.both()
        yield 30 + 4 * gather.steps
        gather.end()
        early = len(net.open)
        for b in range(group):
            at = pl.ds(b * rows, rows)
            gc = dot_nt(branch[b], wo[...]).astype(BF)
            for h in range(heads):
                lane = pl.ds(h * head, head)
                qh, kh, vh = q[at, lane], k[at, lane], v[at, lane]
                gch = gc[:, h * head : (h + 1) * head]
                p = p_ref[b, h]
                gw = dot_nt(gch, vh)
                inner = jnp.sum(p * gw, axis=-1, keepdims=True)
                gs = (p * (gw - inner)).astype(BF)
                g3[b, :, pl.ds(h * head, head)] = (dot(gs, kh) * scale).astype(BF)
                g3[b, :, pl.ds(width + h * head, head)] = (dot_tn(gs, qh) * scale).astype(BF)
                g3[b, :, pl.ds(2 * width + h * head, head)] = dot_tn(p.astype(BF), gch).astype(BF)
            yield 0
        n_col = 512
        for c in range(0, model, n_col):
            lane = pl.ds(c, n_col)
            full = branch[:, :, lane].reshape(group * rows, n_col)
            own_all[pl.ds(out_base, tall), lane] = dot_tn(ctx[...], full).astype(BF)
            yield 0
        arrivals[out_base] = []
        grads = g3[...].reshape(group * rows, 3 * width)
        total = jnp.sum(grads.astype(F32), axis=0, keepdims=True)
        both[8:9] = total[:, :width]
        both[9:10] = total[:, 2 * width :]
        both[10:16] = cols[...]

        def normed_of(j):
            return pltpu.make_async_copy(nrm.at[:, :, place(j)], nbuf.at[j % 2], loads.at[0, j % 2])

        normed_of(0).start()
        grown = {out_base + (i + 1) * tall: [] for i in range(3)}
        for j in range(group):
            if j + 1 < group:
                normed_of(j + 1).start()
            normed_of(j).wait()
            left = nbuf[j % 2].reshape(group * rows, width)
            right = g3[...].reshape(group * rows, 3 * width)
            dw[j] = dot_tn(left, right).astype(BF)
            for i in range(3):
                src = dw.at[j, :, pl.ds(i * width, width)]
                base = out_base + (i + 1) * tall
                dst = own_all.at[pl.ds(base, tall), place(0)]
                if j:
                    grown[base].append(net.to("shard", j, src, dst))
                else:
                    kept_here[base] = [net.own(src, dst)]
            yield 0
        arrivals.update(grown)

        def weight_of(a):
            return [
                pltpu.make_async_copy(w.at[a], wbuf.at[a % 2, i], loads.at[1 + i, a % 2])
                for i, w in enumerate((wq, wk, wv))
            ]

        net.settle(early)
        for copy in weight_of(0):
            copy.start()
        for a in range(group):
            if a + 1 < group:
                for copy in weight_of(a + 1):
                    copy.start()
            for copy in weight_of(a):
                copy.wait()
            left = g3[...].reshape(group * rows, 3 * width)
            res = dot_nt(left[:, :width], wbuf[a % 2, 0])
            res = res + dot_nt(left[:, width : 2 * width], wbuf[a % 2, 1])
            res = res + dot_nt(left[:, 2 * width :], wbuf[a % 2, 2])
            part[:, :, pl.ds(a * width, width)] = res.astype(BF).reshape(group, rows, width)
            yield 0
        red = Reduce(net, part, work[:2], masks)
        red.begin()
        yield 0
        down_of = stream(lambda a: wd.at[:, pl.ds(a * width, width)], dbuf, 4)
        down_of.begin()
        for a in range(group):
            block = down_of.take(a)
            branch[:, :, pl.ds(a * width, width)] = (
                dot(active[...], block).astype(BF).reshape(group, rows, width)
            )
            if a % 2:
                yield 0
        late = Reduce(net, branch, work[2:4], masks)
        late.begin()
        yield 69
        red.prepare()
        for s in range(red.steps - 1):
            yield 75 + 4 * s
            for n in range(2):
                red.advance(n, s)
        yield 80
        for n in range(2):
            red.advance(n, red.steps - 1)

            def first(at, start):
                g = red.total(at)
                w, inv = norm_rows(x_ref[at].astype(F32))
                gin[at] = (gmid[at] + norm_back(g, small[FG : FG + 1], w, inv)).astype(BF)
                sums[FG : FG + 1] += jnp.sum(g * w, axis=0, keepdims=True)
                sums[FS : FS + 1] += jnp.sum(g, axis=0, keepdims=True)

            by_rows(n, rows, first)
        tiny = [net.to("shard", j, sums.at[:, place(j)], land.at[me]) for j in range(1, group)]
        own = net.own(sums.at[:, place(0)], land.at[me])
        yield 83
        late.prepare()
        yield 85
        for copy in tiny:
            copy.wait_recv()
        own.wait()
        total = land[0]
        for j in range(1, group):
            total = total + land[j]
        both[0:8] = total
        tiny = [net.to("rep", h, both, zland.at[rep]) for h in range(1, reps)]
        own = net.own(both, zland.at[rep])
        for s in range(late.steps - 1):
            yield 90 + 4 * s
            for n in range(2):
                late.advance(n, s)
        yield 94
        for n in range(2):
            late.advance(n, late.steps - 1)

            def close(at, start):
                m = mid[at] + (late.total(at) + small[DB : DB + 1])
                out[at] = (m * live_rows(length, start, 16)).astype(BF)

            by_rows(n, rows, close)
        yield 97
        for copy in tiny:
            copy.wait_recv()
        own.wait()
        total = zland[0]
        for h in range(1, reps):
            total = total + zland[h]
        smalls[...] = total

    todo = tasks()
    resume = next(todo)
    for t in range(line.steps):
        base = t // line.each * tall
        if t < line.count and t % line.each == 0 and (base == up_base or base >= out_base):
            while base not in arrivals:
                resume = next(todo, None)
            for copy in arrivals[base]:
                copy.wait_recv()
            for copy in kept_here.pop(base, []):
                copy.wait()
        line.step(t)
        if resume is not None and t >= resume:
            resume = next(todo, None)
    for _ in todo:
        pass
    line.finish()
    net.finish()


def call(body, number, sizes, outs, scratch, copies, args, far=(), far_outs=(), scalars=()):
    return pl.pallas_call(
        functools.partial(body, *sizes),
        out_shape=[jax.ShapeDtypeStruct(s, d) for s, d in outs],
        in_specs=[
            ANY if i in far else SCALAR if i in scalars else VM for i in range(len(args))
        ],
        out_specs=[ANY if i in far_outs else VM for i in range(len(outs))],
        scratch_shapes=list(scratch)
        + [pltpu.SemaphoreType.DMA((copies,)), pltpu.SemaphoreType.DMA((copies,))],
        compiler_params=pltpu.CompilerParams(
            collective_id=number, has_side_effects=True, vmem_limit_bytes=LIMIT
        ),
        name=body.__name__,
    )(*args)


def dot(a, b):
    return jnp.dot(a, b, preferred_element_type=F32)


def dot_nt(a, b):
    return jnp.einsum("tc,rc->tr", a, b, preferred_element_type=F32)


def dot_tn(a, b):
    return jnp.einsum("tr,tc->rc", a, b, preferred_element_type=F32)


def local(
    block_input,
    lengths,
    first_gain,
    first_shift,
    query_weight,
    query_bias,
    key_weight,
    value_weight,
    value_bias,
    out_weight,
    out_bias,
    second_gain,
    second_shift,
    up_weight,
    up_bias,
    down_weight,
    down_bias,
    cotangent,
):
    rows, width = block_input.shape[1], block_input.shape[2]
    hidden = up_weight.shape[1]
    group, reps = lax.axis_size("shard"), lax.axis_size("rep")
    sizes = (group, reps)
    g, f = width // group, hidden // group
    head = width // HEADS
    scale = 1.0 / math.sqrt(head)
    me = lax.axis_index("shard")
    vectors = (
        first_gain,
        first_shift,
        out_bias,
        second_gain,
        second_shift,
        down_bias,
        query_bias,
        value_bias,
    )
    at = lax.broadcasted_iota(jnp.int32, (8, g), 0)
    stacked = jnp.zeros((8, g), F32)
    for i, a in enumerate(vectors):
        stacked = jnp.where(at == i, a.astype(F32)[None], stacked)
    x, cot = block_input[0], cotangent[0]
    blocks = (group, rows, width)
    masks = shard_masks(group)
    work = reduce_shapes(group, rows, width, masks)
    tokens, column = group * rows, ((group, g, g), BF)
    nrm, small_all, wq, wk, wv, wu, queries, keys, values, p, ctx, mid, second, mix = call(
        forward_kernel,
        1,
        (sizes, head),
        [
            (blocks, BF),
            ((8, width), F32),
            column,
            column,
            column,
            ((group, g, f), BF),
            ((tokens, g), BF),
            ((tokens, g), BF),
            ((tokens, g), BF),
            ((group, g // head, rows, rows), F32),
            ((tokens, g), BF),
            ((rows, width), F32),
            (blocks, BF),
            (blocks, BF),
        ],
        work
        + [pltpu.VMEM(blocks, BF), pltpu.VMEM((8, g), F32)]
        + [pltpu.SemaphoreType.DMA((2 * reps,))] * 2
        + [pltpu.VMEM(blocks, BF)]
        + [pltpu.VMEM((group, g, g), BF)] * 3,
        320,
        (
            lengths,
            x,
            cot,
            query_weight,
            key_weight,
            value_weight,
            up_weight,
            out_weight,
            stacked,
        ),
        (3, 4, 5, 6),
        (0, 2, 3, 4),
        (0,),
    )
    flat = lambda a: a.reshape(-1, a.shape[-1])
    wu = flat(wu)
    second = flat(second)
    mixed = flat(mix)
    upper = dot(second, wu) + up_bias.astype(F32)
    cdf = 0.5 * (1.0 + lax.erf(upper * (1.0 / math.sqrt(2.0))))
    pdf = jnp.exp(-0.5 * upper * upper) * (1.0 / math.sqrt(2.0 * math.pi))
    active = (upper * cdf).astype(BF)
    gup = (dot_nt(mixed, down_weight) * (cdf + upper * pdf)).astype(BF)
    down_grad = dot_tn(active, mixed).astype(BF)
    cols = jnp.concatenate(
        [jnp.sum(gup.astype(F32), axis=0).reshape(4, g), jnp.zeros((2, g), F32)]
    )
    blocks_up = hidden // width
    tall_all = f + (4 + blocks_up) * g
    piece = 16
    count = tall_all // 2 // piece
    scratch = (
        work
        + work
        + [
            pltpu.VMEM((rows, width), F32),
            pltpu.VMEM((8, width), F32),
            pltpu.VMEM((group, 8, g), F32),
            pltpu.VMEM((16, g), F32),
            pltpu.VMEM((reps, 16, g), F32),
            pltpu.VMEM((tall_all, width), BF),
            pltpu.VMEM((2, count, piece, width), BF),
            pltpu.VMEM(blocks, BF),
            pltpu.VMEM(blocks, BF),
            pltpu.VMEM((group, rows, 3 * g), BF),
            pltpu.VMEM((group, g, 3 * g), BF),
            pltpu.VMEM((2, group, rows, g), BF),
            pltpu.VMEM((2, 3, g, g), BF),
            pltpu.VMEM((2, g, f), BF),
            pltpu.VMEM((2, f, g), BF),
            pltpu.SemaphoreType.DMA((5, 2)),
        ]
        + [pltpu.SemaphoreType.DMA((4 * count,))] * 2
        + [pltpu.SemaphoreType.DMA((2 * count,))]
    )
    out, gin, smalls, whole = call(
        final_kernel,
        2,
        (sizes, head),
        [
            ((rows, width), BF),
            ((rows, width), BF),
            ((16, g), F32),
            ((tall_all, width), BF),
        ],
        scratch,
        320,
        (
            gup,
            active,
            second.reshape(blocks),
            wu.reshape(group, g, f),
            down_weight,
            down_grad,
            mid,
            cot,
            x,
            small_all,
            queries,
            keys,
            values,
            p,
            ctx,
            nrm,
            wq,
            wk,
            wv,
            out_weight,
            cols,
        ),
        (2, 3, 4, 5, 15, 16, 17, 18),
        (3,),
    )
    dd = whole[:f].astype(F32)
    ups = [whole[f + i * g : f + (i + 1) * g] for i in range(blocks_up)]
    du = jnp.concatenate(ups, axis=1).astype(F32)
    skip = f + blocks_up * g
    do, dq, dk, dv = (whole[skip + i * g : skip + (i + 1) * g].astype(F32) for i in range(4))
    return (
        out[None],
        gin[None],
        smalls[FG],
        smalls[FS],
        dq,
        smalls[8],
        dk,
        dv,
        smalls[9],
        do,
        smalls[OB],
        smalls[SG],
        smalls[SS],
        du,
        smalls[10:14].reshape(-1),
        dd,
        smalls[DB],
    )


def solution(mesh):
    tokens = P(("rep", "shard"), None, None)
    vec, mat = P("shard"), P("shard", None)
    return jax.shard_map(
        local,
        mesh=mesh,
        in_specs=(
            tokens,
            P(("rep", "shard")),
            vec,
            vec,
            mat,
            vec,
            mat,
            mat,
            vec,
            mat,
            vec,
            vec,
            vec,
            mat,
            vec,
            mat,
            vec,
            tokens,
        ),
        out_specs=(
            tokens,
            tokens,
            vec,
            vec,
            mat,
            vec,
            mat,
            mat,
            vec,
            mat,
            vec,
            vec,
            vec,
            mat,
            vec,
            mat,
            vec,
        ),
        check_vma=False,
    )
```
